32 devices in a mesh: dp: 16 (over z, y, core), fsdp: 2 (over x).
Axes of the slice: x: 2, y: 2, z: 4, core: 2. Of those that a mesh axis runs over, the one named last changes fastest.
Arguments:
- frames_in: bfloat16 [16, 1024, 1024], P('dp', 'fsdp'), may hold values from -6 to 6
- prefix_len: int32 [16], P('dp'), may hold values from 1 to 512, as said below
- w_qkv: bfloat16 [1024, 3072], P(('dp', 'fsdp')), may hold values from -0.1875 to 0.1875
- w_out: bfloat16 [1024, 1024], P(('dp', 'fsdp')), may hold values from -1.5 to 1.5
- w_up: bfloat16 [1024, 4096], P(('dp', 'fsdp')), may hold values from -0.1875 to 0.1875
- w_down: bfloat16 [4096, 1024], P(('dp', 'fsdp')), may hold values from -0.09375 to 0.09375
- gains: bfloat16 [2, 1024], P(None, ('dp', 'fsdp')), may hold values from 0.25 to 1.75
- shifts: bfloat16 [2, 1024], P(None, ('dp', 'fsdp')), may hold values from -1.796875 to 1.796875
- cotangent: bfloat16 [16, 1024, 1024], P('dp', 'fsdp'), may hold values from -6 to 6
Outputs:
- frames_out: bfloat16 [16, 1024, 1024], P('dp', 'fsdp')
- grad_in: float32 [16, 1024, 1024], P('dp', 'fsdp')
- grad_qkv: float32 [1024, 3072], P(('dp', 'fsdp'))
- grad_out: float32 [1024, 1024], P(('dp', 'fsdp'))
- grad_up: float32 [1024, 4096], P(('dp', 'fsdp'))
- grad_down: float32 [4096, 1024], P(('dp', 'fsdp'))
- grad_gains: float32 [2, 1024], P(None, ('dp', 'fsdp'))
- grad_shifts: float32 [2, 1024], P(None, ('dp', 'fsdp'))
The draws below stay inside these ranges and needn't reach their ends.
Inputs may be any that keep to these rules, and one draw needn't show every extreme that they name: `prefix_len`: some item's prefix has exactly 512 frames.
All inputs are finite; a program needn't handle non-finite values.
Results may differ from the reference program's by a relative error of at most 0.011.
Values may be sent and summed in bfloat16 or wider, within the bound.
A program may use at most 256 MiB of HBM per device.

```python
import jax
import jax.numpy as jnp
from jax import lax

D = 1024
H = 16
HD = 64
FF = 4096
FRAMES = 1024
ITEMS = 16


def draw_prefix_len(key, part):
    key = jax.random.fold_in(key, 11)
    first, second = jax.random.split(key)
    lengths = jax.random.randint(first, (ITEMS,), 1, FRAMES // 2 + 1)
    chosen = jax.random.randint(second, (), 0, ITEMS)
    places = jnp.arange(ITEMS, dtype=jnp.int32)
    return jnp.where(places == chosen, FRAMES // 2, lengths).astype(jnp.int32)


def block_levels(stream_key, shape, cuts, low, top_value):
    factor_of, own = 1.0, jax.random.fold_in(stream_key, 6)
    for axis_at, blocks in cuts:
        steps = jnp.exp(jax.random.uniform(jax.random.fold_in(own, axis_at), (blocks,), jnp.float32, low / len(cuts), top_value / len(cuts)))
        factor_of = factor_of * jnp.repeat(steps, shape[axis_at] // blocks).reshape([-1 if axis == axis_at else 1 for axis in range(len(shape))])
    return factor_of


def noise(own_key, dims, scale, reach, shards=(), held_as=jnp.bfloat16):
    values = jax.random.normal(own_key, dims, jnp.float32) * scale
    if len(shards) > 0:
        values = block_levels(own_key, dims, shards, -0.22, 0.18) * values
    return jnp.clip(values, min=-reach, max=reach).astype(held_as)


def setup_inputs(seed: int = 0) -> dict:
    seeds = jax.random.split(jax.random.key(seed), 10)
    return {
        "frames_in": noise(seeds[0], (ITEMS, FRAMES, D), 1.0, 6.0, ((0, 16), (1, 2))),
        "prefix_len": draw_prefix_len(jax.random.fold_in(seeds[9], 71), 0),
        "w_qkv": noise(seeds[2], (D, 3 * D), D ** -0.5, 0.1875, ((0, 32),)),
        "w_out": noise(seeds[3], (D, D), (D // 64) ** -0.5, 1.5, ((0, 32),)),
        "w_up": noise(seeds[4], (D, FF), D ** -0.5, 0.1875, ((0, 32),)),
        "w_down": noise(seeds[5], (FF, D), FF ** -0.5, 0.09375, ((0, 32),)),
        "gains": jnp.clip(1.0 + 0.15 * jax.random.normal(seeds[6], (2, D), jnp.float32), 0.25, 1.75).astype(jnp.bfloat16),
        "shifts": noise(seeds[7], (2, D), 0.3, 1.796875, ((1, 32),)),
        "cotangent": noise(seeds[8], (ITEMS, FRAMES, D), 1.0, 6.0, ((0, 16), (1, 2))),
    }


EPS = 1e-05

@jax.custom_vjp
def low(v):
    return lax.optimization_barrier(v.astype(jnp.bfloat16)).astype(jnp.float32)

@jax.custom_vjp
def low_back(v):
    return v

def low_keep(v):
    return (low(v), None)

def low_pass(kept, grad):
    return (grad,)

def back_keep(v):
    return (v, None)

def back_low(kept, grad):
    return (low(grad),)
low.defvjp(low_keep, low_pass)
low_back.defvjp(back_keep, back_low)

def product(left, right):
    return jnp.dot(left, right, precision=lax.Precision.HIGHEST, preferred_element_type=jnp.float32)

def norm_rows(values, gain, shift):
    center = values - lax.optimization_barrier(jnp.mean(values, -1, keepdims=True))
    spread = lax.optimization_barrier(jnp.mean(center * center, -1, keepdims=True))
    return center * lax.rsqrt(spread + EPS) * gain + shift

def head_attend(query_one, key_one, value_one, allowed):
    scores = low_back(product(query_one, key_one.T) * 0.125)
    scores = jnp.where(allowed, scores, -1e+30)
    peak_row = lax.optimization_barrier(jnp.max(scores, -1, keepdims=True))
    log_total = peak_row + jnp.log(lax.optimization_barrier(jnp.sum(jnp.exp(scores - peak_row), -1, keepdims=True)))
    chance = low(jnp.exp(scores - log_total))
    return product(chance, value_one)

def split_heads(matrix):
    return matrix.reshape(FRAMES, H, HD).transpose(1, 0, 2)

def block(inputs, prefix, wq, wo, wu, wd, gain_rows, shift_rows):
    normed = low(norm_rows(inputs, gain_rows[0], shift_rows[0]))
    mixed = product(normed, wq)
    queries = low(low_back(mixed[:, :D]))
    keys_all = low(low_back(mixed[:, D:2 * D]))
    values_all = low(low_back(mixed[:, 2 * D:]))
    places = jnp.arange(FRAMES, dtype=jnp.int32)
    allowed = (places[None, :] <= places[:, None]) | (places[None, :] < prefix)

    def single(pieces):
        return head_attend(pieces[0], pieces[1], pieces[2], allowed)
    heads = lax.map(jax.checkpoint(single), (split_heads(queries), split_heads(keys_all), split_heads(values_all)))
    attended = low(low_back(heads.transpose(1, 0, 2).reshape(FRAMES, D)))
    middle = inputs + low_back(product(attended, wo))
    normed_two = low(norm_rows(middle, gain_rows[1], shift_rows[1]))
    hidden = low_back(product(normed_two, wu))
    active = low(jax.nn.gelu(hidden, approximate=False))
    return middle + low_back(product(active, wd))

def reference(frames_in, prefix_len, w_qkv, w_out, w_up, w_down, gains, shifts, cotangent):
    as_float = [arr.astype(jnp.float32) for arr in (frames_in, w_qkv, w_out, w_up, w_down, gains, shifts)]

    def whole(inputs, wq, wo, wu, wd, gain_rows, shift_rows):

        def item_step(item):
            return block(item[0], item[1], wq, wo, wu, wd, gain_rows, shift_rows)
        return lax.map(jax.checkpoint(item_step), (inputs, prefix_len))
    result, pullback = jax.vjp(whole, *as_float)
    grads = pullback(cotangent.astype(jnp.float32))
    return (result.astype(jnp.bfloat16), grads[0], grads[1], grads[2], grads[3], grads[4], grads[5], grads[6])
```

```python
import functools
import math

import jax
import jax.numpy as jnp
from jax import lax
from jax.experimental import pallas as pl
from jax.experimental.pallas import tpu as pltpu
from jax.sharding import PartitionSpec as P

H = 16
HD = 64
EPS = 1e-05
BF = jnp.bfloat16
F32 = jnp.float32
LOG2E = math.log2(math.e)
SCALE2 = 0.125 * LOG2E
PAIR = 2 * HD
TILE = 512
MESH = pl.DeviceIdType.MESH
DMA = pltpu.SemaphoreType.DMA
VMEM_LIMIT = 60 * 2**20


def coords():
    dp, f = lax.axis_index("dp"), lax.axis_index("fsdp")
    q = lax.div(dp, 2)
    return lax.div(q, 2), lax.rem(q, 2), lax.rem(dp, 2), f


def dev(z, y, c, f):
    return ((z * 2 + y) * 2 + c, f)


def remote(src, dst, send, recv, device):
    return pltpu.make_async_remote_copy(
        src_ref=src, dst_ref=dst, send_sem=send, recv_sem=recv, device_id=device, device_id_type=MESH
    )


def greet(peers):
    barrier = pltpu.get_barrier_semaphore()
    for peer in peers:
        pl.semaphore_signal(barrier, inc=1, device_id=peer, device_id_type=MESH)
    pl.semaphore_wait(barrier, len(peers))


def all_peers(nz, z, y, c, f):
    peers = [dev(lax.rem(z + k, nz), y, c, f) for k in range(1, nz)]
    return peers + [dev(z, 1 - y, c, f), dev(z, y, c, 1 - f), dev(z, y, 1 - c, f)]


def dot_nn(a, b):
    return lax.dot_general(a, b, (((1,), (0,)), ((), ())), preferred_element_type=F32)


def dot_nt(a, b):
    return lax.dot_general(a, b, (((1,), (1,)), ((), ())), preferred_element_type=F32)


def dot_tn(a, b):
    return lax.dot_general(a, b, (((0,), (0,)), ((), ())), preferred_element_type=F32)


def tiles(count, size, body):
    @pl.loop(0, count)
    def _(j):
        body(j, pl.ds(pl.multiple_of(j * size, size), size))


def normalise(v):
    center = v - jnp.mean(v, -1, keepdims=True)
    scale = lax.rsqrt(jnp.mean(center * center, -1, keepdims=True) + EPS)
    return center * scale, scale


class Gather:
    def __init__(self, nz, place, shards, outs, sems):
        self.nz, self.place, self.shards, self.outs = nz, place, shards, outs
        self.send, self.recv, self.core_send, self.core_recv, self.own = sems

    @staticmethod
    def sem_shapes(nz, nw):
        return [DMA((nw, 32)), DMA((nw, 32)), DMA((nw, 4 * nz)), DMA((nw, 4 * nz)), DMA((nw,))]

    def block(self, w, zz, yy, ff):
        return self.outs[w].at[zz, yy, self.place[2], ff]

    def hop(self, w, src, zz, yy, ff, slot, device):
        return remote(src, self.block(w, zz, yy, ff), self.send.at[w, slot], self.recv.at[w, slot], device)

    def arrive(self, w, zz, yy, ff, slot):
        dst = self.block(w, zz, yy, ff)
        remote(dst, dst, self.send.at[w, slot], self.recv.at[w, slot], self.core()).wait_recv()

    def core(self):
        z, y, c, f = self.place
        return dev(z, y, 1 - c, f)

    def to_core(self, w, src, zz, yy, ff, slot):
        remote(
            src, self.block(w, zz, yy, ff), self.core_send.at[w, slot], self.core_recv.at[w, slot], self.core()
        ).start()

    def zk(self, k):
        return lax.rem(self.place[0] + self.nz - k, self.nz)

    def zt(self, k):
        return lax.rem(self.place[0] + k, self.nz)

    def e0(self, w):
        z, y, c, f = self.place
        nz, mine = self.nz, self.shards[w]
        pltpu.make_async_copy(mine, self.block(w, z, y, f), self.own.at[w]).start()

        @pl.when(c == 0)
        def _():
            for k in range(1, nz):
                self.hop(w, mine, z, y, f, k - 1, dev(self.zt(k), y, c, f)).start()
            self.hop(w, mine, z, y, f, 4, dev(z, 1 - y, c, f)).start()
            self.hop(w, mine, z, y, f, 8, dev(z, y, c, 1 - f)).start()

        @pl.when(c == 1)
        def _():
            self.hop(w, mine, z, y, f, 0, dev(z, y, c, 1 - f)).start()
            for k in range(1, nz):
                self.hop(w, mine, z, y, f, k, dev(self.zt(k), y, c, f)).start()
            self.hop(w, mine, z, y, f, 8, dev(z, 1 - y, c, f)).start()

        self.to_core(w, mine, z, y, f, 0)

    def e1(self, w):
        z, y, c, f = self.place
        nz = self.nz

        @pl.when(c == 0)
        def _():
            for k in range(1, nz):
                zz = self.zk(k)
                self.arrive(w, zz, y, f, k - 1)
                src = self.block(w, zz, y, f)
                self.hop(w, src, zz, y, f, 4 + k, dev(z, 1 - y, c, f)).start()
                self.hop(w, src, zz, y, f, 8 + k, dev(z, y, c, 1 - f)).start()
                self.to_core(w, src, zz, y, f, k)

        @pl.when(c == 1)
        def _():
            self.arrive(w, z, y, 1 - f, 0)
            src = self.block(w, z, y, 1 - f)
            for k in range(1, nz):
                self.hop(w, src, z, y, 1 - f, 3 + k, dev(self.zt(k), y, c, f)).start()
            self.hop(w, src, z, y, 1 - f, 12, dev(z, 1 - y, c, f)).start()
            self.to_core(w, src, z, y, 1 - f, 4)

    def e2(self, w):
        z, y, c, f = self.place
        nz = self.nz

        @pl.when(c == 0)
        def _():
            for k in range(nz):
                zz = self.zk(k)
                self.arrive(w, zz, 1 - y, f, 4 + k)
                src = self.block(w, zz, 1 - y, f)
                self.hop(w, src, zz, 1 - y, f, 12 + k, dev(z, y, c, 1 - f)).start()
                self.to_core(w, src, zz, 1 - y, f, 4 + k)

        @pl.when(c == 1)
        def _():
            for h in range(2):
                ff = f if h == 0 else 1 - f
                for k in range(1, nz):
                    zz = self.zk(k)
                    self.arrive(w, zz, y, ff, 3 * h + k)
                    src = self.block(w, zz, y, ff)
                    self.hop(w, src, zz, y, ff, 8 + 4 * h + k, dev(z, 1 - y, c, f)).start()
                    self.to_core(w, src, zz, y, ff, 4 * h + k)

    def e3(self, w):
        z, y, c, f = self.place
        nz = self.nz

        @pl.when(c == 0)
        def _():
            for h in range(2):
                yy = y if h == 0 else 1 - y
                for k in range(nz):
                    zz = self.zk(k)
                    self.arrive(w, zz, yy, 1 - f, 8 + 4 * h + k)
                    self.to_core(w, self.block(w, zz, yy, 1 - f), zz, yy, 1 - f, 8 + 4 * h + k)

        @pl.when(c == 1)
        def _():
            for h in range(2):
                ff = f if h == 0 else 1 - f
                for k in range(nz):
                    zz = self.zk(k)
                    self.arrive(w, zz, 1 - y, ff, 8 + 4 * h + k)
                    self.to_core(w, self.block(w, zz, 1 - y, ff), zz, 1 - y, ff, 8 + 4 * h + k)

    def e4(self, w):
        z, y, c, f = self.place
        pltpu.make_async_copy(self.shards[w], self.block(w, z, y, f), self.own.at[w]).wait()

        def from_core(order):
            for slot, (zz, yy, ff) in enumerate(order):
                dst = self.outs[w].at[zz, yy, 1 - c, ff]
                remote(dst, dst, self.core_send.at[w, slot], self.core_recv.at[w, slot], self.core()).wait_recv()

        ks = range(self.nz)

        @pl.when(c == 1)
        def _():
            from_core([(self.zk(k), yy, ff) for yy, ff in ((y, f), (1 - y, f), (y, 1 - f), (1 - y, 1 - f)) for k in ks])

        @pl.when(c == 0)
        def _():
            from_core([(self.zk(k), yy, ff) for yy, ff in ((y, f), (y, 1 - f), (1 - y, f), (1 - y, 1 - f)) for k in ks])

    def finish(self, w):
        z, y, c, f = self.place
        some = self.shards[w]

        def drain(sems, slots):
            for slot in slots:
                remote(some, self.block(w, z, y, f), sems.at[w, slot], self.recv.at[w, 0], self.core()).wait_send()

        @pl.when(c == 0)
        def _():
            drain(self.send, [k - 1 for k in range(1, self.nz)] + list(range(4, 16)))

        @pl.when(c == 1)
        def _():
            drain(self.send, list(range(0, 7)) + list(range(8, 16)))

        drain(self.core_send, range(16))


def gather_kernel(nz, nw, *refs):
    place = coords()
    g = Gather(nz, place, refs[:nw], refs[nw : 2 * nw], refs[2 * nw :])
    greet(all_peers(nz, *place))
    for step in range(nw + 3):
        for stage, call in enumerate((g.e0, g.e1, g.e2, g.e3)):
            if 0 <= step - stage < nw:
                call(step - stage)
    for w in range(nw):
        g.e4(w)
    for w in range(nw):
        g.finish(w)


def gather(nz, shards):
    nw = len(shards)
    return pl.pallas_call(
        functools.partial(gather_kernel, nz, nw),
        out_shape=[jax.ShapeDtypeStruct((nz, 2, 2, 2) + s.shape, s.dtype) for s in shards],
        in_specs=[pl.BlockSpec(memory_space=pl.ANY)] * nw,
        out_specs=[pl.BlockSpec(memory_space=pl.ANY)] * nw,
        scratch_shapes=Gather.sem_shapes(nz, nw),
        compiler_params=pltpu.CompilerParams(collective_id=0, has_side_effects=True),
    )(*shards)


def lane_half():
    return lax.broadcasted_iota(jnp.int32, (1, PAIR), 1) // HD


def fill_bias(bias, prefix, c, transposed):
    rows = bias.shape[0]
    step = 64

    def body(j, part):
        a = lax.broadcasted_iota(jnp.int32, (step, rows), 0) + j * step
        b = lax.broadcasted_iota(jnp.int32, (step, rows), 1)
        row, key = (b, a) if transposed else (a, b)
        bias[part, :] = jnp.where((key <= row) | (key + c * rows < prefix), 0.0, -1e30)

    tiles(rows // step, step, body)


def attend_forward(c, qkv, cross, bias, att, lse):
    rows, d = att.shape
    half = lane_half()
    lane = lax.broadcasted_iota(jnp.int32, (1, PAIR), 1)
    rt = rows // 2

    def one(q, blocks):
        scores = []
        for keys, _, extra in blocks:
            s = dot_nt(q, keys) * SCALE2
            scores.append(s if extra is None else s + extra)
        peak = functools.reduce(jnp.maximum, [jnp.max(s, -1, keepdims=True) for s in scores])
        total = None
        for s, (_, values, _) in zip(scores, blocks):
            part = dot_nn(jnp.exp2(s - peak).astype(BF), values)
            total = part if total is None else total + part
        return total, peak

    def pair(p, second):
        cols = pl.ds(pl.multiple_of(p * PAIR, PAIR), PAIR)
        kcols = pl.ds(pl.multiple_of(d + p * PAIR, PAIR), PAIR)
        vcols = pl.ds(pl.multiple_of(2 * d + p * PAIR, PAIR), PAIR)
        for r in range(2):
            part = pl.ds(r * rt, rt)
            results = []
            for h in range(2):
                mine = half == h
                q = jnp.where(mine, qkv[part, cols], 0.0).astype(BF)

                def val(v):
                    return jnp.where(mine, v, 1.0).astype(BF)

                if second:
                    blocks = [(cross[:, cols], val(cross[:, pl.ds(pl.multiple_of(d + p * PAIR, PAIR), PAIR)]), None)]
                    if r > 0:
                        blocks.append((qkv[pl.ds(0, rt), kcols], val(qkv[pl.ds(0, rt), vcols]), None))
                    blocks.append((qkv[part, kcols], val(qkv[part, vcols]), bias[part, pl.ds(r * rt, rt)]))
                else:
                    blocks = [(qkv[:, kcols], val(qkv[:, vcols]), bias[part, :])]
                total, peak = one(q, blocks)
                sums = pltpu.roll(total, HD, axis=1)
                results.append(total / sums)
                both = jnp.where(mine, sums, total)
                lse[part, :] = jnp.where(lane == 2 * p + h, peak + jnp.log2(both), lse[part, :])
            att[part, cols] = jnp.where(half == 0, results[0], results[1]).astype(BF)

    for second in range(2):

        @pl.when(c == second)
        def _():
            @pl.loop(0, d // PAIR)
            def _(p):
                pair(p, second == 1)


def gelu_tile(u, a, gp, cols):
    rows = u.shape[0]
    step = 32

    def body(j, part):
        v = u[part, :]
        phi = 0.5 * (1.0 + lax.erf(v * math.sqrt(0.5)))
        dens = jnp.exp2(v * v * (-0.5 * LOG2E)) * (1.0 / math.sqrt(2.0 * math.pi))
        a[part, cols] = (v * phi).astype(BF)
        gp[part, cols] = (phi + v * dens).astype(BF)

    tiles(rows // step, step, body)


def forward_kernel(nz, prefix, x, par, wqkv, wout, wup, wdown, out, h1, qkv, cross, lset, att, x1, h2, a, gp, bias, lse, u, sems):
    z, y, c, f = coords()
    rows, d = x.shape
    ff = wup.shape[1]
    core = dev(z, y, 1 - c, f)
    greet([core])
    step = 64

    def norm_one(j, part):
        n, _ = normalise(x[part, :].astype(F32))
        h1[part, :] = (n * par[0:1, :].astype(F32) + par[2:3, :].astype(F32)).astype(BF)

    tiles(rows // step, step, norm_one)
    fill_bias(bias, prefix[0], c, False)

    def mix(j, cols):
        qkv[:, cols] = dot_nn(h1[...], wqkv[:, cols]).astype(BF)

    nq = d // TILE
    for j in list(range(nq, 3 * nq)) + list(range(nq)):
        mix(j, pl.ds(j * TILE, TILE))
        if j == 3 * nq - 1:
            pass
    keyvals = remote(qkv.at[:, pl.ds(d, 2 * d)], cross, sems.at[0], sems.at[1], core)

    @pl.when(c == 0)
    def _():
        keyvals.start()
        keyvals.wait_send()

    @pl.when(c == 1)
    def _():
        keyvals.wait_recv()

    lse[...] = jnp.zeros_like(lse)
    attend_forward(c, qkv, cross, bias, att, lse)
    lset[...] = lse[...].T[:H, :]
    for j in range(d // TILE):
        cols = pl.ds(j * TILE, TILE)
        x1[:, cols] = x[:, cols].astype(F32) + dot_nn(att[...], wout[:, cols])

    def norm_two(j, part):
        n, _ = normalise(x1[part, :])
        h2[part, :] = (n * par[1:2, :].astype(F32) + par[3:4, :].astype(F32)).astype(BF)

    tiles(rows // step, step, norm_two)

    def up(j, cols):
        u[...] = dot_nn(h2[...], wup[:, cols])
        gelu_tile(u, a, gp, cols)

    tiles(ff // TILE, TILE, up)

    def down(j, cols):
        out[:, cols] = (x1[:, cols] + dot_nn(a[...], wdown[:, cols])).astype(BF)

    tiles(d // 256, 256, down)


def run_forward(nz, prefix, x, par, wqkv, wout, wup, wdown):
    rows, d = x.shape
    ff = wup.shape[1]
    S = jax.ShapeDtypeStruct
    vm = pl.BlockSpec(memory_space=pltpu.VMEM)
    return pl.pallas_call(
        functools.partial(forward_kernel, nz),
        out_shape=[
            S((rows, d), BF), S((rows, d), BF), S((rows, 3 * d), BF), S((rows, 2 * d), BF), S((H, rows), F32),
            S((rows, d), BF), S((rows, d), F32), S((rows, d), BF), S((rows, ff), BF), S((rows, ff), BF),
        ],
        in_specs=[pl.BlockSpec(memory_space=pltpu.SMEM)] + [vm] * 6,
        out_specs=[vm] * 10,
        scratch_shapes=[pltpu.VMEM((rows, rows), F32), pltpu.VMEM((rows, PAIR), F32), pltpu.VMEM((rows, TILE), F32), DMA((2,))],
        compiler_params=pltpu.CompilerParams(collective_id=1, has_side_effects=True, vmem_limit_bytes=VMEM_LIMIT),
    )(prefix, x, par, wqkv, wout, wup, wdown)


def attend_backward(c, qkv, cross, biast, lset, deltat, go, gqkv, dcross, gq):
    rows, d = go.shape
    half = lane_half()
    rt = rows // 2

    def one(keys, values, q, g, lse_row, delta_row, extra):
        s = dot_nt(keys, q) * SCALE2
        if extra is not None:
            s = s + extra
        p = jnp.exp2(s - lse_row)
        gs = (p * (dot_nt(values, g) - delta_row)).astype(BF)
        return dot_nn(gs, q), dot_nn(p.astype(BF), g), dot_tn(gs, keys)

    def pair(p, second):
        cols = pl.ds(pl.multiple_of(p * PAIR, PAIR), PAIR)
        kcols = pl.ds(pl.multiple_of(d + p * PAIR, PAIR), PAIR)
        vcols = pl.ds(pl.multiple_of(2 * d + p * PAIR, PAIR), PAIR)
        if second:
            jobs = [(cross, cols, kcols, r * rt, rt, 0, rows, False) for r in range(2)]
            jobs += [(qkv, kcols, vcols, 0, rt, 0, rows, True), (qkv, kcols, vcols, rt, rt, rt, rt, True)]
        else:
            jobs = [(qkv, kcols, vcols, r * rt, rt, 0, rows, True) for r in range(2)]
        first = {0: True, rt: True}
        gq[...] = jnp.zeros_like(gq)
        for ref, kc, vc, k0, kn, q0, qn, masked in jobs:
            gk = gv = None
            krows, qrows = pl.ds(k0, kn), pl.ds(q0, qn)
            keys, values = ref[krows, kc], ref[krows, vc]
            for h in range(2):
                mine = half == h
                q = jnp.where(mine, qkv[qrows, cols], 0.0).astype(BF)
                g = jnp.where(mine, go[qrows, cols], 0.0).astype(BF)
                km = jnp.where(mine, keys, 0.0).astype(BF)
                lse_row = lset[pl.ds(2 * p + h, 1), qrows]
                delta_row = deltat[pl.ds(2 * p + h, 1), qrows]
                extra = biast[krows, qrows] if masked else None
                s = dot_nt(keys, q) * SCALE2
                if extra is not None:
                    s = s + extra
                pr = jnp.exp2(s - lse_row)
                gs = (pr * (dot_nt(values, g) - delta_row)).astype(BF)
                k1, v1 = dot_nn(gs, q), dot_nn(pr.astype(BF), g)
                gk, gv = (k1, v1) if gk is None else (gk + k1, gv + v1)
                gq[qrows, :] = gq[qrows, :] + dot_tn(gs, km)
            if ref is qkv:
                gqkv[krows, kc] = (gk * 0.125).astype(BF)
                gqkv[krows, vc] = gv.astype(BF)
            else:
                dcross[krows, kc] = (gk * 0.125).astype(BF)
                dcross[krows, vc] = gv.astype(BF)
        gqkv[:, cols] = (gq[...] * 0.125).astype(BF)

    for second in range(2):

        @pl.when(c == second)
        def _():
            @pl.loop(0, d // PAIR)
            def _(p):
                pair(p, second == 1)


def norm_back(gh, n, scale, gain):
    gn = gh * gain
    return scale * (gn - jnp.mean(gn, -1, keepdims=True) - n * jnp.mean(gn * n, -1, keepdims=True))


def backward_kernel(
    nz, prefix, cot, par, wqkv, wout, wup, wdown, x, h1, qkv, cross, lset, att, x1, h2, a, gp,
    grad_in, o_qkv, o_out, o_up, o_down, o_par, r_qkv, r_out, r_up, r_down, r_par,
    wa, wb, buf, pbuf, ht, gh, gx1, gz, go, gqkv, dcross, biast, deltat, gq, acc, wsem, bsem, osem, rsem, xsem,
):
    z, y, c, f = coords()
    rows, d = x.shape
    ff = a.shape[1]
    core = dev(z, y, 1 - c, f)
    greet([core])
    loads = [pltpu.make_async_copy(wdown, wa, wsem.at[0]), pltpu.make_async_copy(wup, wb, wsem.at[1])]
    for load in loads:
        load.start()

    def emit(w, j, slot, own, land, wide):
        if wide:
            mine, theirs = buf.at[slot, :, :, c], buf.at[slot, :, :, 1 - c]
            cols = pl.ds(pl.multiple_of(j * TILE, TILE), TILE)
            to, there = own.at[:, :, :, :, cols], land.at[:, :, :, :, cols]
        else:
            mine, theirs = pbuf.at[slot, c], pbuf.at[slot, 1 - c]
            to, there = own.at[j // 2, j % 2], land.at[j // 2, j % 2]
        return (
            pltpu.make_async_copy(mine, to, osem.at[slot]),
            remote(theirs, there, bsem.at[slot], rsem.at[w], core),
        )

    def produce(w, count, own, land, wide, body):
        @pl.loop(0, count)
        def _(j):
            slot = lax.rem(j, 2)

            @pl.when(j >= 2)
            def _():
                local, away = emit(w, j - 2, slot, own, land, wide)
                local.wait()
                away.wait_send()

            body(j, slot)
            for copy in emit(w, j, slot, own, land, wide):
                copy.start()

        for j in range(count - 2, count):
            local, away = emit(w, j, j % 2, own, land, wide)
            local.wait()
            away.wait_send()

    gf = cot

    def down(j, slot):
        cols = pl.ds(pl.multiple_of(j * TILE, TILE), TILE)
        pbuf[slot] = dot_tn(a[:, cols], gf[...]).astype(BF).reshape(pbuf.shape[1:])

    produce(3, ff // TILE, o_down, r_down, False, down)
    loads[0].wait()
    ht[...] = h2[...].T

    def act(j, cols):
        gp[:, cols] = (dot_nt(gf[...], wa[cols, :]) * gp[:, cols].astype(F32)).astype(BF)

    tiles(ff // TILE, TILE, act)
    for i in range(3):
        pltpu.make_async_copy(wqkv.at[:, pl.ds(i * d, d)], wa.at[pl.ds(i * d, d)], wsem.at[2 + i]).start()
    pltpu.make_async_copy(wout, wa.at[pl.ds(3 * d, d)], wsem.at[5]).start()

    def up(j, slot):
        cols = pl.ds(pl.multiple_of(j * TILE, TILE), TILE)
        buf[slot] = dot_nn(ht[...], gp[:, cols]).astype(BF).reshape(buf.shape[1:])

    produce(2, ff // TILE, o_up, r_up, True, up)
    loads[1].wait()
    for i in range(d // 256):
        gh[:, pl.ds(i * 256, 256)] = dot_nt(gp[...], wb[pl.ds(i * 256, 256), :])

    acc[...] = jnp.zeros_like(acc)
    step = 32

    def norm_two(j, part):
        n, scale = normalise(x1[part, :])
        g = gh[part, :]
        acc[1:2, :] += jnp.sum(g * n, 0, keepdims=True)
        acc[3:4, :] += jnp.sum(g, 0, keepdims=True)
        total = gf[part, :].astype(F32) + norm_back(g, n, scale, par[1:2, :].astype(F32))
        gx1[part, :] = total
        gz[part, :] = total.astype(BF)

    tiles(rows // step, step, norm_two)
    for i in range(3):
        pltpu.make_async_copy(wqkv.at[:, pl.ds(i * d, d)], wa.at[pl.ds(i * d, d)], wsem.at[2 + i]).wait()
    pltpu.make_async_copy(wout, wa.at[pl.ds(3 * d, d)], wsem.at[5]).wait()
    ht[...] = att[...].T

    def outp(j, slot):
        cols = pl.ds(pl.multiple_of(j * TILE, TILE), TILE)
        buf[slot] = dot_nn(ht[...], gz[:, cols]).astype(BF).reshape(buf.shape[1:])

    produce(1, d // TILE, o_out, r_out, True, outp)
    for i in range(d // TILE):
        go[:, pl.ds(i * TILE, TILE)] = dot_nt(gz[...], wa[pl.ds(3 * d + i * TILE, TILE), :]).astype(BF)

    fill_bias(biast, prefix[0], c, True)
    prod = go[...].astype(F32) * att[...].astype(F32)
    high = prod.astype(BF)
    low = (prod - high.astype(F32)).astype(BF)
    pick = (
        lax.broadcasted_iota(jnp.int32, (H, d), 1) // HD == lax.broadcasted_iota(jnp.int32, (H, d), 0)
    ).astype(BF)
    deltat[...] = dot_nt(pick, high) + dot_nt(pick, low)
    attend_backward(c, qkv, cross, biast, lset, deltat, go, gqkv, dcross, gq)
    back = remote(dcross, dcross, xsem.at[0], xsem.at[1], core)

    @pl.when(c == 1)
    def _():
        back.start()
        back.wait_send()

    @pl.when(c == 0)
    def _():
        back.wait_recv()

        def add(j, part):
            cols = pl.ds(d, 2 * d)
            gqkv[part, cols] = (gqkv[part, cols].astype(F32) + dcross[part, :].astype(F32)).astype(BF)

        tiles(rows // step, step, add)

    ht[...] = h1[...].T

    def mixed(j, slot):
        cols = pl.ds(pl.multiple_of(j * TILE, TILE), TILE)
        buf[slot] = dot_nn(ht[...], gqkv[:, cols]).astype(BF).reshape(buf.shape[1:])

    produce(0, 3 * d // TILE, o_qkv, r_qkv, True, mixed)
    for i in range(d // 256):
        total = None
        for b in range(3):
            part = dot_nt(gqkv[:, pl.ds(b * d, d)], wa[pl.ds(b * d + i * 256, 256), :])
            total = part if total is None else total + part
        gh[:, pl.ds(i * 256, 256)] = total

    def norm_one(j, part):
        n, scale = normalise(x[part, :].astype(F32))
        g = gh[part, :]
        acc[0:1, :] += jnp.sum(g * n, 0, keepdims=True)
        acc[2:3, :] += jnp.sum(g, 0, keepdims=True)
        grad_in[part, :] = gx1[part, :] + norm_back(g, n, scale, par[0:1, :].astype(F32))

    tiles(rows // step, step, norm_one)
    for zy in range(d // PAIR):
        row = acc[:, pl.ds(zy * PAIR, PAIR)].astype(BF)
        for k in range(4):
            buf[0, zy // 2, zy % 2, k // 2, k % 2, pl.ds(0, 16), pl.ds(0, PAIR)] = row
    mine = buf.at[0, :, :, c, :, pl.ds(0, 16), pl.ds(0, PAIR)]
    theirs = buf.at[0, :, :, 1 - c, :, pl.ds(0, 16), pl.ds(0, PAIR)]
    last = (pltpu.make_async_copy(mine, o_par, osem.at[0]), remote(theirs, r_par, bsem.at[0], rsem.at[4], core))
    for copy in last:
        copy.start()
    last[0].wait()
    last[1].wait_send()
    for w, land in enumerate((r_qkv, r_out, r_up, r_down, r_par)):
        remote(land, land, bsem.at[0], rsem.at[w], core).wait_recv()


def run_backward(nz, prefix, cot, par, wqkv, wout, wup, wdown, x, h1, qkv, cross, lset, att, x1, h2, a, gp):
    rows, d = x.shape
    ff = a.shape[1]
    S = jax.ShapeDtypeStruct
    vm = pl.BlockSpec(memory_space=pltpu.VMEM)
    hbm = pl.BlockSpec(memory_space=pl.ANY)
    V = pltpu.VMEM
    n = nz * 8
    halves = [S((nz, 2, 2, r, k), BF) for r, k in ((d // n, 3 * d), (d // n, d), (d // n, ff), (ff // n, d), (16, PAIR))]
    return pl.pallas_call(
        functools.partial(backward_kernel, nz),
        out_shape=[S((rows, d), F32)] + halves + halves,
        in_specs=[pl.BlockSpec(memory_space=pltpu.SMEM)] + [vm] * 2 + [hbm] * 4 + [vm] * 10,
        out_specs=[vm] + [hbm] * 10,
        scratch_shapes=[
            V((ff, d), BF), V((d, ff), BF), V((2, nz, 2, 2, 2, d // n, TILE), BF), V((2, 2, 2, ff // n, d), BF),
            V((d, rows), BF), V((rows, d), F32), V((rows, d), F32), V((rows, d), BF), V((rows, d), BF),
            V((rows, 3 * d), BF), V((rows, 2 * d), BF), V((rows, rows), F32), V((H, rows), F32),
            V((rows, PAIR), F32), V((16, d), F32), DMA((6,)), DMA((2,)), DMA((2,)), DMA((5,)), DMA((2,)),
        ],
        compiler_params=pltpu.CompilerParams(collective_id=2, has_side_effects=True, vmem_limit_bytes=VMEM_LIMIT),
    )(prefix, cot, par, wqkv, wout, wup, wdown, x, h1, qkv, cross, lset, att, x1, h2, a, gp)


def add_rows(dst, parts, out=None):
    lead, r = dst.shape[:-2], dst.shape[-2]
    out = dst if out is None else out
    step = 16
    count = math.prod(lead) * (r // step)

    @pl.loop(0, count)
    def _(j):
        at = [pl.ds(pl.multiple_of(lax.rem(j, r // step) * step, step), step)]
        rest = lax.div(j, r // step)
        for size in reversed(lead):
            at.insert(0, lax.rem(rest, size))
            rest = lax.div(rest, size)
        at = tuple(at)
        total = dst[at].astype(F32)
        for p in parts:
            total = total + p[at].astype(F32)
        out[at] = total.astype(out.dtype)


class Scatter:
    def __init__(self, nz, place, sums, lands, second, third, outs, sems):
        self.nz, self.place, self.sums, self.lands = nz, place, sums, lands
        self.second, self.third, self.outs = second, third, outs
        self.send, self.recv = sems

    @staticmethod
    def sem_shapes(nw):
        return [DMA((nw, 8)), DMA((nw, 8))]

    def go(self, w, slot, src, dst, device):
        return remote(src, dst, self.send.at[w, slot], self.recv.at[w, slot], device)

    def zt(self, k):
        return lax.rem(self.place[0] + k, self.nz)

    def first_copy(self, w):
        z, y, c, f = self.place
        s, b = self.sums[w], self.second[w]
        return (
            self.go(w, 0, s.at[:, :, 1 - f], b, dev(z, y, c, 1 - f)),
            self.go(w, 0, s.at[:, 1 - y], b, dev(z, 1 - y, c, f)),
        )

    def second_copies(self, w):
        z, y, c, f = self.place
        s, b = self.sums[w], self.third[w]
        nz = self.nz
        return (
            [self.go(w, 1, s.at[:, 1 - y, f], b.at[pl.ds(0, nz)], dev(z, 1 - y, c, f))],
            [
                self.go(w, k, s.at[self.zt(k), y], b.at[pl.ds(2 * (k - 1), 2)], dev(self.zt(k), y, c, f))
                for k in range(1, nz)
            ],
        )

    def third_copies(self, w):
        z, y, c, f = self.place
        s, b = self.sums[w], self.third[w]
        nz = self.nz
        return (
            [
                self.go(w, 1 + k, s.at[self.zt(k), y, f], b.at[nz + k - 1], dev(self.zt(k), y, c, f))
                for k in range(1, nz)
            ],
            [self.go(w, 4, s.at[z, y, 1 - f], b.at[2 * (nz - 1)], dev(z, y, c, 1 - f))],
        )

    def s1(self, w):
        z, y, c, f = self.place
        s, l = self.sums[w], self.lands[w]

        @pl.when(c == 0)
        def _():
            add_rows(s.at[:, :, 1 - f], [l.at[:, :, 1 - f]])
            self.first_copy(w)[0].start()
            add_rows(s.at[:, :, f], [l.at[:, :, f]])

        @pl.when(c == 1)
        def _():
            add_rows(s.at[:, 1 - y], [l.at[:, 1 - y]])
            self.first_copy(w)[1].start()
            add_rows(s.at[:, y], [l.at[:, y]])

    def s2(self, w):
        z, y, c, f = self.place
        s, b = self.sums[w], self.second[w]

        @pl.when(c == 0)
        def _():
            self.first_copy(w)[0].wait_recv()
            add_rows(s.at[:, 1 - y, f], [b.at[:, 1 - y]])
            for copy in self.second_copies(w)[0]:
                copy.start()
            add_rows(s.at[:, y, f], [b.at[:, y]])

        @pl.when(c == 1)
        def _():
            self.first_copy(w)[1].wait_recv()
            for k, copy in enumerate(self.second_copies(w)[1]):
                zz = self.zt(k + 1)
                add_rows(s.at[zz, y], [b.at[zz]])
                copy.start()
            add_rows(s.at[z, y], [b.at[z]])

    def s3(self, w):
        z, y, c, f = self.place
        s, b = self.sums[w], self.third[w]
        nz = self.nz

        @pl.when(c == 0)
        def _():
            self.second_copies(w)[0][0].wait_recv()
            for k, copy in enumerate(self.third_copies(w)[0]):
                zz = self.zt(k + 1)
                add_rows(s.at[zz, y, f], [b.at[zz]])
                copy.start()
            add_rows(s.at[z, y, f], [b.at[z]])

        @pl.when(c == 1)
        def _():
            for copy in self.second_copies(w)[1]:
                copy.wait_recv()
            add_rows(s.at[z, y, 1 - f], [b.at[2 * k + 1 - f] for k in range(nz - 1)])
            self.third_copies(w)[1][0].start()
            add_rows(s.at[z, y, f], [b.at[2 * k + f] for k in range(nz - 1)])

    def s4(self, w):
        z, y, c, f = self.place
        s, b = self.sums[w], self.third[w]
        nz = self.nz

        @pl.when(c == 0)
        def _():
            for copy in self.third_copies(w)[0]:
                copy.wait_recv()
            add_rows(s.at[z, y, f], [b.at[nz + k] for k in range(nz - 1)], self.outs[w])

        @pl.when(c == 1)
        def _():
            self.third_copies(w)[1][0].wait_recv()
            add_rows(s.at[z, y, f], [b.at[2 * (nz - 1)]], self.outs[w])

    def finish(self, w):
        for core in range(2):

            @pl.when(self.place[2] == core)
            def _():
                for copy in [self.first_copy(w)[core]] + self.second_copies(w)[core] + self.third_copies(w)[core]:
                    copy.wait_send()


def scatter_kernel(nz, nw, *refs):
    own, land, outs = refs[:nw], refs[nw : 2 * nw], refs[2 * nw : 3 * nw]
    sums, lands, second, third = (refs[(3 + i) * nw : (4 + i) * nw] for i in range(4))
    send, recv, load = refs[7 * nw :]
    place = coords()
    greet(all_peers(nz, *place)[:-1])
    s = Scatter(nz, place, sums, lands, second, third, outs, (send, recv))
    order = [3, 2, 1, 0, 4]
    copies = {}
    for w in order:
        copies[w] = (
            pltpu.make_async_copy(own[w], sums[w], load.at[w, 0]),
            pltpu.make_async_copy(land[w], lands[w], load.at[w, 1]),
        )
        for copy in copies[w]:
            copy.start()
    for step in range(nw + 3):
        for stage, call in enumerate((s.s1, s.s2, s.s3, s.s4)):
            if 0 <= step - stage < nw:
                w = order[step - stage]
                if stage == 0:
                    for copy in copies[w]:
                        copy.wait()
                call(w)
    for w in range(nw):
        s.finish(w)


def scatter(nz, own, land):
    nw = len(own)
    V = pltpu.VMEM
    shapes = [o.shape for o in own]
    return pl.pallas_call(
        functools.partial(scatter_kernel, nz, nw),
        out_shape=[jax.ShapeDtypeStruct(s[-2:], F32) for s in shapes],
        in_specs=[pl.BlockSpec(memory_space=pl.ANY)] * (2 * nw),
        out_specs=[pl.BlockSpec(memory_space=pltpu.VMEM)] * nw,
        scratch_shapes=[V(s, BF) for s in shapes]
        + [V(s, BF) for s in shapes]
        + [V((nz, 2) + s[-2:], BF) for s in shapes]
        + [V((7,) + s[-2:], BF) for s in shapes]
        + Scatter.sem_shapes(nw)
        + [DMA((nw, 2))],
        compiler_params=pltpu.CompilerParams(collective_id=3, has_side_effects=True, vmem_limit_bytes=VMEM_LIMIT),
    )(*own, *land)


def norm_rows(values, gain, shift):
    center = values - jnp.mean(values, -1, keepdims=True)
    spread = jnp.mean(center * center, -1, keepdims=True)
    return center * lax.rsqrt(spread + EPS) * gain + shift


def collect(w_qkv, w_out, w_up, w_down, gains, shifts):
    return (
        lax.all_gather(w_qkv, ("dp", "fsdp"), axis=0, tiled=True),
        lax.all_gather(w_out, ("dp", "fsdp"), axis=0, tiled=True),
        lax.all_gather(w_up, ("dp", "fsdp"), axis=0, tiled=True),
        lax.all_gather(w_down, ("dp", "fsdp"), axis=0, tiled=True),
        lax.all_gather(gains, ("dp", "fsdp"), axis=1, tiled=True),
        lax.all_gather(shifts, ("dp", "fsdp"), axis=1, tiled=True),
    )


def split_heads(matrix):
    return matrix.reshape(matrix.shape[0], H, HD).transpose(1, 0, 2)


def join_heads(stacked):
    return stacked.transpose(1, 0, 2).reshape(stacked.shape[1], H * HD)


def masked_scores(query_one, key_one, allowed):
    scores = jnp.dot(query_one, key_one.T, preferred_element_type=jnp.float32) * 0.125
    return jnp.where(allowed, scores, -1e30)


def forward(inputs, weights, allowed):
    w_qkv, w_out, w_up, w_down, gains, shifts = weights
    width = inputs.shape[1]
    gain_rows = gains.astype(jnp.float32)
    shift_rows = shifts.astype(jnp.float32)
    normed = norm_rows(inputs, gain_rows[0], shift_rows[0]).astype(jnp.bfloat16)
    mixed = jnp.dot(normed, w_qkv, preferred_element_type=jnp.float32).astype(jnp.bfloat16)
    queries = mixed[:, :width]
    keys_all, values_all = (
        lax.all_gather(mixed[:, width : 2 * width], "fsdp", axis=0, tiled=True),
        lax.all_gather(mixed[:, 2 * width :], "fsdp", axis=0, tiled=True),
    )
    query_heads = split_heads(queries)
    key_heads = split_heads(keys_all)
    value_heads = split_heads(values_all)

    def single(pieces):
        scores = masked_scores(pieces[0], pieces[1], allowed)
        peak_row = jnp.max(scores, -1, keepdims=True)
        log_total = peak_row + jnp.log(jnp.sum(jnp.exp(scores - peak_row), -1, keepdims=True))
        chance = jnp.exp(scores - log_total).astype(jnp.bfloat16)
        return (jnp.dot(chance, pieces[2], preferred_element_type=jnp.float32), log_total[:, 0])

    outputs, totals = lax.map(single, (query_heads, key_heads, value_heads))
    attended = join_heads(outputs).astype(jnp.bfloat16)
    middle = inputs + jnp.dot(attended, w_out, preferred_element_type=jnp.float32)
    normed_two = norm_rows(middle, gain_rows[1], shift_rows[1]).astype(jnp.bfloat16)
    hidden = jnp.dot(normed_two, w_up, preferred_element_type=jnp.float32)
    active = jax.nn.gelu(hidden, approximate=False).astype(jnp.bfloat16)
    result = middle + jnp.dot(active, w_down, preferred_element_type=jnp.float32)
    saved = (
        normed,
        query_heads,
        key_heads,
        value_heads,
        totals,
        attended,
        middle,
        normed_two,
        hidden,
        active,
    )
    return (result, saved)


def on_device(frames_in, prefix_len, w_qkv, w_out, w_up, w_down, gains, shifts, cotangent):
    inputs = frames_in[0].astype(jnp.float32)
    rows_here = inputs.shape[0]
    frames_all = rows_here * lax.axis_size("fsdp")
    first_row = lax.axis_index("fsdp") * rows_here
    places = first_row + jnp.arange(rows_here, dtype=jnp.int32)
    columns = jnp.arange(frames_all, dtype=jnp.int32)
    allowed = (columns[None, :] <= places[:, None]) | (columns[None, :] < prefix_len[0])
    weights = collect(w_qkv, w_out, w_up, w_down, gains, shifts)
    result, saved = forward(inputs, weights, allowed)
    weights = collect(w_qkv, w_out, w_up, w_down, gains, shifts)
    saved = forward(inputs, weights, allowed)[1]
    full_qkv, full_out, full_up, full_down, full_gains, full_shifts = weights
    (
        normed,
        query_heads,
        key_heads,
        value_heads,
        totals,
        attended,
        middle,
        normed_two,
        hidden,
        active,
    ) = saved
    gain_rows = full_gains.astype(jnp.float32)
    shift_rows = full_shifts.astype(jnp.float32)
    grad_top = cotangent[0].astype(jnp.float32)
    grad_branch = grad_top.astype(jnp.bfloat16)
    part_down = jnp.dot(active.T, grad_branch, preferred_element_type=jnp.float32)
    grad_active = jnp.dot(grad_branch, full_down.T, preferred_element_type=jnp.float32)
    gelu_pull = jax.vjp(functools.partial(jax.nn.gelu, approximate=False), hidden)[1]
    grad_hidden = gelu_pull(grad_active)[0].astype(jnp.bfloat16)
    part_up = jnp.dot(normed_two.T, grad_hidden, preferred_element_type=jnp.float32)
    grad_normed_two = jnp.dot(grad_hidden, full_up.T, preferred_element_type=jnp.float32)
    norm_pull_two = jax.vjp(norm_rows, middle, gain_rows[1], shift_rows[1])[1]
    back_middle, grad_gain_two, grad_shift_two = norm_pull_two(grad_normed_two)
    grad_middle = grad_top + back_middle
    grad_attn_out = grad_middle.astype(jnp.bfloat16)
    part_out = jnp.dot(attended.T, grad_attn_out, preferred_element_type=jnp.float32)
    grad_attended = jnp.dot(grad_attn_out, full_out.T, preferred_element_type=jnp.float32).astype(
        jnp.bfloat16
    )
    grad_att_heads = split_heads(grad_attended)

    def single_back(pieces):
        query_one, key_one, value_one, grad_one, log_total = pieces
        scores = masked_scores(query_one, key_one, allowed)
        chance = jnp.exp(scores - log_total[:, None])
        grad_chance = jnp.dot(grad_one, value_one.T, preferred_element_type=jnp.float32)
        inner = jnp.sum(chance * grad_chance, -1, keepdims=True)
        grad_scores = (chance * (grad_chance - inner)).astype(jnp.bfloat16)
        grad_query = jnp.dot(grad_scores, key_one, preferred_element_type=jnp.float32) * 0.125
        grad_key = (
            jnp.einsum("qk,qd->kd", grad_scores, query_one, preferred_element_type=jnp.float32)
            * 0.125
        )
        grad_value = jnp.einsum(
            "qk,qd->kd", chance.astype(jnp.bfloat16), grad_one, preferred_element_type=jnp.float32
        )
        return (grad_query, grad_key, grad_value)

    grad_q_heads, grad_k_heads, grad_v_heads = lax.map(
        single_back, (query_heads, key_heads, value_heads, grad_att_heads, totals)
    )
    grad_keys, grad_values = (
        lax.psum_scatter(
            join_heads(grad_k_heads).astype(jnp.bfloat16), "fsdp", scatter_dimension=0, tiled=True
        ).astype(jnp.float32),
        lax.psum_scatter(
            join_heads(grad_v_heads).astype(jnp.bfloat16), "fsdp", scatter_dimension=0, tiled=True
        ).astype(jnp.float32),
    )
    grad_mixed = jnp.concatenate([join_heads(grad_q_heads), grad_keys, grad_values], 1).astype(
        jnp.bfloat16
    )
    part_qkv = jnp.dot(normed.T, grad_mixed, preferred_element_type=jnp.float32)
    grad_normed = jnp.dot(grad_mixed, full_qkv.T, preferred_element_type=jnp.float32)
    norm_pull_one = jax.vjp(norm_rows, inputs, gain_rows[0], shift_rows[0])[1]
    back_inputs, grad_gain_one, grad_shift_one = norm_pull_one(grad_normed)
    grad_inputs = grad_middle + back_inputs
    part_gains = jnp.stack([grad_gain_one, grad_gain_two])
    part_shifts = jnp.stack([grad_shift_one, grad_shift_two])
    owned = (
        lax.psum_scatter(part_qkv, ("dp", "fsdp"), scatter_dimension=0, tiled=True),
        lax.psum_scatter(part_out, ("dp", "fsdp"), scatter_dimension=0, tiled=True),
        lax.psum_scatter(part_up, ("dp", "fsdp"), scatter_dimension=0, tiled=True),
        lax.psum_scatter(part_down, ("dp", "fsdp"), scatter_dimension=0, tiled=True),
        lax.psum_scatter(part_gains, ("dp", "fsdp"), scatter_dimension=1, tiled=True),
        lax.psum_scatter(part_shifts, ("dp", "fsdp"), scatter_dimension=1, tiled=True),
    )
    return (
        result.astype(jnp.bfloat16)[None],
        grad_inputs[None],
        owned[0],
        owned[1],
        owned[2],
        owned[3],
        owned[4],
        owned[5],
    )


def exchange(array, ndp):
    pairs = []
    for b in range(ndp // 2):
        pairs += [((2 * b + 1) * 2, (2 * b) * 2 + 1), ((2 * b) * 2 + 1, (2 * b + 1) * 2)]
    moved = lax.ppermute(array, ("dp", "fsdp"), pairs)
    stay = lax.rem(lax.axis_index("dp"), 2) == lax.axis_index("fsdp")
    return jnp.where(stay, array, moved)


def fast_device(ndp, frames_in, prefix_len, w_qkv, w_out, w_up, w_down, gains, shifts, cotangent):
    nz = ndp // 4
    d = frames_in.shape[2]
    here = lax.axis_index("dp") * 2 + lax.axis_index("fsdp")
    width = gains.shape[1]
    per = PAIR // width
    rows = jnp.concatenate([gains, shifts, jnp.zeros((12, width), BF)], 0)
    tile = jnp.where(lax.broadcasted_iota(jnp.int32, (16, per, width), 1) == here % per, rows[:, None], 0.0)
    tile = tile.astype(BF).reshape(16, PAIR)
    x = exchange(frames_in[0], ndp)
    cot = exchange(cotangent[0], ndp)
    prefix = exchange(prefix_len, ndp)
    full = gather(nz, (w_qkv, w_out, w_up, w_down, tile))
    weights = [full[i].reshape(-1, full[i].shape[-1]) for i in range(4)]
    par = full[4].reshape(d // PAIR, per, 16, PAIR).sum(1, dtype=BF).transpose(1, 0, 2).reshape(16, d)
    result = run_forward(nz, prefix, x, par, *weights)
    out, saved = result[0], result[1:]
    grads = run_backward(nz, prefix, cot, par, *weights, x, *saved)
    grad_in = exchange(grads[0], ndp)
    owned = scatter(nz, grads[1:6], grads[6:])
    small = lax.dynamic_slice(owned[4], (0, (here % per) * width), (16, width))
    return (exchange(out, ndp)[None], grad_in[None]) + tuple(owned[:4]) + (small[0:2], small[2:4])


def solution(mesh):
    ndp, nf = mesh.shape["dp"], mesh.shape["fsdp"]
    both = P(("dp", "fsdp"), None)
    lanes = P(None, ("dp", "fsdp"))
    block = P("dp", "fsdp", None)
    body = functools.partial(fast_device, ndp) if (nf == 2 and ndp == 16) else on_device
    return jax.shard_map(
        body,
        mesh=mesh,
        in_specs=(block, P("dp"), both, both, both, both, lanes, lanes, block),
        out_specs=(block, block, both, both, both, both, lanes, lanes),
        check_vma=False,
    )
```

```python
import functools
import math

import jax
import jax.numpy as jnp
from jax import lax
from jax.experimental import pallas as pl
from jax.experimental.pallas import tpu as pltpu
from jax.sharding import PartitionSpec as P

H = 16
HD = 64
EPS = 1e-05
BF = jnp.bfloat16
F32 = jnp.float32
LOG2E = math.log2(math.e)
SCALE2 = 0.125 * LOG2E
PAIR = 2 * HD
TILE = 512
MESH = pl.DeviceIdType.MESH
DMA = pltpu.SemaphoreType.DMA
VMEM_LIMIT = 60 * 2**20


def coords():
    dp, f = lax.axis_index("dp"), lax.axis_index("fsdp")
    q = lax.div(dp, 2)
    return lax.div(q, 2), lax.rem(q, 2), lax.rem(dp, 2), f


def dev(z, y, c, f):
    return ((z * 2 + y) * 2 + c, f)


def remote(src, dst, send, recv, device):
    return pltpu.make_async_remote_copy(
        src_ref=src, dst_ref=dst, send_sem=send, recv_sem=recv, device_id=device, device_id_type=MESH
    )


def greet(peers):
    barrier = pltpu.get_barrier_semaphore()
    for peer in peers:
        pl.semaphore_signal(barrier, inc=1, device_id=peer, device_id_type=MESH)
    pl.semaphore_wait(barrier, len(peers))


def all_peers(nz, z, y, c, f):
    peers = [dev(lax.rem(z + k, nz), y, c, f) for k in range(1, nz)]
    return peers + [dev(z, 1 - y, c, f), dev(z, y, c, 1 - f), dev(z, y, 1 - c, f)]


def dot_nn(a, b):
    return lax.dot_general(a, b, (((1,), (0,)), ((), ())), preferred_element_type=F32)


def dot_nt(a, b):
    return lax.dot_general(a, b, (((1,), (1,)), ((), ())), preferred_element_type=F32)


def dot_tn(a, b):
    return lax.dot_general(a, b, (((0,), (0,)), ((), ())), preferred_element_type=F32)


def normalise(v):
    center = v - jnp.mean(v, -1, keepdims=True)
    scale = lax.rsqrt(jnp.mean(center * center, -1, keepdims=True) + EPS)
    return center * scale, scale


def lane_half():
    return lax.broadcasted_iota(jnp.int32, (1, PAIR), 1) // HD


def fill_bias(bias, prefix, c, transposed):
    rows = bias.shape[0]
    step = 64

    def body(j, part):
        a = lax.broadcasted_iota(jnp.int32, (step, rows), 0) + j * step
        b = lax.broadcasted_iota(jnp.int32, (step, rows), 1)
        row, key = (b, a) if transposed else (a, b)
        bias[part, :] = jnp.where((key <= row) | (key + c * rows < prefix), 0.0, -1e30)

    tiles(rows // step, step, body)


def norm_back(gh, n, scale, gain):
    gn = gh * gain
    return scale * (gn - jnp.mean(gn, -1, keepdims=True) - n * jnp.mean(gn * n, -1, keepdims=True))


class Gather:
    def __init__(self, nz, place, shards, outs, chunks, sems):
        self.nz, self.place, self.shards, self.outs, self.chunks = nz, place, shards, outs, chunks
        self.send, self.recv, self.own = sems

    @staticmethod
    def sem_shapes(n):
        return [DMA((n, 12)), DMA((n, 12)), DMA((n,))]

    def mine(self, i):
        w, r0, r, c0, n = self.chunks[i]
        return self.shards[w].at[pl.ds(r0, r), pl.ds(c0, n)]

    def at(self, i, *where):
        w, r0, r, c0, n = self.chunks[i]
        where += (slice(None),) * (4 - len(where))
        return self.outs[w].at[where + (pl.ds(r0, r), pl.ds(c0, n))]

    def hop(self, i, slot, src, dst, device):
        return remote(src, dst, self.send.at[i, slot], self.recv.at[i, slot], device)

    def copies(self, i):
        z, y, c, f = self.place
        nz = self.nz
        every = slice(None)
        core, xp, yp = dev(z, y, 1 - c, f), dev(z, y, c, 1 - f), dev(z, 1 - y, c, f)
        mine, home = self.mine(i), self.at(i, z, y, c, f)

        def same(slot, ref, device):
            return self.hop(i, slot, ref, ref, device)

        zs = [dev(lax.rem(z + k, nz), y, c, f) for k in range(1, nz)]
        line = self.at(i, every, y, c, f)
        other = self.at(i, every, 1 - y, c, f)
        zero = {
            0: [self.hop(i, k, mine, home, zs[k]) for k in range(nz - 1)],
            1: [same(3, line, yp), same(4, line, xp), same(8, line, core)],
            2: [same(5, other, xp), same(9, other, core)],
            3: [same(10, self.at(i, every, every, c, 1 - f), core)],
        }
        rows = self.at(i, z, y, c)
        plane = self.at(i, every, y, c)
        one = {
            0: [self.hop(i, 3, mine, home, xp)],
            1: [same(k, rows, zs[k]) for k in range(nz - 1)],
            2: [same(4, plane, yp), same(8, plane, core)],
            3: [same(9, self.at(i, every, 1 - y, c), core)],
        }
        return zero, one

    def arrivals(self, i):
        z, y, c, f = self.place
        nz = self.nz
        every = slice(None)
        zk = [lax.rem(z + nz - k, nz) for k in range(1, nz)]
        core = dev(z, y, 1 - c, f)

        def here(slot, *where):
            ref = self.at(i, *where)
            return self.hop(i, slot, ref, ref, core)

        zero = {
            1: [here(k, zk[k], y, c, f) for k in range(nz - 1)],
            2: [here(3, every, 1 - y, c, f)],
            3: [here(4, every, y, c, 1 - f), here(5, every, 1 - y, c, 1 - f)],
            4: [here(8, every, y, 1 - c), here(9, every, 1 - y, 1 - c)],
        }
        one = {
            1: [here(3, z, y, c, 1 - f)],
            2: [here(k, zk[k], y, c) for k in range(nz - 1)],
            3: [here(4, every, 1 - y, c)],
            4: [here(8, every, y, 1 - c, f), here(9, every, 1 - y, 1 - c, f), here(10, every, every, 1 - c, 1 - f)],
        }
        return zero, one

    def local(self, i):
        z, y, c, f = self.place
        return pltpu.make_async_copy(self.mine(i), self.at(i, z, y, c, f), self.own.at[i])

    def stage(self, i, s):
        if s == 0:
            self.local(i).start()
        if s == 1:
            self.local(i).wait()
        for core in range(2):

            @pl.when(self.place[2] == core)
            def _():
                if s:
                    for copy in self.arrivals(i)[core][s]:
                        copy.wait_recv()
                if s < 4:
                    for copy in self.copies(i)[core][s]:
                        copy.start()

    def tick(self, t):
        for s in range(4):
            if 0 <= t - s < len(self.chunks):
                self.stage(t - s, s)

    def finish(self, i):
        for core in range(2):

            @pl.when(self.place[2] == core)
            def _():
                for copies in self.copies(i)[core].values():
                    for copy in copies:
                        copy.wait_send()


RING = 5
BLOCK = 32
WIDE = 1024


def tiles(count, size, body, hooks=None):
    @pl.loop(0, count)
    def _(j):
        body(j, pl.ds(pl.multiple_of(j * size, size), size))
        run_hooks(j, hooks)


def run_hooks(j, hooks):
    for at, hook in (hooks or {}).items():

        @pl.when(j == at)
        def _():
            hook()


def flat(ref, cols):
    v = ref[:, :, :, :, cols]
    return v.reshape(math.prod(v.shape[:-1]), v.shape[-1])


def add_blocks(dst, parts, out=None):
    lead = dst.shape[:-2]

    def one(at):
        total = dst[at].astype(F32)
        for p in parts:
            total = total + p[at].astype(F32)
        if out is None:
            dst[at] = total.astype(dst.dtype)
        else:
            out[at] = total

    if not lead:
        one((slice(None), slice(None)))
        return

    @pl.loop(0, math.prod(lead))
    def _(j):
        at, rest = [], j
        for size in reversed(lead):
            at.insert(0, lax.rem(rest, size))
            rest = lax.div(rest, size)
        one(tuple(at) + (slice(None), slice(None)))


class Scatter:
    def __init__(self, nz, place, sums, second, third, outs, sems):
        self.nz, self.place, self.sums, self.second, self.third = nz, place, sums, second, third
        self.outs = outs
        self.send, self.recv, self.free = sems

    @staticmethod
    def sem_shapes(n):
        return [DMA((n, 5)), DMA((n, 5)), pltpu.SemaphoreType.REGULAR((RING,))]

    def peers(self):
        z, y, c, f = self.place
        zs = [dev(lax.rem(z + k, self.nz), y, c, f) for k in range(1, self.nz)]
        return zs, dev(z, 1 - y, c, f), dev(z, y, c, 1 - f)

    def hop(self, i, slot, src, dst, device):
        return remote(src, dst, self.send.at[i, slot], self.recv.at[i, slot], device)

    def copies(self, i):
        z, y, c, f = self.place
        s, b2, b3, nz = self.sums[i], self.second[i], self.third[i], self.nz
        zs, yp, xp = self.peers()
        zt = [lax.rem(z + k, nz) for k in range(1, nz)]
        zero = {
            0: [self.hop(i, 0, s.at[:, :, 1 - f], b2, xp)],
            1: [self.hop(i, 1, s.at[:, 1 - y, f], b3.at[pl.ds(0, nz)], yp)],
            2: [self.hop(i, 2 + k, s.at[zt[k], y, f], b3.at[nz + k], zs[k]) for k in range(nz - 1)],
        }
        one = {
            0: [self.hop(i, 0, s.at[:, 1 - y], b2, yp)],
            1: [self.hop(i, 1 + k, s.at[zt[k], y], b3.at[pl.ds(2 * k, 2)], zs[k]) for k in range(nz - 1)],
            2: [self.hop(i, nz, s.at[z, y, 1 - f], b3.at[2 * (nz - 1)], xp)],
        }
        return zero, one

    def stage(self, i, st):
        z, y, c, f = self.place
        nz = self.nz
        s, b2, b3 = self.sums[i], self.second[i], self.third[i]
        copies = self.copies(i)
        zs, yp, xp = self.peers()
        ringed = i < len(self.sums) - 1
        if st == 0 and ringed and i >= RING:
            pl.semaphore_wait(self.free.at[i % RING], nz + 1)

        @pl.when(c == 0)
        def _():
            if st:
                for copy in copies[0][st - 1]:
                    copy.wait_recv()
            if st == 0:
                copies[0][0][0].start()
            if st == 1:
                add_blocks(s.at[:, 1 - y, f], [b2.at[:, 1 - y]])
                copies[0][1][0].start()
                add_blocks(s.at[:, y, f], [b2.at[:, y]])
            if st == 2:
                for k in range(nz - 1):
                    zt = lax.rem(z + k + 1, nz)
                    add_blocks(s.at[zt, y, f], [b3.at[zt]])
                    copies[0][2][k].start()
                add_blocks(s.at[z, y, f], [b3.at[z]])
            if st == 3:
                add_blocks(s.at[z, y, f], [b3.at[nz + k] for k in range(nz - 1)], self.outs[i])

        @pl.when(c == 1)
        def _():
            if st:
                for copy in copies[1][st - 1]:
                    copy.wait_recv()
            if st == 0:
                copies[1][0][0].start()
            if st == 1:
                for k in range(nz - 1):
                    zt = lax.rem(z + k + 1, nz)
                    add_blocks(s.at[zt, y], [b2.at[zt]])
                    copies[1][1][k].start()
                add_blocks(s.at[z, y], [b2.at[z]])
            if st == 2:
                add_blocks(s.at[z, y, 1 - f], [b3.at[2 * k + 1 - f] for k in range(nz - 1)])
                copies[1][2][0].start()
                add_blocks(s.at[z, y, f], [b3.at[2 * k + f] for k in range(nz - 1)])
            if st == 3:
                add_blocks(s.at[z, y, f], [b3.at[2 * (nz - 1)]], self.outs[i])

        if st == 3 and ringed and i + RING < len(self.sums) - 1:
            for peer in zs + [yp, xp]:
                pl.semaphore_signal(self.free.at[i % RING], inc=1, device_id=peer, device_id_type=MESH)

    def tick(self, t):
        for st in range(4):
            if 0 <= t - st < len(self.sums):
                self.stage(t - st, st)

    def finish(self, i):
        for core in range(2):

            @pl.when(self.place[2] == core)
            def _():
                for copies in self.copies(i)[core].values():
                    for copy in copies:
                        copy.wait_send()


class Producer:
    def __init__(self, place, theirs, land, sems):
        self.place, self.theirs, self.land = place, theirs, land
        self.send, self.recv, self.credit = sems
        z, y, c, f = place
        self.core = dev(z, y, 1 - c, f)
        self.first = True

    def copy(self, slot):
        return remote(self.theirs.at[slot], self.land.at[slot], self.send.at[slot], self.recv.at[slot], self.core)

    def before(self, slot):
        self.copy(slot).wait_send()
        pl.semaphore_wait(self.credit.at[slot], 1)

    def absorb(self, j, target):
        slot = lax.rem(j, 2)
        self.copy(slot).wait_recv()
        for i in range(4):
            ref = target(j, i)
            for k in range(2):
                ref[k] = (ref[k].astype(F32) + self.land[slot, i, k].astype(F32)).astype(BF)
        pl.semaphore_signal(self.credit.at[slot], inc=1, device_id=self.core, device_id_type=MESH)

    def run(self, count, product, pieces, target, hooks=None):
        c = self.place[2]
        first, self.first = self.first, False

        @pl.loop(0, count)
        def _(j):
            slot = lax.rem(j, 2)
            if first:

                @pl.when(j >= 2)
                def _():
                    self.before(slot)
            else:
                self.before(slot)
            v = product(j)
            for i in range(4):
                for k in range(2):
                    a, b = pieces(v, i, k)
                    target(j, i)[k] = jnp.where(c == 0, a, b).astype(BF)
                    self.theirs[slot, i, k] = jnp.where(c == 0, b, a).astype(BF)
            self.copy(slot).start()

            @pl.when(j >= 1)
            def _():
                self.absorb(j - 1, target)

            run_hooks(j, hooks)

        self.absorb(count - 1, target)

    def finish(self):
        for slot in range(2):
            self.before(slot)


def row_pieces(v, i, k):
    a = 4 * BLOCK * i + BLOCK * k
    return v[a : a + BLOCK], v[a + 2 * BLOCK : a + 3 * BLOCK]


def deep_pieces(v, i, k):
    a = 4 * BLOCK * k + BLOCK * i
    return v[a : a + BLOCK], v[a + 8 * BLOCK : a + 9 * BLOCK]


def attend_forward(c, qkv, cross, bias, att, lse, hooks):
    rows, d = att.shape
    half = lane_half()
    lane = lax.broadcasted_iota(jnp.int32, (1, PAIR), 1)
    rt = rows // 2

    def one(q, blocks):
        scores = []
        for keys, _, extra in blocks:
            s = dot_nt(q, keys) * SCALE2
            scores.append(s if extra is None else s + extra)
        peak = functools.reduce(jnp.maximum, [jnp.max(s, -1, keepdims=True) for s in scores])
        total = None
        for s, (_, values, _) in zip(scores, blocks):
            part = dot_nn(jnp.exp2(s - peak).astype(BF), values)
            total = part if total is None else total + part
        return total, peak

    def pair(p, second):
        cols = pl.ds(pl.multiple_of(p * PAIR, PAIR), PAIR)
        kcols = pl.ds(pl.multiple_of(d + p * PAIR, PAIR), PAIR)
        vcols = pl.ds(pl.multiple_of(2 * d + p * PAIR, PAIR), PAIR)
        for r in range(2):
            part = pl.ds(r * rt, rt)
            results = []
            for h in range(2):
                mine = half == h
                q = jnp.where(mine, qkv[part, cols], 0.0).astype(BF)

                def val(v):
                    return jnp.where(mine, v, 1.0).astype(BF)

                if second:
                    blocks = [(cross[:, cols], val(cross[:, kcols]), None)]
                    if r > 0:
                        blocks.append((qkv[pl.ds(0, rt), kcols], val(qkv[pl.ds(0, rt), vcols]), None))
                    blocks.append((qkv[part, kcols], val(qkv[part, vcols]), bias[part, pl.ds(r * rt, rt)]))
                else:
                    blocks = [(qkv[:, kcols], val(qkv[:, vcols]), bias[part, :])]
                total, peak = one(q, blocks)
                sums = pltpu.roll(total, HD, axis=1)
                results.append(total / sums)
                both = jnp.where(mine, sums, total)
                lse[part, :] = jnp.where(lane == 2 * p + h, peak + jnp.log2(both), lse[part, :])
            att[part, cols] = jnp.where(half == 0, results[0], results[1]).astype(BF)

    @pl.loop(0, d // PAIR)
    def _(p):
        for second in range(2):

            @pl.when(c == second)
            def _():
                pair(p, second == 1)

        run_hooks(p, hooks)


def attend_backward(c, qkv, cross, biast, lset, deltat, go, gq, hooks):
    rows, d = go.shape
    half = lane_half()
    rt = rows // 2

    def pair(p, second):
        cols = pl.ds(pl.multiple_of(p * PAIR, PAIR), PAIR)
        kcols = pl.ds(pl.multiple_of(d + p * PAIR, PAIR), PAIR)
        vcols = pl.ds(pl.multiple_of(2 * d + p * PAIR, PAIR), PAIR)
        if second:
            jobs = [(cross, cols, kcols, r * rt, rt, 0, rows, False) for r in range(2)]
            jobs += [(qkv, kcols, vcols, 0, rt, 0, rows, True), (qkv, kcols, vcols, rt, rt, rt, rt, True)]
        else:
            jobs = [(qkv, kcols, vcols, r * rt, rt, 0, rows, True) for r in range(2)]
        gq[...] = jnp.zeros_like(gq)
        for ref, kc, vc, k0, kn, q0, qn, masked in jobs:
            gk = gv = None
            krows, qrows = pl.ds(k0, kn), pl.ds(q0, qn)
            keys, values = ref[krows, kc], ref[krows, vc]
            for h in range(2):
                mine = half == h
                q = jnp.where(mine, qkv[qrows, cols], 0.0).astype(BF)
                g = jnp.where(mine, go[qrows, cols], 0.0).astype(BF)
                km = jnp.where(mine, keys, 0.0).astype(BF)
                s = dot_nt(keys, q) * SCALE2
                if masked:
                    s = s + biast[krows, qrows]
                pr = jnp.exp2(s - lset[pl.ds(2 * p + h, 1), qrows])
                gs = (pr * (dot_nt(values, g) - deltat[pl.ds(2 * p + h, 1), qrows])).astype(BF)
                k1, v1 = dot_nn(gs, q), dot_nn(pr.astype(BF), g)
                gk, gv = (k1, v1) if gk is None else (gk + k1, gv + v1)
                gq[qrows, :] = gq[qrows, :] + dot_tn(gs, km)
            ref[krows, kc] = (gk * 0.125).astype(BF)
            ref[krows, vc] = gv.astype(BF)
        qkv[:, cols] = (gq[...] * 0.125).astype(BF)

    @pl.loop(0, d // PAIR)
    def _(p):
        for second in range(2):

            @pl.when(c == second)
            def _():
                pair(p, second == 1)

        run_hooks(p, hooks)


def layer_kernel(nz, *refs):
    (
        frames_in, cot_in, pre_in, s_qkv, s_out, s_up, s_down, s_par,
        fo, gi, gl, f_qkv, f_out, f_up, f_down, f_par, g_qkv, g_out, g_up, g_down, g_par,
        x, cot, pre, h1, qkv, cross, att, x1, h2, a, gp, wa, wb, gh, gz, go, bias, narrow, lset, deltat,
        acc, par, parv, ht, theirs, land, sdown, spar, ptheirs, pland, second, third, psecond, pthird,
        ag_send, ag_recv, ag_own, rs_send, rs_recv, rs_free, p_send, p_recv, p_credit,
        load_sem, swap_sem, io_sem, io_recv,
    ) = refs
    place = z, y, c, f = coords()
    rows, d = x.shape
    ff = a.shape[-1]
    core, far = dev(z, y, 1 - c, f), dev(z, y, 1 - c, 1 - f)
    straight = c == f
    nk = d // WIDE

    chunks = [(4, 0, 16, 0, PAIR)]
    chunks += [(0, 0, BLOCK, b * d, d) for b in (1, 2, 0)]
    chunks += [(1, 0, BLOCK, 0, d)]
    chunks += [(2, 0, BLOCK, k * WIDE, WIDE) for k in range(ff // WIDE)]
    chunks += [(3, 0, 4 * BLOCK, k * 256, 256) for k in range(d // 256)]
    ag = Gather(nz, place, (s_qkv, s_out, s_up, s_down, s_par), (f_qkv, f_out, f_up, f_down, f_par), chunks, (ag_send, ag_recv, ag_own))

    ups, downs = ff // WIDE, 4
    sums = [sdown.at[k] for k in range(downs)]
    sums += [a.at[:, :, :, :, pl.ds(k * WIDE, WIDE)] for k in range(ups)]
    sums += [gp.at[:, :, :, :, pl.ds(b * d, d)] for b in (3, 1, 2, 0)]
    goes = [g_down.at[pl.ds(k * BLOCK, BLOCK)] for k in range(downs)]
    goes += [g_up.at[:, pl.ds(k * WIDE, WIDE)] for k in range(ups)]
    goes += [g_out] + [g_qkv.at[:, pl.ds(b * d, d)] for b in (1, 2, 0)]
    n = len(sums)
    rs = Scatter(
        nz, place, sums + [spar], [second.at[i % RING] for i in range(n)] + [psecond],
        [third.at[i % RING] for i in range(n)] + [pthird], goes + [g_par], (rs_send, rs_recv, rs_free),
    )
    maker = Producer(place, theirs, land, (p_send, p_recv, p_credit))

    greet(all_peers(nz, *place) + [far])

    swaps = []
    for i, (src, dst) in enumerate(((frames_in, x), (pre_in, pre), (cot_in, cot))):
        swaps.append((pltpu.make_async_copy(src, dst, swap_sem.at[i, 0]), remote(src, dst, swap_sem.at[i, 1], swap_sem.at[i, 2], far)))

    def swap_start(i):
        @pl.when(straight)
        def _():
            swaps[i][0].start()

        @pl.when(jnp.logical_not(straight))
        def _():
            swaps[i][1].start()

    def swap_wait(i):
        @pl.when(straight)
        def _():
            swaps[i][0].wait()

        @pl.when(jnp.logical_not(straight))
        def _():
            swaps[i][1].wait()

    def ag_tick(t):
        return lambda: ag.tick(t)

    def rs_tick(t):
        return lambda: rs.tick(t)

    def small(b):
        return pl.ds(b * BLOCK, BLOCK)

    def load(i, src, dst):
        return pltpu.make_async_copy(src, dst, load_sem.at[i])

    def load_block(i, b):
        if b == 3:
            return load(i, f_out, wa.at[:, :, :, :, small(3)])
        return load(i, f_qkv.at[:, :, :, :, :, pl.ds(b * d, d)], wa.at[:, :, :, :, small(b)])

    def block(b, at=slice(None)):
        v = wa[at, :, :, :, small(b)]
        return v.reshape(math.prod(v.shape[:-1]), d)

    ag.tick(0)
    swap_start(0)
    swap_start(1)
    ag.tick(1)
    ag.tick(2)
    swap_wait(0)
    swap_wait(1)
    ag.tick(3)
    swap_start(2)
    ag.stage(0, 4)
    get_par = load(0, f_par, parv)
    get_par.start()
    fill_bias(bias, pre[0:1, 0:1], c, False)
    get_par.wait()
    for t in range(d // PAIR):
        total = None
        for k in range(4):
            piece = parv[t // 2, t % 2, k // 2, k % 2].astype(F32)
            total = piece if total is None else total + piece
        par[:, pl.ds(t * PAIR, PAIR)] = total
    step = 64

    def norm_one(j, part):
        nrm, _ = normalise(x[part, :].astype(F32))
        h1[part, :] = (nrm * par[0:1, :] + par[2:3, :]).astype(BF)

    tiles(rows // step, step, norm_one)
    keyvals = remote(qkv.at[:, pl.ds(d, 2 * d)], cross, swap_sem.at[3, 1], swap_sem.at[3, 2], core)
    for i, b in enumerate((1, 2, 0)):
        ag.tick(4 + i)
        ag.stage(1 + i, 4)
        get = load_block(1 + i, b)
        get.start()
        get.wait()
        for t in range(d // TILE):
            cols = pl.ds(t * TILE, TILE)
            w = wa[:, :, :, :, small(b), cols].reshape(d, TILE)
            qkv[:, pl.ds(b * d + t * TILE, TILE)] = dot_nn(h1[...], w).astype(BF)
        if b == 2:

            @pl.when(c == 0)
            def _():
                keyvals.start()

    @pl.when(c == 1)
    def _():
        keyvals.wait_recv()

    narrow[...] = jnp.zeros_like(narrow)
    attend_forward(c, qkv, cross, bias, att, narrow, {1: ag_tick(7), 6: ag_tick(8)})
    ag.stage(4, 4)
    get_out = load_block(4, 3)
    get_out.start()

    @pl.when(c == 0)
    def _():
        keyvals.wait_send()

    lset[...] = narrow[...].T[:H, :]

    def get_up(k):
        return load(5 + k, f_up.at[:, :, :, :, :, pl.ds(k * WIDE, WIDE)], wb.at[:, :, :, :, :, pl.ds(k * WIDE, WIDE)])

    ag.stage(5, 4)
    get_up(0).start()
    get_out.wait()
    for t in range(d // TILE):
        cols = pl.ds(t * TILE, TILE)
        w = wa[:, :, :, :, small(3), cols].reshape(d, TILE)
        x1[:, cols] = x[:, cols].astype(F32) + dot_nn(att[...], w)
    ag.tick(9)

    def norm_two(j, part):
        nrm, _ = normalise(x1[part, :])
        h2[part, :] = (nrm * par[1:2, :] + par[3:4, :]).astype(BF)

    tiles(rows // step, step, norm_two)
    u = gh.at[:, pl.ds(0, TILE)]

    def up(cols):
        gh[:, pl.ds(0, TILE)] = dot_nn(h2[...], wb[:, :, :, :, :, cols].reshape(d, TILE))

        @pl.loop(0, rows // BLOCK)
        def _(j):
            at = (lax.div(j, 4), lax.rem(lax.div(j, 2), 2), lax.rem(j, 2), slice(None), cols)
            v = gh[pl.ds(pl.multiple_of(j * BLOCK, BLOCK), BLOCK), pl.ds(0, TILE)]
            phi = 0.5 * (1.0 + lax.erf(v * math.sqrt(0.5)))
            dens = jnp.exp2(v * v * (-0.5 * LOG2E)) * (1.0 / math.sqrt(2.0 * math.pi))
            a[at] = (v * phi).astype(BF)
            gp[at] = (phi + v * dens).astype(BF)

    for k in range(ups):
        if k:
            ag.stage(5 + k, 4)
            get_up(k).start()
        get_up(k).wait()
        tiles(2, TILE, lambda j, cols: up(pl.ds(pl.multiple_of(k * WIDE + j * TILE, TILE), TILE)))
        ag.tick(10 + k)

    def get_down(k):
        cols = pl.ds(k * 256, 256)
        return load(9 + k, f_down.at[:, :, :, :, :, cols], wa.at[:, :, :, :, :, cols])

    swap_wait(2)

    def down_product(j):
        return dot_tn(flat(a, pl.ds(pl.multiple_of(j * TILE, TILE), TILE)), cot[...])

    maker.run(8, down_product, deep_pieces, lambda j, i: sdown.at[i, lax.div(j, 2), lax.rem(j, 2)], {3: ag_tick(14)})
    rs.tick(0)
    ag.tick(15)
    outs = []
    for k in range(4):
        ag.stage(9 + k, 4)
        get_down(k).start()
    rs.tick(1)
    for k in range(4):
        cols = pl.ds(k * 256, 256)
        get_down(k).wait()
        w = wa[:, :, :, :, :, cols].reshape(ff, 256)
        go[:, cols] = (x1[:, cols] + dot_nn(flat(a, slice(None)), w)).astype(BF)
        outs.append((pltpu.make_async_copy(go.at[:, cols], fo.at[:, cols], io_sem.at[k]), remote(go.at[:, cols], fo.at[:, cols], io_sem.at[k], io_recv.at[k], far)))

        @pl.when(straight)
        def _():
            outs[k][0].start()

        @pl.when(jnp.logical_not(straight))
        def _():
            outs[k][1].start()

    def act(j, cols):
        w = wa[lax.div(j, 2), lax.rem(j, 2)].reshape(TILE, d)
        v = dot_nt(cot[...], w) * flat(gp, cols).astype(F32)
        gp[:, :, :, :, cols] = v.astype(BF).reshape(a.shape[:-1] + (TILE,))

    tiles(8, TILE, act, {4: rs_tick(2)})
    for i, b in enumerate((3, 0, 1, 2)):
        load_block(13 + i, b).start()
    ht[...] = h2[...].T
    for i in range(nz):
        gh[:, pl.ds(i * 256, 256)] = dot_nt(flat(gp, slice(None)), wb[i].reshape(256, ff))
        if i == 1:
            rs.tick(3)
    acc[...] = jnp.zeros_like(acc)
    step = 32

    def back_two(j, part):
        nrm, scale = normalise(x1[part, :])
        g = gh[part, :]
        acc[1:2, :] += jnp.sum(g * nrm, 0, keepdims=True)
        acc[3:4, :] += jnp.sum(g, 0, keepdims=True)
        total = cot[part, :].astype(F32) + norm_back(g, nrm, scale, par[1:2, :])
        x1[part, :] = total
        gz[part, :] = total.astype(BF)

    tiles(rows // step, step, back_two)

    def row_half(j):
        return ht[pl.ds(pl.multiple_of(lax.rem(j, 2) * TILE, TILE), TILE), :]

    def wide(j):
        return pl.ds(pl.multiple_of(lax.div(j, 2) * WIDE, WIDE), WIDE)

    def up_product(j):
        return dot_nn(row_half(j), flat(gp, wide(j)))

    def target(ref, first):
        def of(j, i):
            cols = pl.ds(pl.multiple_of(first + lax.div(j, 2) * WIDE, WIDE), WIDE)
            return ref.at[2 * lax.rem(j, 2) + i // 2, i % 2, :, :, cols]

        return of

    maker.run(2 * ups, up_product, row_pieces, target(a, 0), {3: rs_tick(4)})
    for k in range(4):

        @pl.when(straight)
        def _():
            outs[k][0].wait()

        @pl.when(jnp.logical_not(straight))
        def _():
            outs[k][1].wait()

    load_block(13, 3).wait()
    for i in range(2):
        go[:, pl.ds(i * TILE, TILE)] = dot_nt(gz[...], block(3, pl.ds(2 * i, 2))).astype(BF)
    rs.tick(5)
    ht[...] = att[...].T
    maker.run(2, lambda j: dot_nn(row_half(j), gz[...]), row_pieces, target(gp, 3 * d))
    fill_bias(bias, pre[0:1, 0:1], c, True)
    prod = go[...].astype(F32) * att[...].astype(F32)
    high = prod.astype(BF)
    low = (prod - high.astype(F32)).astype(BF)
    pick = (
        lax.broadcasted_iota(jnp.int32, (H, d), 1) // HD == lax.broadcasted_iota(jnp.int32, (H, d), 0)
    ).astype(BF)
    deltat[...] = dot_nt(pick, high) + dot_nt(pick, low)
    attend_backward(c, qkv, cross, bias, lset, deltat, go, narrow, {0: rs_tick(6), 3: rs_tick(7), 6: rs_tick(8)})
    back = remote(cross, cross, swap_sem.at[4, 1], swap_sem.at[4, 2], core)

    @pl.when(c == 1)
    def _():
        back.start()

    ht[...] = h1[...].T

    @pl.when(c == 1)
    def _():
        back.wait_send()

    @pl.when(c == 0)
    def _():
        back.wait_recv()

        def add(j, part):
            cols = pl.ds(d, 2 * d)
            qkv[part, cols] = (qkv[part, cols].astype(F32) + cross[part, :].astype(F32)).astype(BF)

        tiles(rows // step, step, add)

    def make(b):
        maker.run(2, lambda j: dot_nn(row_half(j), qkv[:, pl.ds(b * d, d)]), row_pieces, target(gp, b * d))

    for i, b in enumerate((1, 2, 0)):
        make(b)
        rs.tick(9 + i)
    for i, b in enumerate((0, 1, 2)):
        load_block(14 + i, b).wait()
    for i in range(nz):
        total = None
        for b in range(3):
            part = dot_nt(qkv[:, pl.ds(b * d, d)], block(b, pl.ds(i, 1)))
            total = part if total is None else total + part
        gh[:, pl.ds(i * 256, 256)] = total

    def back_one(j, part):
        nrm, scale = normalise(x[part, :].astype(F32))
        g = gh[part, :]
        acc[0:1, :] += jnp.sum(g * nrm, 0, keepdims=True)
        acc[2:3, :] += jnp.sum(g, 0, keepdims=True)
        total = x1[part, :] + norm_back(g, nrm, scale, par[0:1, :])
        gh[part, :] = total
        gz[part, :] = total.astype(BF)

    tiles(rows // step, step, back_one)
    keep = pltpu.make_async_copy(gh, gi, io_sem.at[4])
    give = remote(gz, gl, io_sem.at[4], io_recv.at[4], far)

    @pl.when(straight)
    def _():
        keep.start()

    @pl.when(jnp.logical_not(straight))
    def _():
        give.start()

    for t in range(d // PAIR):
        row = acc[:, pl.ds(t * PAIR, PAIR)].astype(BF)
        for k in range(2):
            spar[t // 2, t % 2, k] = row
            ptheirs[t // 2, t % 2, k] = row
    pars = remote(ptheirs, pland, io_sem.at[5], io_recv.at[5], core)
    pars.start()
    pars.wait_recv()
    add_blocks(spar, [pland])
    for t in range(12, n + 4):
        rs.tick(t)

    @pl.when(straight)
    def _():
        keep.wait()

    @pl.when(jnp.logical_not(straight))
    def _():
        give.wait()

    pars.wait_send()
    for i in range(len(chunks)):
        ag.finish(i)
    for i in range(n + 1):
        rs.finish(i)
    maker.finish()


def layer(nz, frames_in, cot, pre, w_qkv, w_out, w_up, w_down, tile):
    rows, d = frames_in.shape
    ff = w_up.shape[1]
    S = jax.ShapeDtypeStruct
    V = pltpu.VMEM
    REG = pltpu.SemaphoreType.REGULAR
    hbm, vm = pl.BlockSpec(memory_space=pl.ANY), pl.BlockSpec(memory_space=V)
    shards = (w_qkv, w_out, w_up, w_down, tile)
    parts = (nz, 2, 2, BLOCK)
    full = (nz, 2, 2, 2)
    return pl.pallas_call(
        functools.partial(layer_kernel, nz),
        out_shape=[S((rows, d), BF), S((rows, d), F32), S((rows, d), BF)]
        + [S(full + w.shape, BF) for w in shards]
        + [S(w.shape, F32) for w in shards],
        in_specs=[hbm] * 8,
        out_specs=[hbm] * 8 + [vm] * 5,
        scratch_shapes=[
            V((rows, d), BF), V((rows, d), BF), V((8, PAIR), jnp.int32), V((rows, d), BF), V((rows, 3 * d), BF),
            V((rows, 2 * d), BF), V((rows, d), BF), V((rows, d), F32), V((rows, d), BF),
            V(parts + (ff,), BF), V(parts + (ff,), BF),
            V(full + w_down.shape, BF), V(full + w_up.shape, BF),
            V((rows, d), F32), V((rows, d), BF), V((rows, d), BF), V((rows, rows), F32), V((rows, PAIR), F32),
            V((H, rows), F32), V((H, rows), F32), V((16, d), F32), V((16, d), F32), V(full + (16, PAIR), BF),
            V((d, rows), BF), V((2, 4, 2, BLOCK, WIDE), BF), V((2, 4, 2, BLOCK, WIDE), BF),
            V((4,) + parts + (d,), BF), V((nz, 2, 2, 16, PAIR), BF), V((nz, 2, 2, 16, PAIR), BF), V((nz, 2, 2, 16, PAIR), BF),
            V((RING, nz, 2, BLOCK, WIDE), BF), V((RING, 7, BLOCK, WIDE), BF), V((nz, 2, 16, PAIR), BF), V((7, 16, PAIR), BF),
        ]
        + Gather.sem_shapes(13)
        + Scatter.sem_shapes(13)
        + [DMA((2,)), DMA((2,)), REG((2,)), DMA((17,)), DMA((5, 3)), DMA((6,)), DMA((6,))],
        compiler_params=pltpu.CompilerParams(collective_id=0, has_side_effects=True, vmem_limit_bytes=63 * 2**20),
    )(frames_in, cot, pre, *shards)


def norm_rows(values, gain, shift):
    center = values - jnp.mean(values, -1, keepdims=True)
    spread = jnp.mean(center * center, -1, keepdims=True)
    return center * lax.rsqrt(spread + EPS) * gain + shift


def collect(w_qkv, w_out, w_up, w_down, gains, shifts):
    return (
        lax.all_gather(w_qkv, ("dp", "fsdp"), axis=0, tiled=True),
        lax.all_gather(w_out, ("dp", "fsdp"), axis=0, tiled=True),
        lax.all_gather(w_up, ("dp", "fsdp"), axis=0, tiled=True),
        lax.all_gather(w_down, ("dp", "fsdp"), axis=0, tiled=True),
        lax.all_gather(gains, ("dp", "fsdp"), axis=1, tiled=True),
        lax.all_gather(shifts, ("dp", "fsdp"), axis=1, tiled=True),
    )


def split_heads(matrix):
    return matrix.reshape(matrix.shape[0], H, HD).transpose(1, 0, 2)


def join_heads(stacked):
    return stacked.transpose(1, 0, 2).reshape(stacked.shape[1], H * HD)


def masked_scores(query_one, key_one, allowed):
    scores = jnp.dot(query_one, key_one.T, preferred_element_type=jnp.float32) * 0.125
    return jnp.where(allowed, scores, -1e30)


def forward(inputs, weights, allowed):
    w_qkv, w_out, w_up, w_down, gains, shifts = weights
    width = inputs.shape[1]
    gain_rows = gains.astype(jnp.float32)
    shift_rows = shifts.astype(jnp.float32)
    normed = norm_rows(inputs, gain_rows[0], shift_rows[0]).astype(jnp.bfloat16)
    mixed = jnp.dot(normed, w_qkv, preferred_element_type=jnp.float32).astype(jnp.bfloat16)
    queries = mixed[:, :width]
    keys_all, values_all = (
        lax.all_gather(mixed[:, width : 2 * width], "fsdp", axis=0, tiled=True),
        lax.all_gather(mixed[:, 2 * width :], "fsdp", axis=0, tiled=True),
    )
    query_heads = split_heads(queries)
    key_heads = split_heads(keys_all)
    value_heads = split_heads(values_all)

    def single(pieces):
        scores = masked_scores(pieces[0], pieces[1], allowed)
        peak_row = jnp.max(scores, -1, keepdims=True)
        log_total = peak_row + jnp.log(jnp.sum(jnp.exp(scores - peak_row), -1, keepdims=True))
        chance = jnp.exp(scores - log_total).astype(jnp.bfloat16)
        return (jnp.dot(chance, pieces[2], preferred_element_type=jnp.float32), log_total[:, 0])

    outputs, totals = lax.map(single, (query_heads, key_heads, value_heads))
    attended = join_heads(outputs).astype(jnp.bfloat16)
    middle = inputs + jnp.dot(attended, w_out, preferred_element_type=jnp.float32)
    normed_two = norm_rows(middle, gain_rows[1], shift_rows[1]).astype(jnp.bfloat16)
    hidden = jnp.dot(normed_two, w_up, preferred_element_type=jnp.float32)
    active = jax.nn.gelu(hidden, approximate=False).astype(jnp.bfloat16)
    result = middle + jnp.dot(active, w_down, preferred_element_type=jnp.float32)
    saved = (
        normed,
        query_heads,
        key_heads,
        value_heads,
        totals,
        attended,
        middle,
        normed_two,
        hidden,
        active,
    )
    return (result, saved)


def on_device(frames_in, prefix_len, w_qkv, w_out, w_up, w_down, gains, shifts, cotangent):
    inputs = frames_in[0].astype(jnp.float32)
    rows_here = inputs.shape[0]
    frames_all = rows_here * lax.axis_size("fsdp")
    first_row = lax.axis_index("fsdp") * rows_here
    places = first_row + jnp.arange(rows_here, dtype=jnp.int32)
    columns = jnp.arange(frames_all, dtype=jnp.int32)
    allowed = (columns[None, :] <= places[:, None]) | (columns[None, :] < prefix_len[0])
    weights = collect(w_qkv, w_out, w_up, w_down, gains, shifts)
    result, saved = forward(inputs, weights, allowed)
    weights = collect(w_qkv, w_out, w_up, w_down, gains, shifts)
    saved = forward(inputs, weights, allowed)[1]
    full_qkv, full_out, full_up, full_down, full_gains, full_shifts = weights
    (
        normed,
        query_heads,
        key_heads,
        value_heads,
        totals,
        attended,
        middle,
        normed_two,
        hidden,
        active,
    ) = saved
    gain_rows = full_gains.astype(jnp.float32)
    shift_rows = full_shifts.astype(jnp.float32)
    grad_top = cotangent[0].astype(jnp.float32)
    grad_branch = grad_top.astype(jnp.bfloat16)
    part_down = jnp.dot(active.T, grad_branch, preferred_element_type=jnp.float32)
    grad_active = jnp.dot(grad_branch, full_down.T, preferred_element_type=jnp.float32)
    gelu_pull = jax.vjp(functools.partial(jax.nn.gelu, approximate=False), hidden)[1]
    grad_hidden = gelu_pull(grad_active)[0].astype(jnp.bfloat16)
    part_up = jnp.dot(normed_two.T, grad_hidden, preferred_element_type=jnp.float32)
    grad_normed_two = jnp.dot(grad_hidden, full_up.T, preferred_element_type=jnp.float32)
    norm_pull_two = jax.vjp(norm_rows, middle, gain_rows[1], shift_rows[1])[1]
    back_middle, grad_gain_two, grad_shift_two = norm_pull_two(grad_normed_two)
    grad_middle = grad_top + back_middle
    grad_attn_out = grad_middle.astype(jnp.bfloat16)
    part_out = jnp.dot(attended.T, grad_attn_out, preferred_element_type=jnp.float32)
    grad_attended = jnp.dot(grad_attn_out, full_out.T, preferred_element_type=jnp.float32).astype(
        jnp.bfloat16
    )
    grad_att_heads = split_heads(grad_attended)

    def single_back(pieces):
        query_one, key_one, value_one, grad_one, log_total = pieces
        scores = masked_scores(query_one, key_one, allowed)
        chance = jnp.exp(scores - log_total[:, None])
        grad_chance = jnp.dot(grad_one, value_one.T, preferred_element_type=jnp.float32)
        inner = jnp.sum(chance * grad_chance, -1, keepdims=True)
        grad_scores = (chance * (grad_chance - inner)).astype(jnp.bfloat16)
        grad_query = jnp.dot(grad_scores, key_one, preferred_element_type=jnp.float32) * 0.125
        grad_key = (
            jnp.einsum("qk,qd->kd", grad_scores, query_one, preferred_element_type=jnp.float32)
            * 0.125
        )
        grad_value = jnp.einsum(
            "qk,qd->kd", chance.astype(jnp.bfloat16), grad_one, preferred_element_type=jnp.float32
        )
        return (grad_query, grad_key, grad_value)

    grad_q_heads, grad_k_heads, grad_v_heads = lax.map(
        single_back, (query_heads, key_heads, value_heads, grad_att_heads, totals)
    )
    grad_keys, grad_values = (
        lax.psum_scatter(
            join_heads(grad_k_heads).astype(jnp.bfloat16), "fsdp", scatter_dimension=0, tiled=True
        ).astype(jnp.float32),
        lax.psum_scatter(
            join_heads(grad_v_heads).astype(jnp.bfloat16), "fsdp", scatter_dimension=0, tiled=True
        ).astype(jnp.float32),
    )
    grad_mixed = jnp.concatenate([join_heads(grad_q_heads), grad_keys, grad_values], 1).astype(
        jnp.bfloat16
    )
    part_qkv = jnp.dot(normed.T, grad_mixed, preferred_element_type=jnp.float32)
    grad_normed = jnp.dot(grad_mixed, full_qkv.T, preferred_element_type=jnp.float32)
    norm_pull_one = jax.vjp(norm_rows, inputs, gain_rows[0], shift_rows[0])[1]
    back_inputs, grad_gain_one, grad_shift_one = norm_pull_one(grad_normed)
    grad_inputs = grad_middle + back_inputs
    part_gains = jnp.stack([grad_gain_one, grad_gain_two])
    part_shifts = jnp.stack([grad_shift_one, grad_shift_two])
    owned = (
        lax.psum_scatter(part_qkv, ("dp", "fsdp"), scatter_dimension=0, tiled=True),
        lax.psum_scatter(part_out, ("dp", "fsdp"), scatter_dimension=0, tiled=True),
        lax.psum_scatter(part_up, ("dp", "fsdp"), scatter_dimension=0, tiled=True),
        lax.psum_scatter(part_down, ("dp", "fsdp"), scatter_dimension=0, tiled=True),
        lax.psum_scatter(part_gains, ("dp", "fsdp"), scatter_dimension=1, tiled=True),
        lax.psum_scatter(part_shifts, ("dp", "fsdp"), scatter_dimension=1, tiled=True),
    )
    return (
        result.astype(jnp.bfloat16)[None],
        grad_inputs[None],
        owned[0],
        owned[1],
        owned[2],
        owned[3],
        owned[4],
        owned[5],
    )


def fast_device(ndp, frames_in, prefix_len, w_qkv, w_out, w_up, w_down, gains, shifts, cotangent):
    here = lax.axis_index("dp") * 2 + lax.axis_index("fsdp")
    width = gains.shape[1]
    per = PAIR // width
    rows = jnp.concatenate([gains, shifts, jnp.zeros((12, width), BF)], 0)
    tile = jnp.where(lax.broadcasted_iota(jnp.int32, (16, per, width), 1) == here % per, rows[:, None], 0.0)
    tile = tile.astype(BF).reshape(16, PAIR)
    pre = jnp.broadcast_to(prefix_len[None], (8, PAIR))
    result = layer(ndp // 4, frames_in[0], cotangent[0], pre, w_qkv, w_out, w_up, w_down, tile)
    stay = lax.rem(lax.axis_index("dp"), 2) == lax.axis_index("fsdp")
    grad_in = jnp.where(stay, result[1], result[2].astype(F32))
    grads = result[8:]
    small = lax.dynamic_slice(grads[4], (0, (here % per) * width), (16, width))
    return (result[0][None], grad_in[None]) + tuple(grads[:4]) + (small[0:2], small[2:4])


def solution(mesh):
    ndp, nf = mesh.shape["dp"], mesh.shape["fsdp"]
    both = P(("dp", "fsdp"), None)
    lanes = P(None, ("dp", "fsdp"))
    block = P("dp", "fsdp", None)
    body = functools.partial(fast_device, ndp) if (nf == 2 and ndp == 16) else on_device
    return jax.shard_map(
        body,
        mesh=mesh,
        in_specs=(block, P("dp"), both, both, both, both, lanes, lanes, block),
        out_specs=(block, block, both, both, both, both, lanes, lanes),
        check_vma=False,
    )
```

```python
import functools
import math

import jax
import jax.numpy as jnp
from jax import lax
from jax.experimental import pallas as pl
from jax.experimental.pallas import tpu as pltpu
from jax.sharding import PartitionSpec as P

H = 16
HD = 64
EPS = 1e-05
BF = jnp.bfloat16
F32 = jnp.float32
LOG2E = math.log2(math.e)
SCALE2 = 0.125 * LOG2E
PAIR = 2 * HD
TILE = 512
MESH = pl.DeviceIdType.MESH
DMA = pltpu.SemaphoreType.DMA
VMEM_LIMIT = 60 * 2**20


def coords():
    dp, f = lax.axis_index("dp"), lax.axis_index("fsdp")
    q = lax.div(dp, 2)
    return lax.div(q, 2), lax.rem(q, 2), lax.rem(dp, 2), f


def dev(z, y, c, f):
    return ((z * 2 + y) * 2 + c, f)


def remote(src, dst, send, recv, device):
    return pltpu.make_async_remote_copy(
        src_ref=src, dst_ref=dst, send_sem=send, recv_sem=recv, device_id=device, device_id_type=MESH
    )


def greet(peers):
    barrier = pltpu.get_barrier_semaphore()
    for peer in peers:
        pl.semaphore_signal(barrier, inc=1, device_id=peer, device_id_type=MESH)
    pl.semaphore_wait(barrier, len(peers))


def all_peers(nz, z, y, c, f):
    peers = [dev(lax.rem(z + k, nz), y, c, f) for k in range(1, nz)]
    return peers + [dev(z, 1 - y, c, f), dev(z, y, c, 1 - f), dev(z, y, 1 - c, f)]


def dot_nn(a, b):
    return lax.dot_general(a, b, (((1,), (0,)), ((), ())), preferred_element_type=F32)


def dot_nt(a, b):
    return lax.dot_general(a, b, (((1,), (1,)), ((), ())), preferred_element_type=F32)


def dot_tn(a, b):
    return lax.dot_general(a, b, (((0,), (0,)), ((), ())), preferred_element_type=F32)


def normalise(v):
    center = v - jnp.mean(v, -1, keepdims=True)
    scale = lax.rsqrt(jnp.mean(center * center, -1, keepdims=True) + EPS)
    return center * scale, scale


def lane_half():
    return lax.broadcasted_iota(jnp.int32, (1, PAIR), 1) // HD


def fill_bias(bias, prefix, c, transposed):
    rows = bias.shape[0]
    step = 64

    def body(j, part):
        a = lax.broadcasted_iota(jnp.int32, (step, rows), 0) + j * step
        b = lax.broadcasted_iota(jnp.int32, (step, rows), 1)
        row, key = (b, a) if transposed else (a, b)
        bias[part, :] = jnp.where((key <= row) | (key + c * rows < prefix), 0.0, -1e30)

    tiles(rows // step, step, body)


def norm_back(gh, n, scale, gain):
    gn = gh * gain
    return scale * (gn - jnp.mean(gn, -1, keepdims=True) - n * jnp.mean(gn * n, -1, keepdims=True))


class Gather:
    def __init__(self, nz, place, shards, outs, chunks, sems):
        self.nz, self.place, self.shards, self.outs, self.chunks = nz, place, shards, outs, chunks
        self.send, self.recv, self.own = sems

    @staticmethod
    def sem_shapes(n):
        return [DMA((n, 12)), DMA((n, 12)), DMA((n,))]

    def mine(self, i):
        w, r0, r, c0, n = self.chunks[i]
        return self.shards[w].at[pl.ds(r0, r), pl.ds(c0, n)]

    def at(self, i, *where):
        w, r0, r, c0, n = self.chunks[i]
        where += (slice(None),) * (4 - len(where))
        return self.outs[w].at[where + (pl.ds(r0, r), pl.ds(c0, n))]

    def hop(self, i, slot, src, dst, device):
        return remote(src, dst, self.send.at[i, slot], self.recv.at[i, slot], device)

    def copies(self, i):
        z, y, c, f = self.place
        nz = self.nz
        every = slice(None)
        core, xp, yp = dev(z, y, 1 - c, f), dev(z, y, c, 1 - f), dev(z, 1 - y, c, f)
        mine, home = self.mine(i), self.at(i, z, y, c, f)

        def same(slot, ref, device):
            return self.hop(i, slot, ref, ref, device)

        zs = [dev(lax.rem(z + k, nz), y, c, f) for k in range(1, nz)]
        line = self.at(i, every, y, c, f)
        other = self.at(i, every, 1 - y, c, f)
        zero = {
            0: [self.hop(i, k, mine, home, zs[k]) for k in range(nz - 1)],
            1: [same(3, line, yp), same(4, line, xp), same(8, line, core)],
            2: [same(5, other, xp), same(9, other, core)],
            3: [same(10, self.at(i, every, every, c, 1 - f), core)],
        }
        rows = self.at(i, z, y, c)
        plane = self.at(i, every, y, c)
        one = {
            0: [self.hop(i, 3, mine, home, xp)],
            1: [same(k, rows, zs[k]) for k in range(nz - 1)],
            2: [same(4, plane, yp), same(8, plane, core)],
            3: [same(9, self.at(i, every, 1 - y, c), core)],
        }
        return zero, one

    def arrivals(self, i):
        z, y, c, f = self.place
        nz = self.nz
        every = slice(None)
        zk = [lax.rem(z + nz - k, nz) for k in range(1, nz)]
        core = dev(z, y, 1 - c, f)

        def here(slot, *where):
            ref = self.at(i, *where)
            return self.hop(i, slot, ref, ref, core)

        zero = {
            1: [here(k, zk[k], y, c, f) for k in range(nz - 1)],
            2: [here(3, every, 1 - y, c, f)],
            3: [here(4, every, y, c, 1 - f), here(5, every, 1 - y, c, 1 - f)],
            4: [here(8, every, y, 1 - c), here(9, every, 1 - y, 1 - c)],
        }
        one = {
            1: [here(3, z, y, c, 1 - f)],
            2: [here(k, zk[k], y, c) for k in range(nz - 1)],
            3: [here(4, every, 1 - y, c)],
            4: [here(8, every, y, 1 - c, f), here(9, every, 1 - y, 1 - c, f), here(10, every, every, 1 - c, 1 - f)],
        }
        return zero, one

    def local(self, i):
        z, y, c, f = self.place
        return pltpu.make_async_copy(self.mine(i), self.at(i, z, y, c, f), self.own.at[i])

    def stage(self, i, s):
        if s == 1:
            self.local(i).wait()
        for core in range(2):

            @pl.when(self.place[2] == core)
            def _():
                if s:
                    for copy in self.arrivals(i)[core][s]:
                        copy.wait_recv()
                if s < 4:
                    for copy in self.copies(i)[core][s]:
                        copy.start()

    def tick(self, t):
        for s in range(4):
            if 0 <= t - s < len(self.chunks):
                self.stage(t - s, s)

    def finish(self, i):
        for core in range(2):

            @pl.when(self.place[2] == core)
            def _():
                for copies in self.copies(i)[core].values():
                    for copy in copies:
                        copy.wait_send()


RING = 6
BLOCK = 32
WIDE = 1024


def tiles(count, size, body, hooks=None):
    @pl.loop(0, count)
    def _(j):
        body(j, pl.ds(pl.multiple_of(j * size, size), size))
        run_hooks(j, hooks)


def run_hooks(j, hooks):
    for at, hook in (hooks or {}).items():

        @pl.when(j == at)
        def _():
            hook()


def flat(ref, cols):
    v = ref[:, :, :, :, cols]
    return v.reshape(math.prod(v.shape[:-1]), v.shape[-1])


def add_blocks(dst, parts, out=None):
    lead, n = dst.shape[:-2], dst.shape[-1]
    size = min(n, 256)

    @pl.loop(0, math.prod(lead) * (n // size))
    def _(j):
        cols = pl.ds(pl.multiple_of(lax.rem(j, n // size) * size, size), size)
        at, rest = [], lax.div(j, n // size)
        for count in reversed(lead):
            at.insert(0, lax.rem(rest, count))
            rest = lax.div(rest, count)
        at = tuple(at) + (slice(None), cols)
        total = dst[at].astype(F32)
        for p in parts:
            total = total + p[at].astype(F32)
        if out is None:
            dst[at] = total.astype(dst.dtype)
        else:
            out[at] = total


class Scatter:
    def __init__(self, nz, place, sums, second, third, outs, sems):
        self.nz, self.place, self.sums, self.second, self.third = nz, place, sums, second, third
        self.outs, self.done = outs, set()
        self.send, self.recv, self.free = sems

    @staticmethod
    def sem_shapes(n):
        return [DMA((n, 5)), DMA((n, 5)), pltpu.SemaphoreType.REGULAR((RING,))]

    def peers(self):
        z, y, c, f = self.place
        zs = [dev(lax.rem(z + k, self.nz), y, c, f) for k in range(1, self.nz)]
        return zs, dev(z, 1 - y, c, f), dev(z, y, c, 1 - f)

    def hop(self, i, slot, src, dst, device):
        return remote(src, dst, self.send.at[i, slot], self.recv.at[i, slot], device)

    def copies(self, i):
        z, y, c, f = self.place
        s, b2, b3, nz = self.sums[i], self.second[i], self.third[i], self.nz
        zs, yp, xp = self.peers()
        zt = [lax.rem(z + k, nz) for k in range(1, nz)]
        zero = {
            0: [self.hop(i, 0, s.at[:, :, 1 - f], b2, xp)],
            1: [self.hop(i, 1, s.at[:, 1 - y, f], b3.at[pl.ds(0, nz)], yp)],
            2: [self.hop(i, 2 + k, s.at[zt[k], y, f], b3.at[nz + k], zs[k]) for k in range(nz - 1)],
        }
        one = {
            0: [self.hop(i, 0, s.at[:, 1 - y], b2, yp)],
            1: [self.hop(i, 1 + k, s.at[zt[k], y], b3.at[pl.ds(2 * k, 2)], zs[k]) for k in range(nz - 1)],
            2: [self.hop(i, nz, s.at[z, y, 1 - f], b3.at[2 * (nz - 1)], xp)],
        }
        return zero, one

    def stage(self, i, st):
        z, y, c, f = self.place
        nz = self.nz
        self.done.add((i, st))
        s, b2, b3 = self.sums[i], self.second[i], self.third[i]
        copies = self.copies(i)
        zs, yp, xp = self.peers()
        ringed = i < len(self.sums) - 1
        if st == 0 and ringed and i >= RING:
            pl.semaphore_wait(self.free.at[i % RING], nz + 1)

        @pl.when(c == 0)
        def _():
            if st:
                for copy in copies[0][st - 1]:
                    copy.wait_recv()
            if st == 0:
                copies[0][0][0].start()
            if st == 1:
                add_blocks(s.at[:, 1 - y, f], [b2.at[:, 1 - y]])
                copies[0][1][0].start()
                add_blocks(s.at[:, y, f], [b2.at[:, y]])
            if st == 2:
                for k in range(nz - 1):
                    zt = lax.rem(z + k + 1, nz)
                    add_blocks(s.at[zt, y, f], [b3.at[zt]])
                    copies[0][2][k].start()
                add_blocks(s.at[z, y, f], [b3.at[z]])
            if st == 3:
                add_blocks(s.at[z, y, f], [b3.at[nz + k] for k in range(nz - 1)], self.outs[i])

        @pl.when(c == 1)
        def _():
            if st:
                for copy in copies[1][st - 1]:
                    copy.wait_recv()
            if st == 0:
                copies[1][0][0].start()
            if st == 1:
                for k in range(nz - 1):
                    zt = lax.rem(z + k + 1, nz)
                    add_blocks(s.at[zt, y], [b2.at[zt]])
                    copies[1][1][k].start()
                add_blocks(s.at[z, y], [b2.at[z]])
            if st == 2:
                add_blocks(s.at[z, y, 1 - f], [b3.at[2 * k + 1 - f] for k in range(nz - 1)])
                copies[1][2][0].start()
                add_blocks(s.at[z, y, f], [b3.at[2 * k + f] for k in range(nz - 1)])
            if st == 3:
                add_blocks(s.at[z, y, f], [b3.at[2 * (nz - 1)]], self.outs[i])

        if st == 3 and ringed and i + RING < len(self.sums) - 1:
            for peer in zs + [yp, xp]:
                pl.semaphore_signal(self.free.at[i % RING], inc=1, device_id=peer, device_id_type=MESH)

    def tick(self, t):
        for st in range(1, 4):
            i = t - st
            if (i, st - 1) in self.done and (i, st) not in self.done:
                self.stage(i, st)

    def finish(self, i):
        for core in range(2):

            @pl.when(self.place[2] == core)
            def _():
                for copies in self.copies(i)[core].values():
                    for copy in copies:
                        copy.wait_send()


class Producer:
    def __init__(self, place, buf, land, sems):
        self.place, self.buf, self.land = place, buf, land
        self.send, self.recv, self.credit = sems
        z, y, c, f = place
        self.core = dev(z, y, 1 - c, f)
        self.made, self.pending = 0, None

    def copy(self, slot):
        theirs = self.buf.at[slot, :, 1 - self.place[2]]
        return remote(theirs, self.land.at[slot], self.send.at[slot], self.recv.at[slot], self.core)

    def before(self, slot):
        self.copy(slot).wait_send()
        pl.semaphore_wait(self.credit.at[slot], 1)

    def absorb(self, j, target):
        c = self.place[2]
        slot = lax.rem(j, 2)
        self.copy(slot).wait_recv()
        for i in range(4):
            ref = target(j, i)
            for k in range(2):
                ref[k] = (self.buf[slot, i, c, k].astype(F32) + self.land[slot, i, k].astype(F32)).astype(BF)
        pl.semaphore_signal(self.credit.at[slot], inc=1, device_id=self.core, device_id_type=MESH)

    def flush(self):
        if self.pending is not None:
            self.absorb(*self.pending)
            self.pending = None

    def run(self, count, product, where, target, hooks=None):
        fresh, pending = self.made == 0, self.pending

        @pl.loop(0, count)
        def _(j):
            slot = lax.rem(j, 2)
            if not fresh:
                self.before(slot)
            elif count > 2:

                @pl.when(j >= 2)
                def _():
                    self.before(slot)

            v = product(j)
            for i in range(4):
                for k in range(2):
                    for core in range(2):
                        at = where(i, core, k)
                        self.buf[slot, i, core, k] = v[at : at + BLOCK].astype(BF)
            self.copy(slot).start()
            if pending is not None:

                @pl.when(j == 0)
                def _():
                    self.absorb(*pending)

            @pl.when(j >= 1)
            def _():
                self.absorb(j - 1, target)

            run_hooks(j, hooks)

        self.made += count
        self.pending = (count - 1, target)

    def finish(self):
        for slot in range(2):
            self.before(slot)


def row_blocks(i, core, k):
    return BLOCK * (4 * i + 2 * core + k)


def deep_blocks(i, core, k):
    return BLOCK * (8 * core + 4 * k + i)


def attend_forward(c, qkv, cross, bias, att, lse, hooks):
    rows, d = att.shape
    half = lane_half()
    lane = lax.broadcasted_iota(jnp.int32, (1, PAIR), 1)
    rt = rows // 2

    def one(q, blocks):
        scores = []
        for keys, _, extra in blocks:
            s = dot_nt(q, keys) * SCALE2
            scores.append(s if extra is None else s + extra)
        peak = functools.reduce(jnp.maximum, [jnp.max(s, -1, keepdims=True) for s in scores])
        total = None
        for s, (_, values, _) in zip(scores, blocks):
            part = dot_nn(jnp.exp2(s - peak).astype(BF), values)
            total = part if total is None else total + part
        return total, peak

    def pair(p, second):
        cols = pl.ds(pl.multiple_of(p * PAIR, PAIR), PAIR)
        kcols = pl.ds(pl.multiple_of(d + p * PAIR, PAIR), PAIR)
        vcols = pl.ds(pl.multiple_of(2 * d + p * PAIR, PAIR), PAIR)
        def half_rows(r, part):
            results = []
            for h in range(2):
                mine = half == h
                q = jnp.where(mine, qkv[part, cols], 0.0).astype(BF)

                def val(v):
                    return jnp.where(mine, v, 1.0).astype(BF)

                if second:
                    blocks = [(cross[:, cols], val(cross[:, kcols]), None)]
                    if r > 0:
                        blocks.append((qkv[pl.ds(0, rt), kcols], val(qkv[pl.ds(0, rt), vcols]), None))
                    blocks.append((qkv[part, kcols], val(qkv[part, vcols]), bias[part, pl.ds(r * rt, rt)]))
                else:
                    blocks = [(qkv[:, kcols], val(qkv[:, vcols]), bias[part, :])]
                total, peak = one(q, blocks)
                sums = pltpu.roll(total, HD, axis=1)
                results.append(total / sums)
                both = jnp.where(mine, sums, total)
                lse[part, :] = jnp.where(lane == 2 * p + h, peak + jnp.log2(both), lse[part, :])
            att[part, cols] = jnp.where(half == 0, results[0], results[1]).astype(BF)

        if second:
            for r in range(2):
                half_rows(r, pl.ds(r * rt, rt))
        else:
            tiles(2, rt, half_rows)

    @pl.loop(0, d // PAIR)
    def _(p):
        for second in range(2):

            @pl.when(c == second)
            def _():
                pair(p, second == 1)

        run_hooks(p, hooks)


SHARED = 5


def attend_backward(c, qkv, cross, biast, lset, deltat, far_lse, far_delta, go, gq, gq2, more, hooks):
    rows, d = go.shape
    half = lane_half()
    rt = rows // 2
    pairs = d // PAIR

    def term(p, keys, values, krows, qrows, queries, grads, lse, delta, masked, total):
        gk = gv = None
        for h in range(2):
            mine = half == h
            q = jnp.where(mine, queries, 0.0).astype(BF)
            g = jnp.where(mine, grads, 0.0).astype(BF)
            km = jnp.where(mine, keys, 0.0).astype(BF)
            s = dot_nt(keys, q) * SCALE2
            if masked:
                s = s + biast[krows, qrows]
            pr = jnp.exp2(s - lse[pl.ds(2 * p + h, 1), qrows])
            gs = (pr * (dot_nt(values, g) - delta[pl.ds(2 * p + h, 1), qrows])).astype(BF)
            k1, v1 = dot_nn(gs, q), dot_nn(pr.astype(BF), g)
            gk, gv = (k1, v1) if gk is None else (gk + k1, gv + v1)
            total[qrows, :] = total[qrows, :] + dot_tn(gs, km)
        return gk, gv

    every = pl.ds(0, rows)
    first, last = pl.ds(0, PAIR), pl.ds(PAIR, PAIR)

    @pl.loop(0, pairs)
    def _(i):
        @pl.when(c == 0)
        def _():
            heavy = i < pairs - SHARED
            p = lax.rem(i + SHARED, pairs)
            cols = pl.ds(pl.multiple_of(p * PAIR, PAIR), PAIR)
            kcols = pl.ds(pl.multiple_of(d + p * PAIR, PAIR), PAIR)
            vcols = pl.ds(pl.multiple_of(2 * d + p * PAIR, PAIR), PAIR)
            gq[...] = jnp.zeros_like(gq)

            @pl.when(heavy)
            def _():
                gq2[...] = jnp.zeros_like(gq2)

                def far_part(r, krows):
                    more[krows, first], more[krows, last] = term(
                        p, qkv[krows, kcols], qkv[krows, vcols], krows, every, cross[:, cols], cross[:, kcols], far_lse, far_delta, False, gq2
                    )

                tiles(2, rt, far_part)
                cross[:, cols] = (gq2[...] * 0.125).astype(BF)

            @pl.when(i == pairs - SHARED)
            def _():
                more[:, first] = jnp.zeros_like(gq)
                more[:, last] = jnp.zeros_like(gq)

            def own_part(r, krows):
                gk, gv = term(
                    p, qkv[krows, kcols], qkv[krows, vcols], krows, every, qkv[:, cols], go[:, cols], lset, deltat, True, gq
                )
                qkv[krows, kcols] = ((gk + more[krows, first]) * 0.125).astype(BF)
                qkv[krows, vcols] = (gv + more[krows, last]).astype(BF)

            tiles(2, rt, own_part)
            qkv[:, cols] = (gq[...] * 0.125).astype(BF)

        @pl.when(c == 1)
        def _():
            p = i
            cols = pl.ds(pl.multiple_of(p * PAIR, PAIR), PAIR)
            kcols = pl.ds(pl.multiple_of(d + p * PAIR, PAIR), PAIR)
            vcols = pl.ds(pl.multiple_of(2 * d + p * PAIR, PAIR), PAIR)
            gq[...] = jnp.zeros_like(gq)

            @pl.when(p < SHARED)
            def _():
                def near_part(r, krows):
                    gk, gv = term(
                        p, cross[krows, cols], cross[krows, kcols], krows, every, qkv[:, cols], go[:, cols], lset, deltat, False, gq
                    )
                    cross[krows, cols] = (gk * 0.125).astype(BF)
                    cross[krows, kcols] = gv.astype(BF)

                tiles(2, rt, near_part)

            for r in range(2):
                krows, qrows = pl.ds(r * rt, rt), pl.ds(r * rt, rows - r * rt)
                gk, gv = term(
                    p, qkv[krows, kcols], qkv[krows, vcols], krows, qrows, qkv[qrows, cols], go[qrows, cols], lset, deltat, True, gq
                )
                qkv[krows, kcols] = (gk * 0.125).astype(BF)
                qkv[krows, vcols] = gv.astype(BF)
            qkv[:, cols] = (gq[...] * 0.125).astype(BF)

        run_hooks(i, hooks)


def layer_kernel(nz, *refs):
    (
        frames_in, cot_in, pre_in, s_qkv, s_out, s_up, s_down, s_par,
        fo, gi, gl, f_qkv, f_out, f_up, f_down, f_par, g_qkv, g_out, g_up, g_down, g_par,
        x, cot, pre, h1, qkv, cross, att, x1, h2, a, gp, wa, wb, gh, gz, go, bias, narrow, narrow2, lset, deltat, far_lse, far_delta,
        acc, par, parv, ht, buf, land, sdown, spar, ptheirs, pland, second, third, psecond, pthird,
        ag_send, ag_recv, ag_own, rs_send, rs_recv, rs_free, p_send, p_recv, p_credit,
        load_sem, swap_sem, io_sem, io_recv,
    ) = refs
    place = z, y, c, f = coords()
    rows, d = x.shape
    ff = a.shape[-1]
    core, far = dev(z, y, 1 - c, f), dev(z, y, 1 - c, 1 - f)
    straight = c == f
    nk = d // WIDE

    chunks = [(4, 0, 16, 0, PAIR)]
    chunks += [(0, 0, BLOCK, d + h * TILE, TILE) for h in range(2)] + [(0, 0, BLOCK, b * d, d) for b in (2, 0)]
    chunks += [(1, 0, BLOCK, 0, d)]
    chunks += [(2, 0, BLOCK, k * WIDE, WIDE) for k in range(ff // WIDE)]
    down_rows = [(0, BLOCK), (BLOCK, BLOCK), (2 * BLOCK, BLOCK), (3 * BLOCK, BLOCK // 2), (7 * BLOCK // 2, BLOCK // 2)]
    chunks += [(3, r0, r, 0, d) for r0, r in down_rows]
    ag = Gather(nz, place, (s_qkv, s_out, s_up, s_down, s_par), (f_qkv, f_out, f_up, f_down, f_par), chunks, (ag_send, ag_recv, ag_own))

    ups, downs = ff // WIDE, 4
    sums = [sdown.at[k] for k in range(downs)]
    sums += [a.at[:, :, :, :, pl.ds(k * WIDE, WIDE)] for k in range(ups)]
    tail = [(3 * d, d), (d, d), (2 * d, d), (0, TILE), (TILE, TILE)]
    sums += [gp.at[:, :, :, :, pl.ds(c0, w)] for c0, w in tail]
    goes = [g_down.at[pl.ds(k * BLOCK, BLOCK)] for k in range(downs)]
    goes += [g_up.at[:, pl.ds(k * WIDE, WIDE)] for k in range(ups)]
    goes += [g_out] + [g_qkv.at[:, pl.ds(c0, w)] for c0, w in tail[1:]]
    n = len(sums)
    widths = [WIDE] * (downs + ups) + [w for _, w in tail]
    rs = Scatter(
        nz, place, sums + [spar], [second.at[i % RING, :, :, :, pl.ds(0, widths[i])] for i in range(n)] + [psecond],
        [third.at[i % RING, :, :, pl.ds(0, widths[i])] for i in range(n)] + [pthird], goes + [g_par], (rs_send, rs_recv, rs_free),
    )
    maker = Producer(place, buf, land, (p_send, p_recv, p_credit))

    for i in range(len(chunks)):
        ag.local(i).start()
    greet(all_peers(nz, *place) + [far])

    swaps = []
    quarter = rows // 4
    quarters = [pl.ds(i * quarter, quarter) for i in range(4)]
    moves = [(pre_in, pre)]
    moves += [(cot_in.at[q], cot.at[q]) for q in quarters] + [(frames_in.at[q], x.at[q]) for q in quarters]
    for i, (src, dst) in enumerate(moves):
        swaps.append((pltpu.make_async_copy(src, dst, swap_sem.at[i, 0]), remote(src, dst, swap_sem.at[i, 1], swap_sem.at[i, 2], far)))

    def swap_start(i):
        @pl.when(straight)
        def _():
            swaps[i][0].start()

        @pl.when(jnp.logical_not(straight))
        def _():
            swaps[i][1].start()

    def swap_wait(i):
        @pl.when(straight)
        def _():
            swaps[i][0].wait()

        @pl.when(jnp.logical_not(straight))
        def _():
            swaps[i][1].wait()

    def between(i, src, dst):
        return remote(src, dst, swap_sem.at[i, 1], swap_sem.at[i, 2], core)

    def ag_tick(t):
        return lambda: ag.tick(t)

    def rs_tick(t):
        return lambda: rs.tick(t)

    def rs_begin(i):
        return lambda: rs.stage(i, 0)

    def small(b):
        return pl.ds(b * BLOCK, BLOCK)

    def load(i, src, dst):
        return pltpu.make_async_copy(src, dst, load_sem.at[i])

    def load_block(i, b):
        if b == 3:
            return load(i, f_out, wa.at[:, :, :, :, small(3)])
        return load(i, f_qkv.at[:, :, :, :, :, pl.ds(b * d, d)], wa.at[:, :, :, :, small(b)])

    def block(b, at=slice(None)):
        v = wa[at, :, :, :, small(b)]
        return v.reshape(math.prod(v.shape[:-1]), d)

    ag.stage(0, 0)
    ag.stage(1, 0)
    swap_start(0)
    swap_start(5)
    ag.stage(0, 1)
    ag.tick(2)
    swap_start(6)
    ag.tick(3)
    swap_start(7)
    ag.stage(0, 4)
    get_par = load(0, f_par, parv)
    get_par.start()
    swap_wait(0)
    fill_bias(bias, pre[0:1, 0:1], c, False)
    get_par.wait()
    for t in range(d // PAIR):
        total = None
        for k in range(4):
            piece = parv[t // 2, t % 2, k // 2, k % 2].astype(F32)
            total = piece if total is None else total + piece
        par[:, pl.ds(t * PAIR, PAIR)] = total
    step = 64

    def norm_one(j, part):
        nrm, _ = normalise(x[part, :].astype(F32))
        h1[part, :] = (nrm * par[0:1, :] + par[2:3, :]).astype(BF)

    ag.tick(4)
    swap_start(8)
    for i in range(4):
        swap_wait(5 + i)
    tiles(rows // step, step, norm_one)
    keyvals = between(14, qkv.at[:, pl.ds(d, 2 * d)], cross)
    ag.stage(1, 4)
    for i, b in enumerate((1, 2, 0)):
        ag.tick(5 + i)
        ag.stage(2 + i, 4)
        get = load_block(1 + i, b)
        get.start()
        get.wait()
        for t in range(d // TILE):
            cols = pl.ds(t * TILE, TILE)
            w = wa[:, :, :, :, small(b), cols].reshape(d, TILE)
            qkv[:, pl.ds(b * d + t * TILE, TILE)] = dot_nn(h1[...], w).astype(BF)
        swap_start(1 + i)
        if b == 2:

            @pl.when(c == 0)
            def _():
                keyvals.start()

    @pl.when(c == 1)
    def _():
        keyvals.wait_recv()

    swap_start(4)
    narrow[...] = jnp.zeros_like(narrow)
    attend_forward(c, qkv, cross, bias, att, narrow, {1: ag_tick(8), 6: ag_tick(9)})
    ag.stage(5, 4)
    get_out = load_block(4, 3)
    get_out.start()

    @pl.when(c == 0)
    def _():
        keyvals.wait_send()

    lset[...] = narrow[...].T[:H, :]

    def get_up(k):
        return load(5 + k, f_up.at[:, :, :, :, :, pl.ds(k * WIDE, WIDE)], wb.at[:, :, :, :, :, pl.ds(k * WIDE, WIDE)])

    ag.stage(6, 4)
    get_up(0).start()
    get_out.wait()
    for t in range(d // TILE):
        cols = pl.ds(t * TILE, TILE)
        w = wa[:, :, :, :, small(3), cols].reshape(d, TILE)
        x1[:, cols] = x[:, cols].astype(F32) + dot_nn(att[...], w)
    ag.tick(10)

    def norm_two(j, part):
        nrm, _ = normalise(x1[part, :])
        h2[part, :] = (nrm * par[1:2, :] + par[3:4, :]).astype(BF)

    tiles(rows // step, step, norm_two)
    u = gh.at[:, pl.ds(0, TILE)]

    def up(cols):
        gh[:, pl.ds(0, TILE)] = dot_nn(h2[...], wb[:, :, :, :, :, cols].reshape(d, TILE))

        @pl.loop(0, rows // BLOCK)
        def _(j):
            at = (lax.div(j, 4), lax.rem(lax.div(j, 2), 2), lax.rem(j, 2), slice(None), cols)
            v = gh[pl.ds(pl.multiple_of(j * BLOCK, BLOCK), BLOCK), pl.ds(0, TILE)]
            phi = 0.5 * (1.0 + lax.erf(v * math.sqrt(0.5)))
            dens = jnp.exp2(v * v * (-0.5 * LOG2E)) * (1.0 / math.sqrt(2.0 * math.pi))
            a[at] = (v * phi).astype(BF)
            gp[at] = (phi + v * dens).astype(BF)

    for i in range(4):
        swap_wait(1 + i)

    def down_product(j):
        for k in range(ups):

            @pl.when(j == 2 * k)
            def _():
                if k:
                    ag.stage(6 + k, 4)
                    get_up(k).start()
                get_up(k).wait()

        cols = pl.ds(pl.multiple_of(j * TILE, TILE), TILE)
        up(cols)
        for k in range(ups):

            @pl.when(j == 2 * k + 1)
            def _():
                ag.tick(11 + k)

        return dot_tn(flat(a, cols), cot[...])

    maker.run(2 * ups, down_product, deep_blocks, lambda j, i: sdown.at[i, lax.div(j, 2), lax.rem(j, 2)])

    def get_down(k):
        part = pl.ds(*down_rows[k])
        return load(9 + k, f_down.at[:, :, :, :, part], wa.at[:, :, :, :, part])

    ag.tick(15)
    maker.flush()
    rs.stage(0, 0)
    ag.tick(16)
    ag.tick(17)
    rs.stage(1, 0)
    for k in range(len(down_rows)):
        ag.stage(10 + k, 4)
        get_down(k).start()
    for k in range(len(down_rows)):
        get_down(k).wait()
    rs.stage(2, 0)
    for k in range(2):
        cols = pl.ds(k * TILE, TILE)
        w = wa[:, :, :, :, :, cols].reshape(ff, TILE)
        go[:, cols] = (x1[:, cols] + dot_nn(flat(a, slice(None)), w)).astype(BF)

    outs = []
    for q in quarters:
        outs.append(
            (
                pltpu.make_async_copy(go.at[q], fo.at[q], io_sem.at[len(outs)]),
                remote(go.at[q], fo.at[q], io_sem.at[len(outs)], io_recv.at[len(outs)], far),
            )
        )

    def either(pair, act_on):
        @pl.when(straight)
        def _():
            act_on(pair[0])

        @pl.when(jnp.logical_not(straight))
        def _():
            act_on(pair[1])

    def begin(pair):
        either(pair, lambda copy: copy.start())

    def end(pair):
        either(pair, lambda copy: copy.wait())

    begin(outs[0])
    def act(j, cols):
        w = wa[lax.div(j, 2), lax.rem(j, 2)].reshape(TILE, d)
        v = dot_nt(cot[...], w) * flat(gp, cols).astype(F32)
        gp[:, :, :, :, cols] = v.astype(BF).reshape(a.shape[:-1] + (TILE,))

    rs.tick(1)
    rs.stage(3, 0)
    tiles(8, TILE, act)
    begin(outs[1])
    for i, b in enumerate((3, 0, 1, 2)):
        load_block(14 + i, b).start()
    ht[...] = h2[...].T
    for i in range(2):
        gh[:, pl.ds(i * TILE, TILE)] = dot_nt(flat(gp, slice(None)), wb[2 * i : 2 * i + 2].reshape(TILE, ff))
        if i == 0:
            rs.tick(2)
    begin(outs[2])
    acc[...] = jnp.zeros_like(acc)
    step = 32

    def collect(row, v):
        part = v.reshape(step // 8, 8, d)
        acc[row] = acc[row] + functools.reduce(jnp.add, [part[i] for i in range(step // 8)])

    def back_two(j, part):
        nrm, scale = normalise(x1[part, :])
        g = gh[part, :]
        collect(1, g * nrm)
        collect(3, g)
        total = cot[part, :].astype(F32) + norm_back(g, nrm, scale, par[1:2, :])
        x1[part, :] = total
        gz[part, :] = total.astype(BF)

    tiles(rows // step, step, back_two)

    def row_half(j):
        return ht[pl.ds(pl.multiple_of(lax.rem(j, 2) * TILE, TILE), TILE), :]

    def wide(j):
        return pl.ds(pl.multiple_of(lax.div(j, 2) * WIDE, WIDE), WIDE)

    def up_product(j):
        return dot_nn(row_half(j), flat(gp, wide(j)))

    def target(ref, first):
        def of(j, i):
            cols = pl.ds(pl.multiple_of(first + lax.div(j, 2) * WIDE, WIDE), WIDE)
            return ref.at[2 * lax.rem(j, 2) + i // 2, i % 2, :, :, cols]

        return of

    rs.tick(3)
    begin(outs[3])
    maker.run(
        2 * ups, up_product, row_blocks, target(a, 0), {2: rs_begin(4), 3: rs_tick(4), 4: rs_begin(5), 6: rs_begin(6)}
    )
    maker.flush()
    rs.stage(7, 0)
    for pair in outs:
        end(pair)
    load_block(14, 3).wait()
    for i in range(2):
        go[:, pl.ds(i * TILE, TILE)] = dot_nt(gz[...], block(3, pl.ds(2 * i, 2))).astype(BF)
    pick = (
        lax.broadcasted_iota(jnp.int32, (H, d), 1) // HD == lax.broadcasted_iota(jnp.int32, (H, d), 0)
    ).astype(BF)
    for i in range(4):
        part = pl.ds(i * quarter, quarter)
        prod = go[part, :].astype(F32) * att[part, :].astype(F32)
        high = prod.astype(BF)
        low = (prod - high.astype(F32)).astype(BF)
        deltat[:, part] = dot_nt(pick, high) + dot_nt(pick, low)
    low_cols, high_cols = pl.ds(0, SHARED * PAIR), pl.ds(SHARED * PAIR, d - SHARED * PAIR)
    high_cols2 = pl.ds(d + SHARED * PAIR, d - SHARED * PAIR)
    low_cols2 = pl.ds(d, SHARED * PAIR)

    lends = [
        between(9, qkv.at[:, high_cols], cross.at[:, high_cols]),
        between(15, go.at[:, high_cols], cross.at[:, high_cols2]),
        between(16, lset, far_lse),
        between(10, deltat, far_delta),
    ]
    gives = [
        between(11, cross.at[:, low_cols], cross.at[:, low_cols]),
        between(12, cross.at[:, low_cols2], cross.at[:, low_cols2]),
    ]
    returns = between(13, cross.at[:, high_cols], cross.at[:, high_cols])

    @pl.when(c == 1)
    def _():
        for copy in lends:
            copy.start()

    rs.tick(5)
    ht[...] = att[...].T
    maker.run(2, lambda j: dot_nn(row_half(j), gz[...]), row_blocks, target(gp, 3 * d))
    fill_bias(bias, pre[0:1, 0:1], c, True)

    @pl.when(c == 0)
    def _():
        for copy in lends:
            copy.wait_recv()

    @pl.when(c == 1)
    def _():
        for copy in lends:
            copy.wait_send()

    def give_back():
        @pl.when(c == 1)
        def _():
            for copy in gives:
                copy.start()

    def return_queries():
        @pl.when(c == 0)
        def _():
            returns.start()

    def flush_tick():
        maker.flush()
        rs.stage(8, 0)
        rs.tick(6)

    hooks = {0: flush_tick, 2: return_queries, 3: rs_tick(7), 4: give_back, 5: rs_tick(8), 7: rs_tick(9)}
    attend_backward(c, qkv, cross, bias, lset, deltat, far_lse, far_delta, go, narrow, narrow2, gh, hooks)
    ht[...] = h1[...].T

    @pl.when(c == 1)
    def _():
        for copy in gives:
            copy.wait_send()
        returns.wait_recv()

        def add(j, part):
            qkv[part, high_cols] = (qkv[part, high_cols].astype(F32) + cross[part, high_cols].astype(F32)).astype(BF)

        tiles(rows // step, step, add)

    @pl.when(c == 0)
    def _():
        returns.wait_send()
        for copy in gives:
            copy.wait_recv()

        def add(j, part):
            for base in (0, d):
                to, src = pl.ds(d + base, SHARED * PAIR), pl.ds(base, SHARED * PAIR)
                qkv[part, to] = (qkv[part, to].astype(F32) + cross[part, src].astype(F32)).astype(BF)

        tiles(rows // step, step, add)

    def mixed_cols(j):
        return pl.ds(pl.multiple_of(lax.rem(lax.div(j, 2) + 1, 3) * d, d), d)

    def mixed_target(j, i):
        return gp.at[2 * lax.rem(j, 2) + i // 2, i % 2, :, :, mixed_cols(j)]

    maker.run(
        6, lambda j: dot_nn(row_half(j), qkv[:, mixed_cols(j)]), row_blocks, mixed_target, {2: rs_begin(9), 4: rs_begin(10)}
    )
    maker.flush()
    rs.stage(11, 0)
    rs.stage(12, 0)
    for i, b in enumerate((0, 1, 2)):
        load_block(15 + i, b).wait()
    for i in range(2):
        total = None
        for b in range(3):
            part = dot_nt(qkv[:, pl.ds(b * d, d)], block(b, pl.ds(2 * i, 2)))
            total = part if total is None else total + part
        gh[:, pl.ds(i * TILE, TILE)] = total
        if i == 0:
            rs.tick(10)

    def back_one(j, part):
        nrm, scale = normalise(x[part, :].astype(F32))
        g = gh[part, :]
        collect(0, g * nrm)
        collect(2, g)
        total = x1[part, :] + norm_back(g, nrm, scale, par[0:1, :])
        gh[part, :] = total
        gz[part, :] = total.astype(BF)

    tiles(rows // step, step, back_one)
    backs = []
    for i, q in enumerate(quarters):
        backs.append(
            (
                pltpu.make_async_copy(gh.at[q], gi.at[q], io_sem.at[4 + i]),
                remote(gz.at[q], gl.at[q], io_sem.at[4 + i], io_recv.at[4 + i], far),
            )
        )
    begin(backs[0])
    for i in range(4):
        par[i : i + 1, :] = jnp.sum(acc[i], 0, keepdims=True)
    for t in range(d // PAIR):
        row = par[:, pl.ds(t * PAIR, PAIR)].astype(BF)
        for k in range(2):
            spar[t // 2, t % 2, k] = row
            ptheirs[t // 2, t % 2, k] = row
    pars = remote(ptheirs, pland, io_sem.at[8], io_recv.at[8], core)
    pars.start()
    rs.tick(11)
    begin(backs[1])
    rs.tick(12)
    pars.wait_recv()
    add_blocks(spar, [pland])
    rs.stage(n, 0)
    rs.tick(13)
    begin(backs[2])
    rs.tick(14)
    begin(backs[3])
    rs.tick(15)
    rs.tick(16)
    for pair in backs:
        end(pair)
    pars.wait_send()
    for i in range(len(chunks)):
        ag.finish(i)
    for i in range(n + 1):
        rs.finish(i)
    maker.finish()


def layer(nz, frames_in, cot, pre, w_qkv, w_out, w_up, w_down, tile):
    rows, d = frames_in.shape
    ff = w_up.shape[1]
    S = jax.ShapeDtypeStruct
    V = pltpu.VMEM
    REG = pltpu.SemaphoreType.REGULAR
    hbm, vm = pl.BlockSpec(memory_space=pl.ANY), pl.BlockSpec(memory_space=V)
    shards = (w_qkv, w_out, w_up, w_down, tile)
    parts = (nz, 2, 2, BLOCK)
    full = (nz, 2, 2, 2)
    return pl.pallas_call(
        functools.partial(layer_kernel, nz),
        out_shape=[S((rows, d), BF), S((rows, d), F32), S((rows, d), BF)]
        + [S(full + w.shape, BF) for w in shards]
        + [S(w.shape, F32) for w in shards],
        in_specs=[hbm] * 8,
        out_specs=[hbm] * 8 + [vm] * 5,
        scratch_shapes=[
            V((rows, d), BF), V((rows, d), BF), V((8, PAIR), jnp.int32), V((rows, d), BF), V((rows, 3 * d), BF),
            V((rows, 2 * d), BF), V((rows, d), BF), V((rows, d), F32), V((rows, d), BF),
            V(parts + (ff,), BF), V(parts + (ff,), BF),
            V(full + w_down.shape, BF), V(full + w_up.shape, BF),
            V((rows, d), F32), V((rows, d), BF), V((rows, d), BF), V((rows, rows), F32), V((rows, PAIR), F32), V((rows, PAIR), F32),
            V((H, rows), F32), V((H, rows), F32), V((H, rows), F32), V((H, rows), F32), V((4, 8, d), F32), V((16, d), F32), V(full + (16, PAIR), BF),
            V((d, rows), BF), V((2, 4, 2, 2, BLOCK, WIDE), BF), V((2, 4, 2, BLOCK, WIDE), BF),
            V((4,) + parts + (d,), BF), V((nz, 2, 2, 16, PAIR), BF), V((nz, 2, 2, 16, PAIR), BF), V((nz, 2, 2, 16, PAIR), BF),
            V((RING, nz, 2, BLOCK, WIDE), BF), V((RING, 7, BLOCK, WIDE), BF), V((nz, 2, 16, PAIR), BF), V((7, 16, PAIR), BF),
        ]
        + Gather.sem_shapes(15)
        + Scatter.sem_shapes(14)
        + [DMA((2,)), DMA((2,)), REG((2,)), DMA((18,)), DMA((17, 3)), DMA((9,)), DMA((9,))],
        compiler_params=pltpu.CompilerParams(collective_id=0, has_side_effects=True, vmem_limit_bytes=63 * 2**20),
    )(frames_in, cot, pre, *shards)


def settle_kernel(fo, gi, gl, g_qkv, g_out, g_up, g_down, g_par, fo_, gi_, qkv_, out_, up_, down_, gains_, shifts_, narrow, wide, *rest):
    straight = lax.rem(lax.axis_index("dp"), 2) == lax.axis_index("fsdp")
    stops, sems = rest[:5], rest[5]
    pairs = ((fo, fo_), (g_qkv, qkv_), (g_out, out_), (g_up, up_), (g_down, down_))
    ins = [pltpu.make_async_copy(src, stop, sems.at[0, i]) for i, ((src, _), stop) in enumerate(zip(pairs, stops))]
    outs = [pltpu.make_async_copy(stop, dst, sems.at[1, i]) for i, ((_, dst), stop) in enumerate(zip(pairs, stops))]
    rows = gi.shape[0] // 4
    parts = [pl.ds(i * rows, rows) for i in range(4)]
    own = [pltpu.make_async_copy(gi.at[p], wide.at[p], sems.at[2, i]) for i, p in enumerate(parts)]
    came = [pltpu.make_async_copy(gl.at[p], narrow.at[p], sems.at[2, i]) for i, p in enumerate(parts)]
    puts = [pltpu.make_async_copy(wide.at[p], gi_.at[p], sems.at[3, i]) for i, p in enumerate(parts)]

    @pl.when(straight)
    def _():
        for get in own:
            get.start()

    @pl.when(jnp.logical_not(straight))
    def _():
        for get in came:
            get.start()

    for copy in ins:
        copy.start()
    width = gains_.shape[1]
    mine = lax.rem(lax.axis_index("dp") * 2 + lax.axis_index("fsdp"), PAIR // width)
    small = g_par[:, pl.ds(0, width)]
    for i in range(1, PAIR // width):
        small = jnp.where(mine == i, g_par[:, pl.ds(i * width, width)], small)
    gains_[...] = small[0:2]
    shifts_[...] = small[2:4]

    @pl.when(straight)
    def _():
        for get, put in zip(own, puts):
            get.wait()
            put.start()

    @pl.when(jnp.logical_not(straight))
    def _():
        for get, put, p in zip(came, puts, parts):
            get.wait()
            wide[p, :] = narrow[p, :].astype(F32)
            put.start()

    for get, put in zip(ins, outs):
        get.wait()
        put.start()
    for put in puts + outs:
        put.wait()


def settle(width, fo, gi, gl, *grads):
    S = jax.ShapeDtypeStruct
    V = pltpu.VMEM
    hbm, vm = pl.BlockSpec(memory_space=pl.ANY), pl.BlockSpec(memory_space=V)
    kept = (fo, gi) + grads[:4]
    return pl.pallas_call(
        settle_kernel,
        out_shape=[S(v.shape, v.dtype) for v in kept] + [S((2, width), F32)] * 2,
        in_specs=[hbm] * 7 + [vm],
        out_specs=[hbm] * 6 + [vm] * 2,
        scratch_shapes=[V(gl.shape, BF), V(gi.shape, F32)] + [V(v.shape, v.dtype) for v in (fo,) + grads[:4]] + [DMA((4, 5))],
        compiler_params=pltpu.CompilerParams(vmem_limit_bytes=VMEM_LIMIT),
    )(fo, gi, gl, *grads)


def norm_rows(values, gain, shift):
    center = values - jnp.mean(values, -1, keepdims=True)
    spread = jnp.mean(center * center, -1, keepdims=True)
    return center * lax.rsqrt(spread + EPS) * gain + shift


def collect(w_qkv, w_out, w_up, w_down, gains, shifts):
    return (
        lax.all_gather(w_qkv, ("dp", "fsdp"), axis=0, tiled=True),
        lax.all_gather(w_out, ("dp", "fsdp"), axis=0, tiled=True),
        lax.all_gather(w_up, ("dp", "fsdp"), axis=0, tiled=True),
        lax.all_gather(w_down, ("dp", "fsdp"), axis=0, tiled=True),
        lax.all_gather(gains, ("dp", "fsdp"), axis=1, tiled=True),
        lax.all_gather(shifts, ("dp", "fsdp"), axis=1, tiled=True),
    )


def split_heads(matrix):
    return matrix.reshape(matrix.shape[0], H, HD).transpose(1, 0, 2)


def join_heads(stacked):
    return stacked.transpose(1, 0, 2).reshape(stacked.shape[1], H * HD)


def masked_scores(query_one, key_one, allowed):
    scores = jnp.dot(query_one, key_one.T, preferred_element_type=jnp.float32) * 0.125
    return jnp.where(allowed, scores, -1e30)


def forward(inputs, weights, allowed):
    w_qkv, w_out, w_up, w_down, gains, shifts = weights
    width = inputs.shape[1]
    gain_rows = gains.astype(jnp.float32)
    shift_rows = shifts.astype(jnp.float32)
    normed = norm_rows(inputs, gain_rows[0], shift_rows[0]).astype(jnp.bfloat16)
    mixed = jnp.dot(normed, w_qkv, preferred_element_type=jnp.float32).astype(jnp.bfloat16)
    queries = mixed[:, :width]
    keys_all, values_all = (
        lax.all_gather(mixed[:, width : 2 * width], "fsdp", axis=0, tiled=True),
        lax.all_gather(mixed[:, 2 * width :], "fsdp", axis=0, tiled=True),
    )
    query_heads = split_heads(queries)
    key_heads = split_heads(keys_all)
    value_heads = split_heads(values_all)

    def single(pieces):
        scores = masked_scores(pieces[0], pieces[1], allowed)
        peak_row = jnp.max(scores, -1, keepdims=True)
        log_total = peak_row + jnp.log(jnp.sum(jnp.exp(scores - peak_row), -1, keepdims=True))
        chance = jnp.exp(scores - log_total).astype(jnp.bfloat16)
        return (jnp.dot(chance, pieces[2], preferred_element_type=jnp.float32), log_total[:, 0])

    outputs, totals = lax.map(single, (query_heads, key_heads, value_heads))
    attended = join_heads(outputs).astype(jnp.bfloat16)
    middle = inputs + jnp.dot(attended, w_out, preferred_element_type=jnp.float32)
    normed_two = norm_rows(middle, gain_rows[1], shift_rows[1]).astype(jnp.bfloat16)
    hidden = jnp.dot(normed_two, w_up, preferred_element_type=jnp.float32)
    active = jax.nn.gelu(hidden, approximate=False).astype(jnp.bfloat16)
    result = middle + jnp.dot(active, w_down, preferred_element_type=jnp.float32)
    saved = (
        normed,
        query_heads,
        key_heads,
        value_heads,
        totals,
        attended,
        middle,
        normed_two,
        hidden,
        active,
    )
    return (result, saved)


def on_device(frames_in, prefix_len, w_qkv, w_out, w_up, w_down, gains, shifts, cotangent):
    inputs = frames_in[0].astype(jnp.float32)
    rows_here = inputs.shape[0]
    frames_all = rows_here * lax.axis_size("fsdp")
    first_row = lax.axis_index("fsdp") * rows_here
    places = first_row + jnp.arange(rows_here, dtype=jnp.int32)
    columns = jnp.arange(frames_all, dtype=jnp.int32)
    allowed = (columns[None, :] <= places[:, None]) | (columns[None, :] < prefix_len[0])
    weights = collect(w_qkv, w_out, w_up, w_down, gains, shifts)
    result, saved = forward(inputs, weights, allowed)
    weights = collect(w_qkv, w_out, w_up, w_down, gains, shifts)
    saved = forward(inputs, weights, allowed)[1]
    full_qkv, full_out, full_up, full_down, full_gains, full_shifts = weights
    (
        normed,
        query_heads,
        key_heads,
        value_heads,
        totals,
        attended,
        middle,
        normed_two,
        hidden,
        active,
    ) = saved
    gain_rows = full_gains.astype(jnp.float32)
    shift_rows = full_shifts.astype(jnp.float32)
    grad_top = cotangent[0].astype(jnp.float32)
    grad_branch = grad_top.astype(jnp.bfloat16)
    part_down = jnp.dot(active.T, grad_branch, preferred_element_type=jnp.float32)
    grad_active = jnp.dot(grad_branch, full_down.T, preferred_element_type=jnp.float32)
    gelu_pull = jax.vjp(functools.partial(jax.nn.gelu, approximate=False), hidden)[1]
    grad_hidden = gelu_pull(grad_active)[0].astype(jnp.bfloat16)
    part_up = jnp.dot(normed_two.T, grad_hidden, preferred_element_type=jnp.float32)
    grad_normed_two = jnp.dot(grad_hidden, full_up.T, preferred_element_type=jnp.float32)
    norm_pull_two = jax.vjp(norm_rows, middle, gain_rows[1], shift_rows[1])[1]
    back_middle, grad_gain_two, grad_shift_two = norm_pull_two(grad_normed_two)
    grad_middle = grad_top + back_middle
    grad_attn_out = grad_middle.astype(jnp.bfloat16)
    part_out = jnp.dot(attended.T, grad_attn_out, preferred_element_type=jnp.float32)
    grad_attended = jnp.dot(grad_attn_out, full_out.T, preferred_element_type=jnp.float32).astype(
        jnp.bfloat16
    )
    grad_att_heads = split_heads(grad_attended)

    def single_back(pieces):
        query_one, key_one, value_one, grad_one, log_total = pieces
        scores = masked_scores(query_one, key_one, allowed)
        chance = jnp.exp(scores - log_total[:, None])
        grad_chance = jnp.dot(grad_one, value_one.T, preferred_element_type=jnp.float32)
        inner = jnp.sum(chance * grad_chance, -1, keepdims=True)
        grad_scores = (chance * (grad_chance - inner)).astype(jnp.bfloat16)
        grad_query = jnp.dot(grad_scores, key_one, preferred_element_type=jnp.float32) * 0.125
        grad_key = (
            jnp.einsum("qk,qd->kd", grad_scores, query_one, preferred_element_type=jnp.float32)
            * 0.125
        )
        grad_value = jnp.einsum(
            "qk,qd->kd", chance.astype(jnp.bfloat16), grad_one, preferred_element_type=jnp.float32
        )
        return (grad_query, grad_key, grad_value)

    grad_q_heads, grad_k_heads, grad_v_heads = lax.map(
        single_back, (query_heads, key_heads, value_heads, grad_att_heads, totals)
    )
    grad_keys, grad_values = (
        lax.psum_scatter(
            join_heads(grad_k_heads).astype(jnp.bfloat16), "fsdp", scatter_dimension=0, tiled=True
        ).astype(jnp.float32),
        lax.psum_scatter(
            join_heads(grad_v_heads).astype(jnp.bfloat16), "fsdp", scatter_dimension=0, tiled=True
        ).astype(jnp.float32),
    )
    grad_mixed = jnp.concatenate([join_heads(grad_q_heads), grad_keys, grad_values], 1).astype(
        jnp.bfloat16
    )
    part_qkv = jnp.dot(normed.T, grad_mixed, preferred_element_type=jnp.float32)
    grad_normed = jnp.dot(grad_mixed, full_qkv.T, preferred_element_type=jnp.float32)
    norm_pull_one = jax.vjp(norm_rows, inputs, gain_rows[0], shift_rows[0])[1]
    back_inputs, grad_gain_one, grad_shift_one = norm_pull_one(grad_normed)
    grad_inputs = grad_middle + back_inputs
    part_gains = jnp.stack([grad_gain_one, grad_gain_two])
    part_shifts = jnp.stack([grad_shift_one, grad_shift_two])
    owned = (
        lax.psum_scatter(part_qkv, ("dp", "fsdp"), scatter_dimension=0, tiled=True),
        lax.psum_scatter(part_out, ("dp", "fsdp"), scatter_dimension=0, tiled=True),
        lax.psum_scatter(part_up, ("dp", "fsdp"), scatter_dimension=0, tiled=True),
        lax.psum_scatter(part_down, ("dp", "fsdp"), scatter_dimension=0, tiled=True),
        lax.psum_scatter(part_gains, ("dp", "fsdp"), scatter_dimension=1, tiled=True),
        lax.psum_scatter(part_shifts, ("dp", "fsdp"), scatter_dimension=1, tiled=True),
    )
    return (
        result.astype(jnp.bfloat16)[None],
        grad_inputs[None],
        owned[0],
        owned[1],
        owned[2],
        owned[3],
        owned[4],
        owned[5],
    )


def fast_device(ndp, frames_in, prefix_len, w_qkv, w_out, w_up, w_down, gains, shifts, cotangent):
    here = lax.axis_index("dp") * 2 + lax.axis_index("fsdp")
    width = gains.shape[1]
    per = PAIR // width
    rows = jnp.concatenate([gains, shifts, jnp.zeros((12, width), BF)], 0)
    tile = jnp.where(lax.broadcasted_iota(jnp.int32, (16, per, width), 1) == here % per, rows[:, None], 0.0)
    tile = tile.astype(BF).reshape(16, PAIR)
    pre = jnp.broadcast_to(prefix_len[None], (8, PAIR))
    result = layer(ndp // 4, frames_in[0], cotangent[0], pre, w_qkv, w_out, w_up, w_down, tile)
    frames_out, grad_in, *owned = settle(width, *result[:3], *result[8:])
    return (frames_out[None], grad_in[None]) + tuple(owned)


def solution(mesh):
    ndp, nf = mesh.shape["dp"], mesh.shape["fsdp"]
    both = P(("dp", "fsdp"), None)
    lanes = P(None, ("dp", "fsdp"))
    block = P("dp", "fsdp", None)
    body = functools.partial(fast_device, ndp) if (nf == 2 and ndp == 16) else on_device
    return jax.shard_map(
        body,
        mesh=mesh,
        in_specs=(block, P("dp"), both, both, both, both, lanes, lanes, block),
        out_specs=(block, block, both, both, both, both, lanes, lanes),
        check_vma=False,
    )
```

```python
import functools
import math

import jax
import jax.numpy as jnp
from jax import lax
from jax.experimental import pallas as pl
from jax.experimental.pallas import tpu as pltpu
from jax.sharding import PartitionSpec as P

H = 16
HD = 64
EPS = 1e-05
BF = jnp.bfloat16
F32 = jnp.float32
LOG2E = math.log2(math.e)
SCALE2 = 0.125 * LOG2E
PAIR = 2 * HD
TILE = 512
MESH = pl.DeviceIdType.MESH
DMA = pltpu.SemaphoreType.DMA
VMEM_LIMIT = 60 * 2**20


def coords():
    dp, f = lax.axis_index("dp"), lax.axis_index("fsdp")
    q = lax.div(dp, 2)
    return lax.div(q, 2), lax.rem(q, 2), lax.rem(dp, 2), f


def dev(z, y, c, f):
    return ((z * 2 + y) * 2 + c, f)


def remote(src, dst, send, recv, device):
    return pltpu.make_async_remote_copy(
        src_ref=src, dst_ref=dst, send_sem=send, recv_sem=recv, device_id=device, device_id_type=MESH
    )


def greet(peers):
    barrier = pltpu.get_barrier_semaphore()
    for peer in peers:
        pl.semaphore_signal(barrier, inc=1, device_id=peer, device_id_type=MESH)
    pl.semaphore_wait(barrier, len(peers))


def all_peers(nz, z, y, c, f):
    peers = [dev(lax.rem(z + k, nz), y, c, f) for k in range(1, nz)]
    return peers + [dev(z, 1 - y, c, f), dev(z, y, c, 1 - f), dev(z, y, 1 - c, f)]


def dot_nn(a, b):
    return lax.dot_general(a, b, (((1,), (0,)), ((), ())), preferred_element_type=F32)


def dot_nt(a, b):
    return lax.dot_general(a, b, (((1,), (1,)), ((), ())), preferred_element_type=F32)


def dot_tn(a, b):
    return lax.dot_general(a, b, (((0,), (0,)), ((), ())), preferred_element_type=F32)


def normalise(v):
    center = v - jnp.mean(v, -1, keepdims=True)
    scale = lax.rsqrt(jnp.mean(center * center, -1, keepdims=True) + EPS)
    return center * scale, scale


def lane_half():
    return lax.broadcasted_iota(jnp.int32, (1, PAIR), 1) // HD


def fill_bias(bias, prefix, c, transposed):
    rows = bias.shape[0]
    step = 64

    def body(j, part):
        a = lax.broadcasted_iota(jnp.int32, (step, rows), 0) + j * step
        b = lax.broadcasted_iota(jnp.int32, (step, rows), 1)
        row, key = (b, a) if transposed else (a, b)
        bias[part, :] = jnp.where((key <= row) | (key + c * rows < prefix), 0.0, -1e30)

    tiles(rows // step, step, body)


def norm_back(gh, n, scale, gain):
    gn = gh * gain
    return scale * (gn - jnp.mean(gn, -1, keepdims=True) - n * jnp.mean(gn * n, -1, keepdims=True))


class Gather:
    def __init__(self, nz, place, shards, outs, chunks, sems):
        self.nz, self.place, self.shards, self.outs, self.chunks = nz, place, shards, outs, chunks
        self.send, self.recv, self.own = sems

    @staticmethod
    def sem_shapes(n):
        return [DMA((n, 12)), DMA((n, 12)), DMA((n,))]

    def mine(self, i):
        w, r0, r, c0, n = self.chunks[i]
        return self.shards[w].at[pl.ds(r0, r), pl.ds(c0, n)]

    def at(self, i, *where):
        w, r0, r, c0, n = self.chunks[i]
        where += (slice(None),) * (4 - len(where))
        return self.outs[w].at[where + (pl.ds(r0, r), pl.ds(c0, n))]

    def hop(self, i, slot, src, dst, device):
        return remote(src, dst, self.send.at[i, slot], self.recv.at[i, slot], device)

    def copies(self, i):
        z, y, c, f = self.place
        nz = self.nz
        every = slice(None)
        core, xp, yp = dev(z, y, 1 - c, f), dev(z, y, c, 1 - f), dev(z, 1 - y, c, f)
        mine, home = self.mine(i), self.at(i, z, y, c, f)

        def same(slot, ref, device):
            return self.hop(i, slot, ref, ref, device)

        zs = [dev(lax.rem(z + k, nz), y, c, f) for k in range(1, nz)]
        line = self.at(i, every, y, c, f)
        other = self.at(i, every, 1 - y, c, f)
        zero = {
            0: [self.hop(i, k, mine, home, zs[k]) for k in range(nz - 1)],
            1: [same(3, line, yp), same(4, line, xp), same(8, line, core)],
            2: [same(5, other, xp), same(9, other, core)],
            3: [same(10, self.at(i, every, every, c, 1 - f), core)],
        }
        rows = self.at(i, z, y, c)
        plane = self.at(i, every, y, c)
        one = {
            0: [self.hop(i, 3, mine, home, xp)],
            1: [same(k, rows, zs[k]) for k in range(nz - 1)],
            2: [same(4, plane, yp), same(8, plane, core)],
            3: [same(9, self.at(i, every, 1 - y, c), core)],
        }
        return zero, one

    def arrivals(self, i):
        z, y, c, f = self.place
        nz = self.nz
        every = slice(None)
        zk = [lax.rem(z + nz - k, nz) for k in range(1, nz)]
        core = dev(z, y, 1 - c, f)

        def here(slot, *where):
            ref = self.at(i, *where)
            return self.hop(i, slot, ref, ref, core)

        zero = {
            1: [here(k, zk[k], y, c, f) for k in range(nz - 1)],
            2: [here(3, every, 1 - y, c, f)],
            3: [here(4, every, y, c, 1 - f), here(5, every, 1 - y, c, 1 - f)],
            4: [here(8, every, y, 1 - c), here(9, every, 1 - y, 1 - c)],
        }
        one = {
            1: [here(3, z, y, c, 1 - f)],
            2: [here(k, zk[k], y, c) for k in range(nz - 1)],
            3: [here(4, every, 1 - y, c)],
            4: [here(8, every, y, 1 - c, f), here(9, every, 1 - y, 1 - c, f), here(10, every, every, 1 - c, 1 - f)],
        }
        return zero, one

    def local(self, i):
        z, y, c, f = self.place
        return pltpu.make_async_copy(self.mine(i), self.at(i, z, y, c, f), self.own.at[i])

    def stage(self, i, s):
        if s == 1:
            self.local(i).wait()
        for core in range(2):

            @pl.when(self.place[2] == core)
            def _():
                if s:
                    for copy in self.arrivals(i)[core][s]:
                        copy.wait_recv()
                if s < 4:
                    for copy in self.copies(i)[core][s]:
                        copy.start()

    def tick(self, t, stages=(0, 1, 2, 3)):
        for s in stages:
            if 0 <= t - s < len(self.chunks):
                self.stage(t - s, s)

    def finish(self, i):
        for core in range(2):

            @pl.when(self.place[2] == core)
            def _():
                for copies in self.copies(i)[core].values():
                    for copy in copies:
                        copy.wait_send()


RING = 6
BLOCK = 32
WIDE = 1024


def tiles(count, size, body, hooks=None):
    @pl.loop(0, count)
    def _(j):
        body(j, pl.ds(pl.multiple_of(j * size, size), size))
        run_hooks(j, hooks)


def run_hooks(j, hooks):
    for at, hook in (hooks or {}).items():

        @pl.when(j == at)
        def _():
            hook()


def flat(ref, cols):
    v = ref[:, :, :, :, cols]
    return v.reshape(math.prod(v.shape[:-1]), v.shape[-1])


def add_blocks(dst, parts, out=None):
    lead, n = dst.shape[:-2], dst.shape[-1]
    size = min(n, 256)

    @pl.loop(0, math.prod(lead) * (n // size))
    def _(j):
        cols = pl.ds(pl.multiple_of(lax.rem(j, n // size) * size, size), size)
        at, rest = [], lax.div(j, n // size)
        for count in reversed(lead):
            at.insert(0, lax.rem(rest, count))
            rest = lax.div(rest, count)
        at = tuple(at) + (slice(None), cols)
        total = dst[at].astype(F32)
        for p in parts:
            total = total + p[at].astype(F32)
        if out is None:
            dst[at] = total.astype(dst.dtype)
        else:
            out[at] = total


class Scatter:
    def __init__(self, nz, place, sums, second, third, outs, sems):
        self.nz, self.place, self.sums, self.second, self.third = nz, place, sums, second, third
        self.outs, self.done = outs, set()
        self.send, self.recv, self.free = sems

    @staticmethod
    def sem_shapes(n):
        return [DMA((n, 5)), DMA((n, 5)), pltpu.SemaphoreType.REGULAR((RING,))]

    def peers(self):
        z, y, c, f = self.place
        zs = [dev(lax.rem(z + k, self.nz), y, c, f) for k in range(1, self.nz)]
        return zs, dev(z, 1 - y, c, f), dev(z, y, c, 1 - f)

    def hop(self, i, slot, src, dst, device):
        return remote(src, dst, self.send.at[i, slot], self.recv.at[i, slot], device)

    def copies(self, i):
        z, y, c, f = self.place
        s, b2, b3, nz = self.sums[i], self.second[i], self.third[i], self.nz
        zs, yp, xp = self.peers()
        zt = [lax.rem(z + k, nz) for k in range(1, nz)]
        zero = {
            0: [self.hop(i, 0, s.at[:, :, 1 - f], b2, xp)],
            1: [self.hop(i, 1, s.at[:, 1 - y, f], b3.at[pl.ds(0, nz)], yp)],
            2: [self.hop(i, 2 + k, s.at[zt[k], y, f], b3.at[nz + k], zs[k]) for k in range(nz - 1)],
        }
        one = {
            0: [self.hop(i, 0, s.at[:, 1 - y], b2, yp)],
            1: [self.hop(i, 1 + k, s.at[zt[k], y], b3.at[pl.ds(2 * k, 2)], zs[k]) for k in range(nz - 1)],
            2: [self.hop(i, nz, s.at[z, y, 1 - f], b3.at[2 * (nz - 1)], xp)],
        }
        return zero, one

    def stage(self, i, st):
        z, y, c, f = self.place
        nz = self.nz
        self.done.add((i, st))
        s, b2, b3 = self.sums[i], self.second[i], self.third[i]
        copies = self.copies(i)
        zs, yp, xp = self.peers()
        ringed = i < len(self.sums) - 1
        if st == 0 and ringed and i >= RING:
            pl.semaphore_wait(self.free.at[i % RING], nz + 1)

        @pl.when(c == 0)
        def _():
            if st:
                for copy in copies[0][st - 1]:
                    copy.wait_recv()
            if st == 0:
                copies[0][0][0].start()
            if st == 1:
                add_blocks(s.at[:, 1 - y, f], [b2.at[:, 1 - y]])
                copies[0][1][0].start()
                add_blocks(s.at[:, y, f], [b2.at[:, y]])
            if st == 2:
                for k in range(nz - 1):
                    zt = lax.rem(z + k + 1, nz)
                    add_blocks(s.at[zt, y, f], [b3.at[zt]])
                    copies[0][2][k].start()
                add_blocks(s.at[z, y, f], [b3.at[z]])
            if st == 3:
                add_blocks(s.at[z, y, f], [b3.at[nz + k] for k in range(nz - 1)], self.outs[i])

        @pl.when(c == 1)
        def _():
            if st:
                for copy in copies[1][st - 1]:
                    copy.wait_recv()
            if st == 0:
                copies[1][0][0].start()
            if st == 1:
                for k in range(nz - 1):
                    zt = lax.rem(z + k + 1, nz)
                    add_blocks(s.at[zt, y], [b2.at[zt]])
                    copies[1][1][k].start()
                add_blocks(s.at[z, y], [b2.at[z]])
            if st == 2:
                add_blocks(s.at[z, y, 1 - f], [b3.at[2 * k + 1 - f] for k in range(nz - 1)])
                copies[1][2][0].start()
                add_blocks(s.at[z, y, f], [b3.at[2 * k + f] for k in range(nz - 1)])
            if st == 3:
                add_blocks(s.at[z, y, f], [b3.at[2 * (nz - 1)]], self.outs[i])

        if st == 3 and ringed and i + RING < len(self.sums) - 1:
            for peer in zs + [yp, xp]:
                pl.semaphore_signal(self.free.at[i % RING], inc=1, device_id=peer, device_id_type=MESH)

    def tick(self, t):
        for st in range(1, 4):
            i = t - st
            if (i, st - 1) in self.done and (i, st) not in self.done:
                self.stage(i, st)

    def finish(self, i):
        for core in range(2):

            @pl.when(self.place[2] == core)
            def _():
                for copies in self.copies(i)[core].values():
                    for copy in copies:
                        copy.wait_send()


class Producer:
    def __init__(self, place, buf, land, sems):
        self.place, self.buf, self.land = place, buf, land
        self.send, self.recv, self.credit = sems
        z, y, c, f = place
        self.core = dev(z, y, 1 - c, f)
        self.made, self.pending = 0, None

    def copy(self, slot):
        theirs = self.buf.at[slot, :, 1 - self.place[2]]
        return remote(theirs, self.land.at[slot], self.send.at[slot], self.recv.at[slot], self.core)

    def before(self, slot):
        self.copy(slot).wait_send()
        pl.semaphore_wait(self.credit.at[slot], 1)

    def absorb(self, j, target):
        c = self.place[2]
        slot = lax.rem(j, 2)
        self.copy(slot).wait_recv()
        for i in range(4):
            ref = target(j, i)
            for k in range(2):
                ref[k] = (self.buf[slot, i, c, k].astype(F32) + self.land[slot, i, k].astype(F32)).astype(BF)
        pl.semaphore_signal(self.credit.at[slot], inc=1, device_id=self.core, device_id_type=MESH)

    def flush(self):
        if self.pending is not None:
            self.absorb(*self.pending)
            self.pending = None

    def run(self, count, product, where, target, hooks=None):
        fresh, pending = self.made == 0, self.pending

        @pl.loop(0, count)
        def _(j):
            slot = lax.rem(j, 2)
            if not fresh:
                self.before(slot)
            elif count > 2:

                @pl.when(j >= 2)
                def _():
                    self.before(slot)

            v = product(j)
            for i in range(4):
                for k in range(2):
                    for core in range(2):
                        at = where(i, core, k)
                        self.buf[slot, i, core, k] = v[at : at + BLOCK].astype(BF)
            self.copy(slot).start()
            if pending is not None:

                @pl.when(j == 0)
                def _():
                    self.absorb(*pending)

            @pl.when(j >= 1)
            def _():
                self.absorb(j - 1, target)

            run_hooks(j, hooks)

        self.made += count
        self.pending = (count - 1, target)

    def finish(self):
        for slot in range(2):
            self.before(slot)


def row_blocks(i, core, k):
    return BLOCK * (4 * i + 2 * core + k)


def deep_blocks(i, core, k):
    return BLOCK * (8 * core + 4 * k + i)


def attend_forward(c, qkv, cross, bias, att, lse, hooks):
    rows, d = att.shape
    half = lane_half()
    lane = lax.broadcasted_iota(jnp.int32, (1, PAIR), 1)
    rt = rows // 2

    def one(q, blocks):
        scores = []
        for keys, _, extra in blocks:
            s = dot_nt(q, keys) * SCALE2
            scores.append(s if extra is None else s + extra)
        peak = functools.reduce(jnp.maximum, [jnp.max(s, -1, keepdims=True) for s in scores])
        total = None
        for s, (_, values, _) in zip(scores, blocks):
            part = dot_nn(jnp.exp2(s - peak).astype(BF), values)
            total = part if total is None else total + part
        return total, peak

    def pair(p, second):
        cols = pl.ds(pl.multiple_of(p * PAIR, PAIR), PAIR)
        kcols = pl.ds(pl.multiple_of(d + p * PAIR, PAIR), PAIR)
        vcols = pl.ds(pl.multiple_of(2 * d + p * PAIR, PAIR), PAIR)
        def half_rows(r, part):
            results = []
            for h in range(2):
                mine = half == h
                q = jnp.where(mine, qkv[part, cols], 0.0).astype(BF)

                def val(v):
                    return jnp.where(mine, v, 1.0).astype(BF)

                if second:
                    blocks = [(cross[:, cols], val(cross[:, kcols]), None)]
                    if r > 0:
                        blocks.append((qkv[pl.ds(0, rt), kcols], val(qkv[pl.ds(0, rt), vcols]), None))
                    blocks.append((qkv[part, kcols], val(qkv[part, vcols]), bias[part, pl.ds(r * rt, rt)]))
                else:
                    blocks = [(qkv[:, kcols], val(qkv[:, vcols]), bias[part, :])]
                total, peak = one(q, blocks)
                sums = pltpu.roll(total, HD, axis=1)
                results.append(total / sums)
                both = jnp.where(mine, sums, total)
                lse[part, :] = jnp.where(lane == 2 * p + h, peak + jnp.log2(both), lse[part, :])
            att[part, cols] = jnp.where(half == 0, results[0], results[1]).astype(BF)

        if second:
            for r in range(2):
                half_rows(r, pl.ds(r * rt, rt))
        else:
            tiles(2, rt, half_rows)

    @pl.loop(0, d // PAIR)
    def _(p):
        for second in range(2):

            @pl.when(c == second)
            def _():
                pair(p, second == 1)

        run_hooks(p, hooks)


SHARED = 5


def attend_backward(c, qkv, cross, biast, lset, deltat, far_lse, far_delta, go, gq, gq2, more, hooks):
    rows, d = go.shape
    half = lane_half()
    rt = rows // 2
    pairs = d // PAIR

    def term(p, keys, values, krows, qrows, queries, grads, lse, delta, masked, total):
        gk = gv = None
        for h in range(2):
            mine = half == h
            q = jnp.where(mine, queries, 0.0).astype(BF)
            g = jnp.where(mine, grads, 0.0).astype(BF)
            km = jnp.where(mine, keys, 0.0).astype(BF)
            s = dot_nt(keys, q) * SCALE2
            if masked:
                s = s + biast[krows, qrows]
            pr = jnp.exp2(s - lse[pl.ds(2 * p + h, 1), qrows])
            gs = (pr * (dot_nt(values, g) - delta[pl.ds(2 * p + h, 1), qrows])).astype(BF)
            k1, v1 = dot_nn(gs, q), dot_nn(pr.astype(BF), g)
            gk, gv = (k1, v1) if gk is None else (gk + k1, gv + v1)
            total[qrows, :] = total[qrows, :] + dot_tn(gs, km)
        return gk, gv

    every = pl.ds(0, rows)
    first, last = pl.ds(0, PAIR), pl.ds(PAIR, PAIR)

    @pl.loop(0, pairs)
    def _(i):
        @pl.when(c == 0)
        def _():
            heavy = i < pairs - SHARED
            p = lax.rem(i + SHARED, pairs)
            cols = pl.ds(pl.multiple_of(p * PAIR, PAIR), PAIR)
            kcols = pl.ds(pl.multiple_of(d + p * PAIR, PAIR), PAIR)
            vcols = pl.ds(pl.multiple_of(2 * d + p * PAIR, PAIR), PAIR)
            gq[...] = jnp.zeros_like(gq)

            @pl.when(heavy)
            def _():
                gq2[...] = jnp.zeros_like(gq2)

                def far_part(r, krows):
                    more[krows, first], more[krows, last] = term(
                        p, qkv[krows, kcols], qkv[krows, vcols], krows, every, cross[:, cols], cross[:, kcols], far_lse, far_delta, False, gq2
                    )

                tiles(2, rt, far_part)
                cross[:, cols] = (gq2[...] * 0.125).astype(BF)

            @pl.when(i == pairs - SHARED)
            def _():
                more[:, first] = jnp.zeros_like(gq)
                more[:, last] = jnp.zeros_like(gq)

            def own_part(r, krows):
                gk, gv = term(
                    p, qkv[krows, kcols], qkv[krows, vcols], krows, every, qkv[:, cols], go[:, cols], lset, deltat, True, gq
                )
                qkv[krows, kcols] = ((gk + more[krows, first]) * 0.125).astype(BF)
                qkv[krows, vcols] = (gv + more[krows, last]).astype(BF)

            tiles(2, rt, own_part)
            qkv[:, cols] = (gq[...] * 0.125).astype(BF)

        @pl.when(c == 1)
        def _():
            p = i
            cols = pl.ds(pl.multiple_of(p * PAIR, PAIR), PAIR)
            kcols = pl.ds(pl.multiple_of(d + p * PAIR, PAIR), PAIR)
            vcols = pl.ds(pl.multiple_of(2 * d + p * PAIR, PAIR), PAIR)
            gq[...] = jnp.zeros_like(gq)

            @pl.when(p < SHARED)
            def _():
                def near_part(r, krows):
                    gk, gv = term(
                        p, cross[krows, cols], cross[krows, kcols], krows, every, qkv[:, cols], go[:, cols], lset, deltat, False, gq
                    )
                    cross[krows, cols] = (gk * 0.125).astype(BF)
                    cross[krows, kcols] = gv.astype(BF)

                tiles(2, rt, near_part)

            for r in range(2):
                krows, qrows = pl.ds(r * rt, rt), pl.ds(r * rt, rows - r * rt)
                gk, gv = term(
                    p, qkv[krows, kcols], qkv[krows, vcols], krows, qrows, qkv[qrows, cols], go[qrows, cols], lset, deltat, True, gq
                )
                qkv[krows, kcols] = (gk * 0.125).astype(BF)
                qkv[krows, vcols] = gv.astype(BF)
            qkv[:, cols] = (gq[...] * 0.125).astype(BF)

        run_hooks(i, hooks)


def layer_kernel(nz, *refs):
    (
        frames_in, cot_in, pre_in, s_qkv, s_out, s_up, s_down, s_par,
        fo, gi, gl, f_qkv, f_out, f_up, f_down, f_par, g_qkv, g_out, g_up, g_down, g_par,
        x, cot, pre, h1, qkv, cross, att, x1, h2, a, gp, wa, wb, gh, gz, go, bias, narrow, narrow2, lset, deltat, far_lse, far_delta,
        acc, par, parv, ht, buf, land, sdown, spar, ptheirs, pland, second, third, psecond, pthird,
        ag_send, ag_recv, ag_own, rs_send, rs_recv, rs_free, p_send, p_recv, p_credit,
        load_sem, swap_sem, io_sem, io_recv,
    ) = refs
    place = z, y, c, f = coords()
    rows, d = x.shape
    ff = a.shape[-1]
    core, far = dev(z, y, 1 - c, f), dev(z, y, 1 - c, 1 - f)
    straight = c == f
    nk = d // WIDE

    chunks = [(4, 0, 16, 0, PAIR)]
    chunks += [(0, 0, BLOCK, d + h * TILE, TILE) for h in range(2)] + [(0, 0, BLOCK, b * d, d) for b in (2, 0)]
    chunks += [(1, 0, BLOCK, 0, d)]
    chunks += [(2, 0, BLOCK, k * WIDE, WIDE) for k in range(ff // WIDE)]
    down_rows = [(0, BLOCK), (BLOCK, BLOCK), (2 * BLOCK, BLOCK), (3 * BLOCK, BLOCK // 2), (7 * BLOCK // 2, BLOCK // 2)]
    chunks += [(3, r0, r, 0, d) for r0, r in down_rows]
    ag = Gather(nz, place, (s_qkv, s_out, s_up, s_down, s_par), (f_qkv, f_out, f_up, f_down, f_par), chunks, (ag_send, ag_recv, ag_own))

    ups, downs = ff // WIDE, 4
    sums = [sdown.at[k] for k in range(downs)]
    sums += [a.at[:, :, :, :, pl.ds(k * WIDE, WIDE)] for k in range(ups)]
    tail = [(3 * d, d), (d, d), (2 * d, d), (0, TILE), (TILE, TILE)]
    sums += [gp.at[:, :, :, :, pl.ds(c0, w)] for c0, w in tail]
    goes = [g_down.at[pl.ds(k * BLOCK, BLOCK)] for k in range(downs)]
    goes += [g_up.at[:, pl.ds(k * WIDE, WIDE)] for k in range(ups)]
    goes += [g_out] + [g_qkv.at[:, pl.ds(c0, w)] for c0, w in tail[1:]]
    n = len(sums)
    widths = [WIDE] * (downs + ups) + [w for _, w in tail]
    rs = Scatter(
        nz, place, sums + [spar], [second.at[i % RING, :, :, :, pl.ds(0, widths[i])] for i in range(n)] + [psecond],
        [third.at[i % RING, :, :, pl.ds(0, widths[i])] for i in range(n)] + [pthird], goes + [g_par], (rs_send, rs_recv, rs_free),
    )
    maker = Producer(place, buf, land, (p_send, p_recv, p_credit))

    for i in range(len(chunks)):
        ag.local(i).start()
    greet(all_peers(nz, *place) + [far])

    swaps = []
    quarter = rows // 4
    quarters = [pl.ds(i * quarter, quarter) for i in range(4)]
    moves = [(pre_in, pre)]
    moves += [(cot_in.at[q], cot.at[q]) for q in quarters] + [(frames_in.at[q], x.at[q]) for q in quarters]
    for i, (src, dst) in enumerate(moves):
        swaps.append((pltpu.make_async_copy(src, dst, swap_sem.at[i, 0]), remote(src, dst, swap_sem.at[i, 1], swap_sem.at[i, 2], far)))

    def swap_start(i):
        @pl.when(straight)
        def _():
            swaps[i][0].start()

        @pl.when(jnp.logical_not(straight))
        def _():
            swaps[i][1].start()

    def swap_wait(i):
        @pl.when(straight)
        def _():
            swaps[i][0].wait()

        @pl.when(jnp.logical_not(straight))
        def _():
            swaps[i][1].wait()

    def between(i, src, dst):
        return remote(src, dst, swap_sem.at[i, 1], swap_sem.at[i, 2], core)

    def ag_tick(t):
        return lambda: ag.tick(t)

    def rs_tick(t):
        return lambda: rs.tick(t)

    def rs_begin(i):
        return lambda: rs.stage(i, 0)

    def small(b):
        return pl.ds(b * BLOCK, BLOCK)

    def load(i, src, dst):
        return pltpu.make_async_copy(src, dst, load_sem.at[i])

    def load_block(i, b):
        if b == 3:
            return load(i, f_out, wa.at[:, :, :, :, small(3)])
        return load(i, f_qkv.at[:, :, :, :, :, pl.ds(b * d, d)], wa.at[:, :, :, :, small(b)])

    def block(b, at=slice(None)):
        v = wa[at, :, :, :, small(b)]
        return v.reshape(math.prod(v.shape[:-1]), d)

    ag.stage(0, 0)
    ag.stage(1, 0)
    swap_start(0)
    swap_start(5)
    ag.stage(0, 1)
    ag.tick(2)
    swap_start(6)
    ag.tick(3)
    swap_start(7)
    ag.stage(0, 4)
    get_par = load(0, f_par, parv)
    get_par.start()
    swap_wait(0)
    fill_bias(bias, pre[0:1, 0:1], c, False)
    get_par.wait()
    for t in range(d // PAIR):
        total = None
        for k in range(4):
            piece = parv[t // 2, t % 2, k // 2, k % 2].astype(F32)
            total = piece if total is None else total + piece
        par[:, pl.ds(t * PAIR, PAIR)] = total
    step = 64

    def norm_one(j, part):
        nrm, _ = normalise(x[part, :].astype(F32))
        h1[part, :] = (nrm * par[0:1, :] + par[2:3, :]).astype(BF)

    ag.tick(4)
    swap_start(8)
    for i in range(4):
        swap_wait(5 + i)
    tiles(rows // step, step, norm_one)
    keyvals = between(14, qkv.at[:, pl.ds(d, 2 * d)], cross)
    ag.stage(1, 4)
    for i, b in enumerate((1, 2, 0)):
        ag.tick(5 + i)
        ag.stage(2 + i, 4)
        get = load_block(1 + i, b)
        get.start()
        get.wait()
        for t in range(d // TILE):
            cols = pl.ds(t * TILE, TILE)
            w = wa[:, :, :, :, small(b), cols].reshape(d, TILE)
            qkv[:, pl.ds(b * d + t * TILE, TILE)] = dot_nn(h1[...], w).astype(BF)
        swap_start(1 + i)
        if b == 2:

            @pl.when(c == 0)
            def _():
                keyvals.start()

    @pl.when(c == 1)
    def _():
        keyvals.wait_recv()

    swap_start(4)
    narrow[...] = jnp.zeros_like(narrow)
    attend_forward(c, qkv, cross, bias, att, narrow, {0: ag_tick(8), 5: ag_tick(9)})
    ag.stage(5, 4)
    get_out = load_block(4, 3)
    get_out.start()

    @pl.when(c == 0)
    def _():
        keyvals.wait_send()

    lset[...] = narrow[...].T[:H, :]

    def get_up(k):
        return load(5 + k, f_up.at[:, :, :, :, :, pl.ds(k * WIDE, WIDE)], wb.at[:, :, :, :, :, pl.ds(k * WIDE, WIDE)])

    ag.stage(6, 4)
    get_up(0).start()
    get_out.wait()
    for t in range(d // TILE):
        cols = pl.ds(t * TILE, TILE)
        w = wa[:, :, :, :, small(3), cols].reshape(d, TILE)
        x1[:, cols] = x[:, cols].astype(F32) + dot_nn(att[...], w)
    ag.tick(10)

    def norm_two(j, part):
        nrm, _ = normalise(x1[part, :])
        h2[part, :] = (nrm * par[1:2, :] + par[3:4, :]).astype(BF)

    tiles(rows // step, step, norm_two)
    u = gh.at[:, pl.ds(0, TILE)]

    def up(cols):
        gh[:, pl.ds(0, TILE)] = dot_nn(h2[...], wb[:, :, :, :, :, cols].reshape(d, TILE))

        @pl.loop(0, rows // BLOCK)
        def _(j):
            at = (lax.div(j, 4), lax.rem(lax.div(j, 2), 2), lax.rem(j, 2), slice(None), cols)
            v = gh[pl.ds(pl.multiple_of(j * BLOCK, BLOCK), BLOCK), pl.ds(0, TILE)]
            phi = 0.5 * (1.0 + lax.erf(v * math.sqrt(0.5)))
            dens = jnp.exp2(v * v * (-0.5 * LOG2E)) * (1.0 / math.sqrt(2.0 * math.pi))
            a[at] = (v * phi).astype(BF)
            gp[at] = (phi + v * dens).astype(BF)

    for i in range(4):
        swap_wait(1 + i)

    def down_product(j):
        for k in range(ups):

            @pl.when(j == 2 * k)
            def _():
                if k:
                    ag.stage(6 + k, 4)
                    get_up(k).start()
                get_up(k).wait()

        cols = pl.ds(pl.multiple_of(j * TILE, TILE), TILE)
        up(cols)
        for k in range(ups):

            @pl.when(j == 2 * k)
            def _():
                ag.tick(11 + k, (0, 1))

            @pl.when(j == 2 * k + 1)
            def _():
                ag.tick(11 + k, (2, 3))

        return dot_tn(flat(a, cols), cot[...])

    maker.run(2 * ups, down_product, deep_blocks, lambda j, i: sdown.at[i, lax.div(j, 2), lax.rem(j, 2)])

    def get_down(k):
        part = pl.ds(*down_rows[k])
        return load(9 + k, f_down.at[:, :, :, :, part], wa.at[:, :, :, :, part])

    ag.tick(15)
    maker.flush()
    ag.tick(16)
    ag.tick(17)
    rs.stage(0, 0)
    for k in range(len(down_rows)):
        ag.stage(10 + k, 4)
        get_down(k).start()
    for k in range(len(down_rows)):
        get_down(k).wait()
    for k in range(2):
        rs.stage(1 + k, 0)
        cols = pl.ds(k * TILE, TILE)
        w = wa[:, :, :, :, :, cols].reshape(ff, TILE)
        go[:, cols] = (x1[:, cols] + dot_nn(flat(a, slice(None)), w)).astype(BF)

    outs = []
    for q in quarters:
        outs.append(
            (
                pltpu.make_async_copy(go.at[q], fo.at[q], io_sem.at[len(outs)]),
                remote(go.at[q], fo.at[q], io_sem.at[len(outs)], io_recv.at[len(outs)], far),
            )
        )

    def either(pair, act_on):
        @pl.when(straight)
        def _():
            act_on(pair[0])

        @pl.when(jnp.logical_not(straight))
        def _():
            act_on(pair[1])

    def begin(pair):
        either(pair, lambda copy: copy.start())

    def end(pair):
        either(pair, lambda copy: copy.wait())

    begin(outs[0])
    def act(j, cols):
        w = wa[lax.div(j, 2), lax.rem(j, 2)].reshape(TILE, d)
        v = dot_nt(cot[...], w) * flat(gp, cols).astype(F32)
        gp[:, :, :, :, cols] = v.astype(BF).reshape(a.shape[:-1] + (TILE,))

    rs.tick(1)
    rs.stage(3, 0)
    tiles(8, TILE, act)
    begin(outs[1])
    for i, b in enumerate((3, 0, 1, 2)):
        load_block(14 + i, b).start()
    ht[...] = h2[...].T
    for i in range(2):
        gh[:, pl.ds(i * TILE, TILE)] = dot_nt(flat(gp, slice(None)), wb[2 * i : 2 * i + 2].reshape(TILE, ff))
        if i == 0:
            rs.tick(2)
    begin(outs[2])
    acc[...] = jnp.zeros_like(acc)
    step = 32

    def collect(row, v):
        part = v.reshape(step // 8, 8, d)
        acc[row] = acc[row] + functools.reduce(jnp.add, [part[i] for i in range(step // 8)])

    def back_two(j, part):
        nrm, scale = normalise(x1[part, :])
        g = gh[part, :]
        collect(1, g * nrm)
        collect(3, g)
        total = cot[part, :].astype(F32) + norm_back(g, nrm, scale, par[1:2, :])
        x1[part, :] = total
        gz[part, :] = total.astype(BF)

    tiles(rows // step, step, back_two)

    def row_half(j):
        return ht[pl.ds(pl.multiple_of(lax.rem(j, 2) * TILE, TILE), TILE), :]

    def wide(j):
        return pl.ds(pl.multiple_of(lax.div(j, 2) * WIDE, WIDE), WIDE)

    def up_product(j):
        return dot_nn(row_half(j), flat(gp, wide(j)))

    def target(ref, first):
        def of(j, i):
            cols = pl.ds(pl.multiple_of(first + lax.div(j, 2) * WIDE, WIDE), WIDE)
            return ref.at[2 * lax.rem(j, 2) + i // 2, i % 2, :, :, cols]

        return of

    rs.tick(3)
    begin(outs[3])
    maker.run(
        2 * ups, up_product, row_blocks, target(a, 0), {2: rs_begin(4), 3: rs_tick(4), 4: rs_begin(5), 6: rs_begin(6)}
    )
    maker.flush()
    rs.stage(7, 0)
    for pair in outs:
        end(pair)
    load_block(14, 3).wait()
    for i in range(2):
        go[:, pl.ds(i * TILE, TILE)] = dot_nt(gz[...], block(3, pl.ds(2 * i, 2))).astype(BF)
    pick = (
        lax.broadcasted_iota(jnp.int32, (H, d), 1) // HD == lax.broadcasted_iota(jnp.int32, (H, d), 0)
    ).astype(BF)
    for i in range(4):
        part = pl.ds(i * quarter, quarter)
        prod = go[part, :].astype(F32) * att[part, :].astype(F32)
        high = prod.astype(BF)
        low = (prod - high.astype(F32)).astype(BF)
        deltat[:, part] = dot_nt(pick, high) + dot_nt(pick, low)
    low_cols, high_cols = pl.ds(0, SHARED * PAIR), pl.ds(SHARED * PAIR, d - SHARED * PAIR)
    high_cols2 = pl.ds(d + SHARED * PAIR, d - SHARED * PAIR)
    low_cols2 = pl.ds(d, SHARED * PAIR)

    lends = [
        between(9, qkv.at[:, high_cols], cross.at[:, high_cols]),
        between(15, go.at[:, high_cols], cross.at[:, high_cols2]),
        between(16, lset, far_lse),
        between(10, deltat, far_delta),
    ]
    gives = [
        between(11, cross.at[:, low_cols], cross.at[:, low_cols]),
        between(12, cross.at[:, low_cols2], cross.at[:, low_cols2]),
    ]
    returns = between(13, cross.at[:, high_cols], cross.at[:, high_cols])

    @pl.when(c == 1)
    def _():
        for copy in lends:
            copy.start()

    rs.tick(5)
    ht[...] = att[...].T
    maker.run(2, lambda j: dot_nn(row_half(j), gz[...]), row_blocks, target(gp, 3 * d))
    fill_bias(bias, pre[0:1, 0:1], c, True)

    @pl.when(c == 0)
    def _():
        for copy in lends:
            copy.wait_recv()

    @pl.when(c == 1)
    def _():
        for copy in lends:
            copy.wait_send()

    def give_back():
        @pl.when(c == 1)
        def _():
            for copy in gives:
                copy.start()

    def return_queries():
        @pl.when(c == 0)
        def _():
            returns.start()

    def flush_tick():
        maker.flush()
        rs.stage(8, 0)
        rs.tick(6)

    hooks = {0: flush_tick, 2: return_queries, 3: rs_tick(7), 4: give_back, 6: rs_tick(8)}
    attend_backward(c, qkv, cross, bias, lset, deltat, far_lse, far_delta, go, narrow, narrow2, gh, hooks)
    ht[...] = h1[...].T

    @pl.when(c == 1)
    def _():
        for copy in gives:
            copy.wait_send()
        returns.wait_recv()

        def add(j, part):
            qkv[part, high_cols] = (qkv[part, high_cols].astype(F32) + cross[part, high_cols].astype(F32)).astype(BF)

        tiles(rows // step, step, add)

    @pl.when(c == 0)
    def _():
        returns.wait_send()
        for copy in gives:
            copy.wait_recv()

        def add(j, part):
            for base in (0, d):
                to, src = pl.ds(d + base, SHARED * PAIR), pl.ds(base, SHARED * PAIR)
                qkv[part, to] = (qkv[part, to].astype(F32) + cross[part, src].astype(F32)).astype(BF)

        tiles(rows // step, step, add)

    def mixed_cols(j):
        return pl.ds(pl.multiple_of(lax.rem(lax.div(j, 2) + 1, 3) * d, d), d)

    def mixed_target(j, i):
        return gp.at[2 * lax.rem(j, 2) + i // 2, i % 2, :, :, mixed_cols(j)]

    maker.run(
        6, lambda j: dot_nn(row_half(j), qkv[:, mixed_cols(j)]), row_blocks, mixed_target, {1: rs_tick(9), 2: rs_begin(9), 4: rs_begin(10)}
    )
    maker.flush()
    rs.stage(11, 0)
    rs.stage(12, 0)
    for i, b in enumerate((0, 1, 2)):
        load_block(15 + i, b).wait()
    for i in range(2):
        total = None
        for b in range(3):
            part = dot_nt(qkv[:, pl.ds(b * d, d)], block(b, pl.ds(2 * i, 2)))
            total = part if total is None else total + part
        gh[:, pl.ds(i * TILE, TILE)] = total
        if i == 0:
            rs.tick(10)

    def back_one(j, part):
        nrm, scale = normalise(x[part, :].astype(F32))
        g = gh[part, :]
        collect(0, g * nrm)
        collect(2, g)
        total = x1[part, :] + norm_back(g, nrm, scale, par[0:1, :])
        gh[part, :] = total
        gz[part, :] = total.astype(BF)

    tiles(rows // step, step, back_one)
    backs = []
    for i, q in enumerate(quarters):
        backs.append(
            (
                pltpu.make_async_copy(gh.at[q], gi.at[q], io_sem.at[4 + i]),
                remote(gz.at[q], gl.at[q], io_sem.at[4 + i], io_recv.at[4 + i], far),
            )
        )
    begin(backs[0])
    for i in range(4):
        par[i : i + 1, :] = jnp.sum(acc[i], 0, keepdims=True)
    for t in range(d // PAIR):
        row = par[:, pl.ds(t * PAIR, PAIR)].astype(BF)
        for k in range(2):
            spar[t // 2, t % 2, k] = row
            ptheirs[t // 2, t % 2, k] = row
    pars = remote(ptheirs, pland, io_sem.at[8], io_recv.at[8], core)
    pars.start()
    rs.tick(11)
    pars.wait_recv()
    add_blocks(spar, [pland])
    rs.stage(n, 0)
    begin(backs[1])
    for i, st in ((11, 1), (12, 1), (10, 2), (9, 3)):
        rs.stage(i, st)
    begin(backs[2])
    for i, st in ((n, 1), (11, 2), (12, 2)):
        rs.stage(i, st)
    begin(backs[3])
    for i, st in ((10, 3), (n, 2), (11, 3), (12, 3), (n, 3)):
        rs.stage(i, st)
    for pair in backs:
        end(pair)
    pars.wait_send()
    for i in range(len(chunks)):
        ag.finish(i)
    for i in range(n + 1):
        rs.finish(i)
    maker.finish()


def layer(nz, frames_in, cot, pre, w_qkv, w_out, w_up, w_down, tile):
    rows, d = frames_in.shape
    ff = w_up.shape[1]
    S = jax.ShapeDtypeStruct
    V = pltpu.VMEM
    REG = pltpu.SemaphoreType.REGULAR
    hbm, vm = pl.BlockSpec(memory_space=pl.ANY), pl.BlockSpec(memory_space=V)
    shards = (w_qkv, w_out, w_up, w_down, tile)
    parts = (nz, 2, 2, BLOCK)
    full = (nz, 2, 2, 2)
    return pl.pallas_call(
        functools.partial(layer_kernel, nz),
        out_shape=[S((rows, d), BF), S((rows, d), F32), S((rows, d), BF)]
        + [S(full + w.shape, BF) for w in shards]
        + [S(w.shape, F32) for w in shards],
        in_specs=[hbm] * 8,
        out_specs=[hbm] * 8 + [vm] * 5,
        scratch_shapes=[
            V((rows, d), BF), V((rows, d), BF), V((8, PAIR), jnp.int32), V((rows, d), BF), V((rows, 3 * d), BF),
            V((rows, 2 * d), BF), V((rows, d), BF), V((rows, d), F32), V((rows, d), BF),
            V(parts + (ff,), BF), V(parts + (ff,), BF),
            V(full + w_down.shape, BF), V(full + w_up.shape, BF),
            V((rows, d), F32), V((rows, d), BF), V((rows, d), BF), V((rows, rows), F32), V((rows, PAIR), F32), V((rows, PAIR), F32),
            V((H, rows), F32), V((H, rows), F32), V((H, rows), F32), V((H, rows), F32), V((4, 8, d), F32), V((16, d), F32), V(full + (16, PAIR), BF),
            V((d, rows), BF), V((2, 4, 2, 2, BLOCK, WIDE), BF), V((2, 4, 2, BLOCK, WIDE), BF),
            V((4,) + parts + (d,), BF), V((nz, 2, 2, 16, PAIR), BF), V((nz, 2, 2, 16, PAIR), BF), V((nz, 2, 2, 16, PAIR), BF),
            V((RING, nz, 2, BLOCK, WIDE), BF), V((RING, 7, BLOCK, WIDE), BF), V((nz, 2, 16, PAIR), BF), V((7, 16, PAIR), BF),
        ]
        + Gather.sem_shapes(15)
        + Scatter.sem_shapes(14)
        + [DMA((2,)), DMA((2,)), REG((2,)), DMA((18,)), DMA((17, 3)), DMA((9,)), DMA((9,))],
        compiler_params=pltpu.CompilerParams(collective_id=0, has_side_effects=True, vmem_limit_bytes=63 * 2**20),
    )(frames_in, cot, pre, *shards)


def settle_kernel(fo, gi, gl, g_qkv, g_out, g_up, g_down, g_par, fo_, gi_, qkv_, out_, up_, down_, gains_, shifts_, narrow, wide, *rest):
    straight = lax.rem(lax.axis_index("dp"), 2) == lax.axis_index("fsdp")
    stops, sems = rest[:5], rest[5]
    pairs = ((fo, fo_), (g_qkv, qkv_), (g_out, out_), (g_up, up_), (g_down, down_))
    ins = [pltpu.make_async_copy(src, stop, sems.at[0, i]) for i, ((src, _), stop) in enumerate(zip(pairs, stops))]
    outs = [pltpu.make_async_copy(stop, dst, sems.at[1, i]) for i, ((_, dst), stop) in enumerate(zip(pairs, stops))]
    rows = gi.shape[0] // 4
    parts = [pl.ds(i * rows, rows) for i in range(4)]
    own = [pltpu.make_async_copy(gi.at[p], wide.at[p], sems.at[2, i]) for i, p in enumerate(parts)]
    came = [pltpu.make_async_copy(gl.at[p], narrow.at[p], sems.at[2, i]) for i, p in enumerate(parts)]
    puts = [pltpu.make_async_copy(wide.at[p], gi_.at[p], sems.at[3, i]) for i, p in enumerate(parts)]

    @pl.when(straight)
    def _():
        for get in own:
            get.start()

    @pl.when(jnp.logical_not(straight))
    def _():
        for get in came:
            get.start()

    for copy in ins:
        copy.start()
    width = gains_.shape[1]
    mine = lax.rem(lax.axis_index("dp") * 2 + lax.axis_index("fsdp"), PAIR // width)
    small = g_par[:, pl.ds(0, width)]
    for i in range(1, PAIR // width):
        small = jnp.where(mine == i, g_par[:, pl.ds(i * width, width)], small)
    gains_[...] = small[0:2]
    shifts_[...] = small[2:4]

    @pl.when(straight)
    def _():
        for get, put in zip(own, puts):
            get.wait()
            put.start()

    @pl.when(jnp.logical_not(straight))
    def _():
        for get, put, p in zip(came, puts, parts):
            get.wait()
            wide[p, :] = narrow[p, :].astype(F32)
            put.start()

    for get, put in zip(ins, outs):
        get.wait()
        put.start()
    for put in puts + outs:
        put.wait()


def settle(width, fo, gi, gl, *grads):
    S = jax.ShapeDtypeStruct
    V = pltpu.VMEM
    hbm, vm = pl.BlockSpec(memory_space=pl.ANY), pl.BlockSpec(memory_space=V)
    kept = (fo, gi) + grads[:4]
    return pl.pallas_call(
        settle_kernel,
        out_shape=[S(v.shape, v.dtype) for v in kept] + [S((2, width), F32)] * 2,
        in_specs=[hbm] * 7 + [vm],
        out_specs=[hbm] * 6 + [vm] * 2,
        scratch_shapes=[V(gl.shape, BF), V(gi.shape, F32)] + [V(v.shape, v.dtype) for v in (fo,) + grads[:4]] + [DMA((4, 5))],
        compiler_params=pltpu.CompilerParams(vmem_limit_bytes=VMEM_LIMIT),
    )(fo, gi, gl, *grads)


def norm_rows(values, gain, shift):
    center = values - jnp.mean(values, -1, keepdims=True)
    spread = jnp.mean(center * center, -1, keepdims=True)
    return center * lax.rsqrt(spread + EPS) * gain + shift


def collect(w_qkv, w_out, w_up, w_down, gains, shifts):
    return (
        lax.all_gather(w_qkv, ("dp", "fsdp"), axis=0, tiled=True),
        lax.all_gather(w_out, ("dp", "fsdp"), axis=0, tiled=True),
        lax.all_gather(w_up, ("dp", "fsdp"), axis=0, tiled=True),
        lax.all_gather(w_down, ("dp", "fsdp"), axis=0, tiled=True),
        lax.all_gather(gains, ("dp", "fsdp"), axis=1, tiled=True),
        lax.all_gather(shifts, ("dp", "fsdp"), axis=1, tiled=True),
    )


def split_heads(matrix):
    return matrix.reshape(matrix.shape[0], H, HD).transpose(1, 0, 2)


def join_heads(stacked):
    return stacked.transpose(1, 0, 2).reshape(stacked.shape[1], H * HD)


def masked_scores(query_one, key_one, allowed):
    scores = jnp.dot(query_one, key_one.T, preferred_element_type=jnp.float32) * 0.125
    return jnp.where(allowed, scores, -1e30)


def forward(inputs, weights, allowed):
    w_qkv, w_out, w_up, w_down, gains, shifts = weights
    width = inputs.shape[1]
    gain_rows = gains.astype(jnp.float32)
    shift_rows = shifts.astype(jnp.float32)
    normed = norm_rows(inputs, gain_rows[0], shift_rows[0]).astype(jnp.bfloat16)
    mixed = jnp.dot(normed, w_qkv, preferred_element_type=jnp.float32).astype(jnp.bfloat16)
    queries = mixed[:, :width]
    keys_all, values_all = (
        lax.all_gather(mixed[:, width : 2 * width], "fsdp", axis=0, tiled=True),
        lax.all_gather(mixed[:, 2 * width :], "fsdp", axis=0, tiled=True),
    )
    query_heads = split_heads(queries)
    key_heads = split_heads(keys_all)
    value_heads = split_heads(values_all)

    def single(pieces):
        scores = masked_scores(pieces[0], pieces[1], allowed)
        peak_row = jnp.max(scores, -1, keepdims=True)
        log_total = peak_row + jnp.log(jnp.sum(jnp.exp(scores - peak_row), -1, keepdims=True))
        chance = jnp.exp(scores - log_total).astype(jnp.bfloat16)
        return (jnp.dot(chance, pieces[2], preferred_element_type=jnp.float32), log_total[:, 0])

    outputs, totals = lax.map(single, (query_heads, key_heads, value_heads))
    attended = join_heads(outputs).astype(jnp.bfloat16)
    middle = inputs + jnp.dot(attended, w_out, preferred_element_type=jnp.float32)
    normed_two = norm_rows(middle, gain_rows[1], shift_rows[1]).astype(jnp.bfloat16)
    hidden = jnp.dot(normed_two, w_up, preferred_element_type=jnp.float32)
    active = jax.nn.gelu(hidden, approximate=False).astype(jnp.bfloat16)
    result = middle + jnp.dot(active, w_down, preferred_element_type=jnp.float32)
    saved = (
        normed,
        query_heads,
        key_heads,
        value_heads,
        totals,
        attended,
        middle,
        normed_two,
        hidden,
        active,
    )
    return (result, saved)


def on_device(frames_in, prefix_len, w_qkv, w_out, w_up, w_down, gains, shifts, cotangent):
    inputs = frames_in[0].astype(jnp.float32)
    rows_here = inputs.shape[0]
    frames_all = rows_here * lax.axis_size("fsdp")
    first_row = lax.axis_index("fsdp") * rows_here
    places = first_row + jnp.arange(rows_here, dtype=jnp.int32)
    columns = jnp.arange(frames_all, dtype=jnp.int32)
    allowed = (columns[None, :] <= places[:, None]) | (columns[None, :] < prefix_len[0])
    weights = collect(w_qkv, w_out, w_up, w_down, gains, shifts)
    result, saved = forward(inputs, weights, allowed)
    weights = collect(w_qkv, w_out, w_up, w_down, gains, shifts)
    saved = forward(inputs, weights, allowed)[1]
    full_qkv, full_out, full_up, full_down, full_gains, full_shifts = weights
    (
        normed,
        query_heads,
        key_heads,
        value_heads,
        totals,
        attended,
        middle,
        normed_two,
        hidden,
        active,
    ) = saved
    gain_rows = full_gains.astype(jnp.float32)
    shift_rows = full_shifts.astype(jnp.float32)
    grad_top = cotangent[0].astype(jnp.float32)
    grad_branch = grad_top.astype(jnp.bfloat16)
    part_down = jnp.dot(active.T, grad_branch, preferred_element_type=jnp.float32)
    grad_active = jnp.dot(grad_branch, full_down.T, preferred_element_type=jnp.float32)
    gelu_pull = jax.vjp(functools.partial(jax.nn.gelu, approximate=False), hidden)[1]
    grad_hidden = gelu_pull(grad_active)[0].astype(jnp.bfloat16)
    part_up = jnp.dot(normed_two.T, grad_hidden, preferred_element_type=jnp.float32)
    grad_normed_two = jnp.dot(grad_hidden, full_up.T, preferred_element_type=jnp.float32)
    norm_pull_two = jax.vjp(norm_rows, middle, gain_rows[1], shift_rows[1])[1]
    back_middle, grad_gain_two, grad_shift_two = norm_pull_two(grad_normed_two)
    grad_middle = grad_top + back_middle
    grad_attn_out = grad_middle.astype(jnp.bfloat16)
    part_out = jnp.dot(attended.T, grad_attn_out, preferred_element_type=jnp.float32)
    grad_attended = jnp.dot(grad_attn_out, full_out.T, preferred_element_type=jnp.float32).astype(
        jnp.bfloat16
    )
    grad_att_heads = split_heads(grad_attended)

    def single_back(pieces):
        query_one, key_one, value_one, grad_one, log_total = pieces
        scores = masked_scores(query_one, key_one, allowed)
        chance = jnp.exp(scores - log_total[:, None])
        grad_chance = jnp.dot(grad_one, value_one.T, preferred_element_type=jnp.float32)
        inner = jnp.sum(chance * grad_chance, -1, keepdims=True)
        grad_scores = (chance * (grad_chance - inner)).astype(jnp.bfloat16)
        grad_query = jnp.dot(grad_scores, key_one, preferred_element_type=jnp.float32) * 0.125
        grad_key = (
            jnp.einsum("qk,qd->kd", grad_scores, query_one, preferred_element_type=jnp.float32)
            * 0.125
        )
        grad_value = jnp.einsum(
            "qk,qd->kd", chance.astype(jnp.bfloat16), grad_one, preferred_element_type=jnp.float32
        )
        return (grad_query, grad_key, grad_value)

    grad_q_heads, grad_k_heads, grad_v_heads = lax.map(
        single_back, (query_heads, key_heads, value_heads, grad_att_heads, totals)
    )
    grad_keys, grad_values = (
        lax.psum_scatter(
            join_heads(grad_k_heads).astype(jnp.bfloat16), "fsdp", scatter_dimension=0, tiled=True
        ).astype(jnp.float32),
        lax.psum_scatter(
            join_heads(grad_v_heads).astype(jnp.bfloat16), "fsdp", scatter_dimension=0, tiled=True
        ).astype(jnp.float32),
    )
    grad_mixed = jnp.concatenate([join_heads(grad_q_heads), grad_keys, grad_values], 1).astype(
        jnp.bfloat16
    )
    part_qkv = jnp.dot(normed.T, grad_mixed, preferred_element_type=jnp.float32)
    grad_normed = jnp.dot(grad_mixed, full_qkv.T, preferred_element_type=jnp.float32)
    norm_pull_one = jax.vjp(norm_rows, inputs, gain_rows[0], shift_rows[0])[1]
    back_inputs, grad_gain_one, grad_shift_one = norm_pull_one(grad_normed)
    grad_inputs = grad_middle + back_inputs
    part_gains = jnp.stack([grad_gain_one, grad_gain_two])
    part_shifts = jnp.stack([grad_shift_one, grad_shift_two])
    owned = (
        lax.psum_scatter(part_qkv, ("dp", "fsdp"), scatter_dimension=0, tiled=True),
        lax.psum_scatter(part_out, ("dp", "fsdp"), scatter_dimension=0, tiled=True),
        lax.psum_scatter(part_up, ("dp", "fsdp"), scatter_dimension=0, tiled=True),
        lax.psum_scatter(part_down, ("dp", "fsdp"), scatter_dimension=0, tiled=True),
        lax.psum_scatter(part_gains, ("dp", "fsdp"), scatter_dimension=1, tiled=True),
        lax.psum_scatter(part_shifts, ("dp", "fsdp"), scatter_dimension=1, tiled=True),
    )
    return (
        result.astype(jnp.bfloat16)[None],
        grad_inputs[None],
        owned[0],
        owned[1],
        owned[2],
        owned[3],
        owned[4],
        owned[5],
    )


def fast_device(ndp, frames_in, prefix_len, w_qkv, w_out, w_up, w_down, gains, shifts, cotangent):
    here = lax.axis_index("dp") * 2 + lax.axis_index("fsdp")
    width = gains.shape[1]
    per = PAIR // width
    rows = jnp.concatenate([gains, shifts, jnp.zeros((12, width), BF)], 0)
    tile = jnp.where(lax.broadcasted_iota(jnp.int32, (16, per, width), 1) == here % per, rows[:, None], 0.0)
    tile = tile.astype(BF).reshape(16, PAIR)
    pre = jnp.broadcast_to(prefix_len[None], (8, PAIR))
    result = layer(ndp // 4, frames_in[0], cotangent[0], pre, w_qkv, w_out, w_up, w_down, tile)
    frames_out, grad_in, *owned = settle(width, *result[:3], *result[8:])
    return (frames_out[None], grad_in[None]) + tuple(owned)


def solution(mesh):
    ndp, nf = mesh.shape["dp"], mesh.shape["fsdp"]
    both = P(("dp", "fsdp"), None)
    lanes = P(None, ("dp", "fsdp"))
    block = P("dp", "fsdp", None)
    body = functools.partial(fast_device, ndp) if (nf == 2 and ndp == 16) else on_device
    return jax.shard_map(
        body,
        mesh=mesh,
        in_specs=(block, P("dp"), both, both, both, both, lanes, lanes, block),
        out_specs=(block, block, both, both, both, both, lanes, lanes),
        check_vma=False,
    )
```

```python
import functools
import math

import jax
import jax.numpy as jnp
from jax import lax
from jax.experimental import pallas as pl
from jax.experimental.pallas import tpu as pltpu
from jax.sharding import PartitionSpec as P

H = 16
HD = 64
EPS = 1e-05
BF = jnp.bfloat16
F32 = jnp.float32
LOG2E = math.log2(math.e)
SCALE2 = 0.125 * LOG2E
PAIR = 2 * HD
TILE = 512
MESH = pl.DeviceIdType.MESH
DMA = pltpu.SemaphoreType.DMA
VMEM_LIMIT = 60 * 2**20


def coords():
    dp, f = lax.axis_index("dp"), lax.axis_index("fsdp")
    q = lax.div(dp, 2)
    return lax.div(q, 2), lax.rem(q, 2), lax.rem(dp, 2), f


def dev(z, y, c, f):
    return ((z * 2 + y) * 2 + c, f)


def remote(src, dst, send, recv, device):
    return pltpu.make_async_remote_copy(
        src_ref=src, dst_ref=dst, send_sem=send, recv_sem=recv, device_id=device, device_id_type=MESH
    )


def greet(peers):
    barrier = pltpu.get_barrier_semaphore()
    for peer in peers:
        pl.semaphore_signal(barrier, inc=1, device_id=peer, device_id_type=MESH)
    pl.semaphore_wait(barrier, len(peers))


def all_peers(nz, z, y, c, f):
    peers = [dev(lax.rem(z + k, nz), y, c, f) for k in range(1, nz)]
    return peers + [dev(z, 1 - y, c, f), dev(z, y, c, 1 - f), dev(z, y, 1 - c, f)]


def dot_nn(a, b):
    return lax.dot_general(a, b, (((1,), (0,)), ((), ())), preferred_element_type=F32)


def dot_nt(a, b):
    return lax.dot_general(a, b, (((1,), (1,)), ((), ())), preferred_element_type=F32)


def dot_tn(a, b):
    return lax.dot_general(a, b, (((0,), (0,)), ((), ())), preferred_element_type=F32)


def normalise(v):
    center = v - jnp.mean(v, -1, keepdims=True)
    scale = lax.rsqrt(jnp.mean(center * center, -1, keepdims=True) + EPS)
    return center * scale, scale


def lane_half():
    return lax.broadcasted_iota(jnp.int32, (1, PAIR), 1) // HD


def fill_bias(bias, prefix, c, transposed):
    rows = bias.shape[0]
    step = 64

    def body(j, part):
        a = lax.broadcasted_iota(jnp.int32, (step, rows), 0) + j * step
        b = lax.broadcasted_iota(jnp.int32, (step, rows), 1)
        row, key = (b, a) if transposed else (a, b)
        bias[part, :] = jnp.where((key <= row) | (key + c * rows < prefix), 0.0, -1e30)

    tiles(rows // step, step, body)


def norm_back(gh, n, scale, gain):
    gn = gh * gain
    return scale * (gn - jnp.mean(gn, -1, keepdims=True) - n * jnp.mean(gn * n, -1, keepdims=True))


class Gather:
    def __init__(self, nz, place, shards, outs, chunks, sems):
        self.nz, self.place, self.shards, self.outs, self.chunks = nz, place, shards, outs, chunks
        self.send, self.recv, self.own = sems

    @staticmethod
    def sem_shapes(n):
        return [DMA((n, 12)), DMA((n, 12)), DMA((n,))]

    def mine(self, i):
        w, r0, r, c0, n = self.chunks[i]
        return self.shards[w].at[pl.ds(r0, r), pl.ds(c0, n)]

    def at(self, i, *where):
        w, r0, r, c0, n = self.chunks[i]
        where += (slice(None),) * (4 - len(where))
        return self.outs[w].at[where + (pl.ds(r0, r), pl.ds(c0, n))]

    def hop(self, i, slot, src, dst, device):
        return remote(src, dst, self.send.at[i, slot], self.recv.at[i, slot], device)

    def copies(self, i):
        z, y, c, f = self.place
        nz = self.nz
        every = slice(None)
        core, xp, yp = dev(z, y, 1 - c, f), dev(z, y, c, 1 - f), dev(z, 1 - y, c, f)
        mine, home = self.mine(i), self.at(i, z, y, c, f)

        def same(slot, ref, device):
            return self.hop(i, slot, ref, ref, device)

        zs = [dev(lax.rem(z + k, nz), y, c, f) for k in range(1, nz)]
        line = self.at(i, every, y, c, f)
        other = self.at(i, every, 1 - y, c, f)
        zero = {
            0: [self.hop(i, k, mine, home, zs[k]) for k in range(nz - 1)],
            1: [same(3, line, yp), same(4, line, xp), same(8, line, core)],
            2: [same(5, other, xp), same(9, other, core)],
            3: [same(10, self.at(i, every, every, c, 1 - f), core)],
        }
        rows = self.at(i, z, y, c)
        plane = self.at(i, every, y, c)
        one = {
            0: [self.hop(i, 3, mine, home, xp)],
            1: [same(k, rows, zs[k]) for k in range(nz - 1)],
            2: [same(4, plane, yp), same(8, plane, core)],
            3: [same(9, self.at(i, every, 1 - y, c), core)],
        }
        return zero, one

    def arrivals(self, i):
        z, y, c, f = self.place
        nz = self.nz
        every = slice(None)
        zk = [lax.rem(z + nz - k, nz) for k in range(1, nz)]
        core = dev(z, y, 1 - c, f)

        def here(slot, *where):
            ref = self.at(i, *where)
            return self.hop(i, slot, ref, ref, core)

        zero = {
            1: [here(k, zk[k], y, c, f) for k in range(nz - 1)],
            2: [here(3, every, 1 - y, c, f)],
            3: [here(4, every, y, c, 1 - f), here(5, every, 1 - y, c, 1 - f)],
            4: [here(8, every, y, 1 - c), here(9, every, 1 - y, 1 - c)],
        }
        one = {
            1: [here(3, z, y, c, 1 - f)],
            2: [here(k, zk[k], y, c) for k in range(nz - 1)],
            3: [here(4, every, 1 - y, c)],
            4: [here(8, every, y, 1 - c, f), here(9, every, 1 - y, 1 - c, f), here(10, every, every, 1 - c, 1 - f)],
        }
        return zero, one

    def local(self, i):
        z, y, c, f = self.place
        return pltpu.make_async_copy(self.mine(i), self.at(i, z, y, c, f), self.own.at[i])

    def stage(self, i, s):
        if s == 1:
            self.local(i).wait()
        for core in range(2):

            @pl.when(self.place[2] == core)
            def _():
                if s:
                    for copy in self.arrivals(i)[core][s]:
                        copy.wait_recv()
                if s < 4:
                    for copy in self.copies(i)[core][s]:
                        copy.start()

    def tick(self, t, stages=(0, 1, 2, 3)):
        for s in stages:
            if 0 <= t - s < len(self.chunks):
                self.stage(t - s, s)

    def finish(self, i):
        for core in range(2):

            @pl.when(self.place[2] == core)
            def _():
                for copies in self.copies(i)[core].values():
                    for copy in copies:
                        copy.wait_send()


RING = 6
BLOCK = 32
WIDE = 1024


def tiles(count, size, body, hooks=None):
    @pl.loop(0, count)
    def _(j):
        body(j, pl.ds(pl.multiple_of(j * size, size), size))
        run_hooks(j, hooks)


def run_hooks(j, hooks):
    for at, hook in (hooks or {}).items():

        @pl.when(j == at)
        def _():
            hook()


def flat(ref, cols):
    v = ref[:, :, :, :, cols]
    return v.reshape(math.prod(v.shape[:-1]), v.shape[-1])


def add_blocks(dst, parts, out=None):
    lead, n = dst.shape[:-2], dst.shape[-1]
    size = min(n, 256)

    @pl.loop(0, math.prod(lead) * (n // size))
    def _(j):
        cols = pl.ds(pl.multiple_of(lax.rem(j, n // size) * size, size), size)
        at, rest = [], lax.div(j, n // size)
        for count in reversed(lead):
            at.insert(0, lax.rem(rest, count))
            rest = lax.div(rest, count)
        at = tuple(at) + (slice(None), cols)
        total = dst[at].astype(F32)
        for p in parts:
            total = total + p[at].astype(F32)
        if out is None:
            dst[at] = total.astype(dst.dtype)
        else:
            out[at] = total


class Scatter:
    def __init__(self, nz, place, sums, second, third, outs, sems):
        self.nz, self.place, self.sums, self.second, self.third = nz, place, sums, second, third
        self.outs, self.done = outs, set()
        self.send, self.recv, self.free = sems

    @staticmethod
    def sem_shapes(n):
        return [DMA((n, 5)), DMA((n, 5)), pltpu.SemaphoreType.REGULAR((RING,))]

    def peers(self):
        z, y, c, f = self.place
        zs = [dev(lax.rem(z + k, self.nz), y, c, f) for k in range(1, self.nz)]
        return zs, dev(z, 1 - y, c, f), dev(z, y, c, 1 - f)

    def hop(self, i, slot, src, dst, device):
        return remote(src, dst, self.send.at[i, slot], self.recv.at[i, slot], device)

    def copies(self, i):
        z, y, c, f = self.place
        s, b2, b3, nz = self.sums[i], self.second[i], self.third[i], self.nz
        zs, yp, xp = self.peers()
        zt = [lax.rem(z + k, nz) for k in range(1, nz)]
        zero = {
            0: [self.hop(i, 0, s.at[:, :, 1 - f], b2, xp)],
            1: [self.hop(i, 1, s.at[:, 1 - y, f], b3.at[pl.ds(0, nz)], yp)],
            2: [self.hop(i, 2 + k, s.at[zt[k], y, f], b3.at[nz + k], zs[k]) for k in range(nz - 1)],
        }
        one = {
            0: [self.hop(i, 0, s.at[:, 1 - y], b2, yp)],
            1: [self.hop(i, 1 + k, s.at[zt[k], y], b3.at[pl.ds(2 * k, 2)], zs[k]) for k in range(nz - 1)],
            2: [self.hop(i, nz, s.at[z, y, 1 - f], b3.at[2 * (nz - 1)], xp)],
        }
        return zero, one

    def stage(self, i, st):
        z, y, c, f = self.place
        nz = self.nz
        self.done.add((i, st))
        s, b2, b3 = self.sums[i], self.second[i], self.third[i]
        copies = self.copies(i)
        zs, yp, xp = self.peers()
        ringed = i < len(self.sums) - 1
        if st == 0 and ringed and i >= RING:
            pl.semaphore_wait(self.free.at[i % RING], nz + 1)

        @pl.when(c == 0)
        def _():
            if st:
                for copy in copies[0][st - 1]:
                    copy.wait_recv()
            if st == 0:
                copies[0][0][0].start()
            if st == 1:
                add_blocks(s.at[:, 1 - y, f], [b2.at[:, 1 - y]])
                copies[0][1][0].start()
                add_blocks(s.at[:, y, f], [b2.at[:, y]])
            if st == 2:
                for k in range(nz - 1):
                    zt = lax.rem(z + k + 1, nz)
                    add_blocks(s.at[zt, y, f], [b3.at[zt]])
                    copies[0][2][k].start()
                add_blocks(s.at[z, y, f], [b3.at[z]])
            if st == 3:
                add_blocks(s.at[z, y, f], [b3.at[nz + k] for k in range(nz - 1)], self.outs[i])

        @pl.when(c == 1)
        def _():
            if st:
                for copy in copies[1][st - 1]:
                    copy.wait_recv()
            if st == 0:
                copies[1][0][0].start()
            if st == 1:
                for k in range(nz - 1):
                    zt = lax.rem(z + k + 1, nz)
                    add_blocks(s.at[zt, y], [b2.at[zt]])
                    copies[1][1][k].start()
                add_blocks(s.at[z, y], [b2.at[z]])
            if st == 2:
                add_blocks(s.at[z, y, 1 - f], [b3.at[2 * k + 1 - f] for k in range(nz - 1)])
                copies[1][2][0].start()
                add_blocks(s.at[z, y, f], [b3.at[2 * k + f] for k in range(nz - 1)])
            if st == 3:
                add_blocks(s.at[z, y, f], [b3.at[2 * (nz - 1)]], self.outs[i])

        if st == 3 and ringed and i + RING < len(self.sums) - 1:
            for peer in zs + [yp, xp]:
                pl.semaphore_signal(self.free.at[i % RING], inc=1, device_id=peer, device_id_type=MESH)

    def tick(self, t):
        for st in range(1, 4):
            i = t - st
            if (i, st - 1) in self.done and (i, st) not in self.done:
                self.stage(i, st)

    def finish(self, i):
        for core in range(2):

            @pl.when(self.place[2] == core)
            def _():
                for copies in self.copies(i)[core].values():
                    for copy in copies:
                        copy.wait_send()


class Producer:
    def __init__(self, place, buf, land, sems):
        self.place, self.buf, self.land = place, buf, land
        self.send, self.recv, self.credit = sems
        z, y, c, f = place
        self.core = dev(z, y, 1 - c, f)
        self.made, self.pending = 0, None

    def copy(self, slot):
        theirs = self.buf.at[slot, :, 1 - self.place[2]]
        return remote(theirs, self.land.at[slot], self.send.at[slot], self.recv.at[slot], self.core)

    def before(self, slot):
        self.copy(slot).wait_send()
        pl.semaphore_wait(self.credit.at[slot], 1)

    def absorb(self, j, target):
        c = self.place[2]
        slot = lax.rem(j, 2)
        self.copy(slot).wait_recv()
        for i in range(4):
            ref = target(j, i)
            for k in range(2):
                ref[k] = (self.buf[slot, i, c, k].astype(F32) + self.land[slot, i, k].astype(F32)).astype(BF)
        pl.semaphore_signal(self.credit.at[slot], inc=1, device_id=self.core, device_id_type=MESH)

    def flush(self):
        if self.pending is not None:
            self.absorb(*self.pending)
            self.pending = None

    def run(self, count, product, where, target, hooks=None):
        fresh, pending = self.made == 0, self.pending

        @pl.loop(0, count)
        def _(j):
            slot = lax.rem(j, 2)
            if not fresh:
                self.before(slot)
            elif count > 2:

                @pl.when(j >= 2)
                def _():
                    self.before(slot)

            v = product(j)
            for i in range(4):
                for k in range(2):
                    for core in range(2):
                        at = where(i, core, k)
                        self.buf[slot, i, core, k] = v[at : at + BLOCK].astype(BF)
            self.copy(slot).start()
            if pending is not None:

                @pl.when(j == 0)
                def _():
                    self.absorb(*pending)

            @pl.when(j >= 1)
            def _():
                self.absorb(j - 1, target)

            run_hooks(j, hooks)

        self.made += count
        self.pending = (count - 1, target)

    def finish(self):
        for slot in range(2):
            self.before(slot)


def row_blocks(i, core, k):
    return BLOCK * (4 * i + 2 * core + k)


def deep_blocks(i, core, k):
    return BLOCK * (8 * core + 4 * k + i)


def attend_forward(c, qkv, cross, bias, att, lse, hooks):
    rows, d = att.shape
    half = lane_half()
    lane = lax.broadcasted_iota(jnp.int32, (1, PAIR), 1)
    rt = rows // 2

    def one(q, blocks):
        scores = []
        for keys, _, extra in blocks:
            s = dot_nt(q, keys) * SCALE2
            scores.append(s if extra is None else s + extra)
        peak = functools.reduce(jnp.maximum, [jnp.max(s, -1, keepdims=True) for s in scores])
        total = None
        for s, (_, values, _) in zip(scores, blocks):
            part = dot_nn(jnp.exp2(s - peak).astype(BF), values)
            total = part if total is None else total + part
        return total, peak

    def pair(p, second):
        cols = pl.ds(pl.multiple_of(p * PAIR, PAIR), PAIR)
        kcols = pl.ds(pl.multiple_of(d + p * PAIR, PAIR), PAIR)
        vcols = pl.ds(pl.multiple_of(2 * d + p * PAIR, PAIR), PAIR)
        def half_rows(r, part):
            results = []
            for h in range(2):
                mine = half == h
                q = jnp.where(mine, qkv[part, cols], 0.0).astype(BF)

                def val(v):
                    return jnp.where(mine, v, 1.0).astype(BF)

                if second:
                    blocks = [(cross[:, cols], val(cross[:, kcols]), None)]
                    if r > 0:
                        blocks.append((qkv[pl.ds(0, rt), kcols], val(qkv[pl.ds(0, rt), vcols]), None))
                    blocks.append((qkv[part, kcols], val(qkv[part, vcols]), bias[part, pl.ds(r * rt, rt)]))
                else:
                    blocks = [(qkv[:, kcols], val(qkv[:, vcols]), bias[part, :])]
                total, peak = one(q, blocks)
                sums = pltpu.roll(total, HD, axis=1)
                results.append(total / sums)
                both = jnp.where(mine, sums, total)
                lse[part, :] = jnp.where(lane == 2 * p + h, peak + jnp.log2(both), lse[part, :])
            att[part, cols] = jnp.where(half == 0, results[0], results[1]).astype(BF)

        if second:
            for r in range(2):
                half_rows(r, pl.ds(r * rt, rt))
        else:
            tiles(2, rt, half_rows)

    @pl.loop(0, d // PAIR)
    def _(p):
        for second in range(2):

            @pl.when(c == second)
            def _():
                pair(p, second == 1)

        run_hooks(p, hooks)


SHARED = 5


def attend_backward(c, qkv, cross, biast, lset, deltat, far_lse, far_delta, go, gq, gq2, more, hooks):
    rows, d = go.shape
    half = lane_half()
    rt = rows // 2
    pairs = d // PAIR

    def term(p, keys, values, krows, qrows, queries, grads, lse, delta, masked, total):
        gk = gv = None
        for h in range(2):
            mine = half == h
            q = jnp.where(mine, queries, 0.0).astype(BF)
            g = jnp.where(mine, grads, 0.0).astype(BF)
            km = jnp.where(mine, keys, 0.0).astype(BF)
            s = dot_nt(keys, q) * SCALE2
            if masked:
                s = s + biast[krows, qrows]
            pr = jnp.exp2(s - lse[pl.ds(2 * p + h, 1), qrows])
            gs = (pr * (dot_nt(values, g) - delta[pl.ds(2 * p + h, 1), qrows])).astype(BF)
            k1, v1 = dot_nn(gs, q), dot_nn(pr.astype(BF), g)
            gk, gv = (k1, v1) if gk is None else (gk + k1, gv + v1)
            total[qrows, :] = total[qrows, :] + dot_tn(gs, km)
        return gk, gv

    every = pl.ds(0, rows)
    first, last = pl.ds(0, PAIR), pl.ds(PAIR, PAIR)

    @pl.loop(0, pairs)
    def _(i):
        @pl.when(c == 0)
        def _():
            heavy = i < pairs - SHARED
            p = lax.rem(i + SHARED, pairs)
            cols = pl.ds(pl.multiple_of(p * PAIR, PAIR), PAIR)
            kcols = pl.ds(pl.multiple_of(d + p * PAIR, PAIR), PAIR)
            vcols = pl.ds(pl.multiple_of(2 * d + p * PAIR, PAIR), PAIR)
            gq[...] = jnp.zeros_like(gq)

            @pl.when(heavy)
            def _():
                gq2[...] = jnp.zeros_like(gq2)

                def far_part(r, krows):
                    more[krows, first], more[krows, last] = term(
                        p, qkv[krows, kcols], qkv[krows, vcols], krows, every, cross[:, cols], cross[:, kcols], far_lse, far_delta, False, gq2
                    )

                tiles(2, rt, far_part)
                cross[:, cols] = (gq2[...] * 0.125).astype(BF)

            @pl.when(i == pairs - SHARED)
            def _():
                more[:, first] = jnp.zeros_like(gq)
                more[:, last] = jnp.zeros_like(gq)

            def own_part(r, krows):
                gk, gv = term(
                    p, qkv[krows, kcols], qkv[krows, vcols], krows, every, qkv[:, cols], go[:, cols], lset, deltat, True, gq
                )
                qkv[krows, kcols] = ((gk + more[krows, first]) * 0.125).astype(BF)
                qkv[krows, vcols] = (gv + more[krows, last]).astype(BF)

            tiles(2, rt, own_part)
            qkv[:, cols] = (gq[...] * 0.125).astype(BF)

        @pl.when(c == 1)
        def _():
            p = i
            cols = pl.ds(pl.multiple_of(p * PAIR, PAIR), PAIR)
            kcols = pl.ds(pl.multiple_of(d + p * PAIR, PAIR), PAIR)
            vcols = pl.ds(pl.multiple_of(2 * d + p * PAIR, PAIR), PAIR)
            gq[...] = jnp.zeros_like(gq)

            @pl.when(p < SHARED)
            def _():
                def near_part(r, krows):
                    gk, gv = term(
                        p, cross[krows, cols], cross[krows, kcols], krows, every, qkv[:, cols], go[:, cols], lset, deltat, False, gq
                    )
                    cross[krows, cols] = (gk * 0.125).astype(BF)
                    cross[krows, kcols] = gv.astype(BF)

                tiles(2, rt, near_part)

            for r in range(2):
                krows, qrows = pl.ds(r * rt, rt), pl.ds(r * rt, rows - r * rt)
                gk, gv = term(
                    p, qkv[krows, kcols], qkv[krows, vcols], krows, qrows, qkv[qrows, cols], go[qrows, cols], lset, deltat, True, gq
                )
                qkv[krows, kcols] = (gk * 0.125).astype(BF)
                qkv[krows, vcols] = gv.astype(BF)
            qkv[:, cols] = (gq[...] * 0.125).astype(BF)

        run_hooks(i, hooks)


def layer_kernel(nz, *refs):
    (
        frames_in, cot_in, pre_in, s_qkv, s_out, s_up, s_down, s_par,
        fo, gi, gl, f_qkv, f_out, f_up, f_down, f_par, g_qkv, g_out, g_up, g_down, g_par,
        x, cot, pre, h1, qkv, cross, att, x1, h2, a, gp, wa, wb, gh, gz, go, bias, narrow, narrow2, lset, deltat, far_lse, far_delta,
        acc, par, parv, ht, buf, land, sdown, spar, ptheirs, pland, second, third, psecond, pthird,
        ag_send, ag_recv, ag_own, rs_send, rs_recv, rs_free, p_send, p_recv, p_credit,
        load_sem, swap_sem, io_sem, io_recv,
    ) = refs
    place = z, y, c, f = coords()
    rows, d = x.shape
    ff = a.shape[-1]
    core, far = dev(z, y, 1 - c, f), dev(z, y, 1 - c, 1 - f)
    straight = c == f
    nk = d // WIDE

    chunks = [(4, 0, 16, 0, PAIR)]
    chunks += [(0, 0, BLOCK, d + h * TILE, TILE) for h in range(2)] + [(0, 0, BLOCK, b * d, d) for b in (2, 0)]
    chunks += [(1, 0, BLOCK, 0, d)]
    chunks += [(2, 0, BLOCK, k * WIDE, WIDE) for k in range(ff // WIDE)]
    down_cols = [(0, 256), (256, 256), (512, 256), (768, 128), (896, 128)]
    chunks += [(3, 0, 4 * BLOCK, c0, w) for c0, w in down_cols]
    ag = Gather(nz, place, (s_qkv, s_out, s_up, s_down, s_par), (f_qkv, f_out, f_up, f_down, f_par), chunks, (ag_send, ag_recv, ag_own))

    ups, downs = ff // WIDE, 4
    sums = [sdown.at[k] for k in range(downs)]
    sums += [a.at[:, :, :, :, pl.ds(k * WIDE, WIDE)] for k in range(ups)]
    tail = [(3 * d, d), (d, d), (2 * d, d), (0, TILE), (TILE, TILE)]
    sums += [gp.at[:, :, :, :, pl.ds(c0, w)] for c0, w in tail]
    goes = [g_down.at[pl.ds(k * BLOCK, BLOCK)] for k in range(downs)]
    goes += [g_up.at[:, pl.ds(k * WIDE, WIDE)] for k in range(ups)]
    goes += [g_out] + [g_qkv.at[:, pl.ds(c0, w)] for c0, w in tail[1:]]
    n = len(sums)
    widths = [WIDE] * (downs + ups) + [w for _, w in tail]
    rs = Scatter(
        nz, place, sums + [spar], [second.at[i % RING, :, :, :, pl.ds(0, widths[i])] for i in range(n)] + [psecond],
        [third.at[i % RING, :, :, pl.ds(0, widths[i])] for i in range(n)] + [pthird], goes + [g_par], (rs_send, rs_recv, rs_free),
    )
    maker = Producer(place, buf, land, (p_send, p_recv, p_credit))

    for i in range(len(chunks)):
        ag.local(i).start()
    greet(all_peers(nz, *place) + [far])

    swaps = []
    quarter = rows // 4
    quarters = [pl.ds(i * quarter, quarter) for i in range(4)]
    moves = [(pre_in, pre)]
    moves += [(cot_in.at[q], cot.at[q]) for q in quarters] + [(frames_in.at[q], x.at[q]) for q in quarters]
    for i, (src, dst) in enumerate(moves):
        swaps.append((pltpu.make_async_copy(src, dst, swap_sem.at[i, 0]), remote(src, dst, swap_sem.at[i, 1], swap_sem.at[i, 2], far)))

    def swap_start(i):
        @pl.when(straight)
        def _():
            swaps[i][0].start()

        @pl.when(jnp.logical_not(straight))
        def _():
            swaps[i][1].start()

    def swap_wait(i):
        @pl.when(straight)
        def _():
            swaps[i][0].wait()

        @pl.when(jnp.logical_not(straight))
        def _():
            swaps[i][1].wait()

    def between(i, src, dst):
        return remote(src, dst, swap_sem.at[i, 1], swap_sem.at[i, 2], core)

    def ag_tick(t):
        return lambda: ag.tick(t)

    def rs_tick(t):
        return lambda: rs.tick(t)

    def rs_begin(i):
        return lambda: rs.stage(i, 0)

    def small(b):
        return pl.ds(b * BLOCK, BLOCK)

    def load(i, src, dst):
        return pltpu.make_async_copy(src, dst, load_sem.at[i])

    def load_block(i, b):
        if b == 3:
            return load(i, f_out, wa.at[:, :, :, :, small(3)])
        return load(i, f_qkv.at[:, :, :, :, :, pl.ds(b * d, d)], wa.at[:, :, :, :, small(b)])

    def block(b, at=slice(None)):
        v = wa[at, :, :, :, small(b)]
        return v.reshape(math.prod(v.shape[:-1]), d)

    ag.stage(0, 0)
    ag.stage(1, 0)
    swap_start(0)
    swap_start(5)
    ag.stage(0, 1)
    ag.tick(2)
    swap_start(6)
    ag.tick(3)
    swap_start(7)
    ag.stage(0, 4)
    get_par = load(0, f_par, parv)
    get_par.start()
    swap_wait(0)
    fill_bias(bias, pre[0:1, 0:1], c, False)
    get_par.wait()
    for t in range(d // PAIR):
        total = None
        for k in range(4):
            piece = parv[t // 2, t % 2, k // 2, k % 2].astype(F32)
            total = piece if total is None else total + piece
        par[:, pl.ds(t * PAIR, PAIR)] = total
    step = 64

    def norm_one(j, part):
        nrm, _ = normalise(x[part, :].astype(F32))
        h1[part, :] = (nrm * par[0:1, :] + par[2:3, :]).astype(BF)

    ag.tick(4)
    swap_start(8)
    for i in range(4):
        swap_wait(5 + i)
    tiles(rows // step, step, norm_one)
    keyvals = between(14, qkv.at[:, pl.ds(d, 2 * d)], cross)
    ag.stage(1, 4)
    for i, b in enumerate((1, 2, 0)):
        ag.tick(5 + i)
        ag.stage(2 + i, 4)
        get = load_block(1 + i, b)
        get.start()
        get.wait()
        for t in range(d // TILE):
            cols = pl.ds(t * TILE, TILE)
            w = wa[:, :, :, :, small(b), cols].reshape(d, TILE)
            qkv[:, pl.ds(b * d + t * TILE, TILE)] = dot_nn(h1[...], w).astype(BF)
        swap_start(1 + i)
        if b == 2:

            @pl.when(c == 0)
            def _():
                keyvals.start()

    @pl.when(c == 1)
    def _():
        keyvals.wait_recv()

    swap_start(4)
    narrow[...] = jnp.zeros_like(narrow)
    attend_forward(c, qkv, cross, bias, att, narrow, {0: ag_tick(8), 5: ag_tick(9)})
    ag.stage(5, 4)
    get_out = load_block(4, 3)
    get_out.start()

    @pl.when(c == 0)
    def _():
        keyvals.wait_send()

    lset[...] = narrow[...].T[:H, :]

    def get_up(k):
        return load(5 + k, f_up.at[:, :, :, :, :, pl.ds(k * WIDE, WIDE)], wb.at[:, :, :, :, :, pl.ds(k * WIDE, WIDE)])

    ag.stage(6, 4)
    get_up(0).start()
    get_out.wait()
    for t in range(d // TILE):
        cols = pl.ds(t * TILE, TILE)
        w = wa[:, :, :, :, small(3), cols].reshape(d, TILE)
        x1[:, cols] = x[:, cols].astype(F32) + dot_nn(att[...], w)
    ag.tick(10)

    def norm_two(j, part):
        nrm, _ = normalise(x1[part, :])
        h2[part, :] = (nrm * par[1:2, :] + par[3:4, :]).astype(BF)

    tiles(rows // step, step, norm_two)
    u = gh.at[:, pl.ds(0, TILE)]

    def up(cols):
        gh[:, pl.ds(0, TILE)] = dot_nn(h2[...], wb[:, :, :, :, :, cols].reshape(d, TILE))

        @pl.loop(0, rows // BLOCK)
        def _(j):
            at = (lax.div(j, 4), lax.rem(lax.div(j, 2), 2), lax.rem(j, 2), slice(None), cols)
            v = gh[pl.ds(pl.multiple_of(j * BLOCK, BLOCK), BLOCK), pl.ds(0, TILE)]
            phi = 0.5 * (1.0 + lax.erf(v * math.sqrt(0.5)))
            dens = jnp.exp2(v * v * (-0.5 * LOG2E)) * (1.0 / math.sqrt(2.0 * math.pi))
            a[at] = (v * phi).astype(BF)
            gp[at] = (phi + v * dens).astype(BF)

    for i in range(4):
        swap_wait(1 + i)

    def down_product(j):
        for k in range(ups):

            @pl.when(j == 2 * k)
            def _():
                if k:
                    ag.stage(6 + k, 4)
                    get_up(k).start()
                get_up(k).wait()

        cols = pl.ds(pl.multiple_of(j * TILE, TILE), TILE)
        up(cols)
        for k in range(ups):

            @pl.when(j == 2 * k)
            def _():
                ag.tick(11 + k, (0, 1))

            @pl.when(j == 2 * k + 1)
            def _():
                ag.tick(11 + k, (2, 3))

        return dot_tn(flat(a, cols), cot[...])

    maker.run(2 * ups, down_product, deep_blocks, lambda j, i: sdown.at[i, lax.div(j, 2), lax.rem(j, 2)])

    def get_down(k):
        part = pl.ds(*down_cols[k])
        return load(9 + k, f_down.at[:, :, :, :, :, part], wa.at[:, :, :, :, :, part])

    def down(k):
        cols = pl.ds(k * TILE, TILE)
        w = wa[:, :, :, :, :, cols].reshape(ff, TILE)
        go[:, cols] = (x1[:, cols] + dot_nn(flat(a, slice(None)), w)).astype(BF)

    ag.tick(15)
    maker.flush()
    for k in range(2):
        ag.stage(10 + k, 4)
        get_down(k).start()
    ag.tick(16)
    ag.tick(17)
    rs.stage(0, 0)
    for k in range(2):
        get_down(k).wait()
    down(0)
    for k in range(2, len(down_cols)):
        ag.stage(10 + k, 4)
        get_down(k).start()
    for k in range(2, len(down_cols)):
        get_down(k).wait()
    rs.stage(1, 0)
    down(1)
    rs.stage(2, 0)
    outs = []
    for q in quarters:
        outs.append(
            (
                pltpu.make_async_copy(go.at[q], fo.at[q], io_sem.at[len(outs)]),
                remote(go.at[q], fo.at[q], io_sem.at[len(outs)], io_recv.at[len(outs)], far),
            )
        )

    def either(pair, act_on):
        @pl.when(straight)
        def _():
            act_on(pair[0])

        @pl.when(jnp.logical_not(straight))
        def _():
            act_on(pair[1])

    def begin(pair):
        either(pair, lambda copy: copy.start())

    def end(pair):
        either(pair, lambda copy: copy.wait())

    begin(outs[0])
    def act(j, cols):
        w = wa[lax.div(j, 2), lax.rem(j, 2)].reshape(TILE, d)
        v = dot_nt(cot[...], w) * flat(gp, cols).astype(F32)
        gp[:, :, :, :, cols] = v.astype(BF).reshape(a.shape[:-1] + (TILE,))

    rs.stage(3, 0)
    tiles(8, TILE, act, {5: rs_tick(1)})
    begin(outs[1])
    for i, b in enumerate((3, 0, 1, 2)):
        load_block(14 + i, b).start()
    ht[...] = h2[...].T
    for i in range(2):
        gh[:, pl.ds(i * TILE, TILE)] = dot_nt(flat(gp, slice(None)), wb[2 * i : 2 * i + 2].reshape(TILE, ff))
        if i == 0:
            rs.tick(2)
    begin(outs[2])
    acc[...] = jnp.zeros_like(acc)
    step = 32

    def collect(row, v):
        part = v.reshape(step // 8, 8, d)
        acc[row] = acc[row] + functools.reduce(jnp.add, [part[i] for i in range(step // 8)])

    def back_two(j, part):
        nrm, scale = normalise(x1[part, :])
        g = gh[part, :]
        collect(1, g * nrm)
        collect(3, g)
        total = cot[part, :].astype(F32) + norm_back(g, nrm, scale, par[1:2, :])
        x1[part, :] = total
        gz[part, :] = total.astype(BF)

    tiles(rows // step, step, back_two)

    def row_half(j):
        return ht[pl.ds(pl.multiple_of(lax.rem(j, 2) * TILE, TILE), TILE), :]

    def wide(j):
        return pl.ds(pl.multiple_of(lax.div(j, 2) * WIDE, WIDE), WIDE)

    def up_product(j):
        return dot_nn(row_half(j), flat(gp, wide(j)))

    def target(ref, first):
        def of(j, i):
            cols = pl.ds(pl.multiple_of(first + lax.div(j, 2) * WIDE, WIDE), WIDE)
            return ref.at[2 * lax.rem(j, 2) + i // 2, i % 2, :, :, cols]

        return of

    rs.tick(3)
    begin(outs[3])
    maker.run(
        2 * ups, up_product, row_blocks, target(a, 0), {2: rs_begin(4), 3: rs_tick(4), 4: rs_begin(5), 6: rs_begin(6)}
    )
    maker.flush()
    rs.stage(7, 0)
    for pair in outs:
        end(pair)
    load_block(14, 3).wait()
    for i in range(2):
        go[:, pl.ds(i * TILE, TILE)] = dot_nt(gz[...], block(3, pl.ds(2 * i, 2))).astype(BF)
    pick = (
        lax.broadcasted_iota(jnp.int32, (H, d), 1) // HD == lax.broadcasted_iota(jnp.int32, (H, d), 0)
    ).astype(BF)
    for i in range(4):
        part = pl.ds(i * quarter, quarter)
        prod = go[part, :].astype(F32) * att[part, :].astype(F32)
        high = prod.astype(BF)
        low = (prod - high.astype(F32)).astype(BF)
        deltat[:, part] = dot_nt(pick, high) + dot_nt(pick, low)
    low_cols, high_cols = pl.ds(0, SHARED * PAIR), pl.ds(SHARED * PAIR, d - SHARED * PAIR)
    high_cols2 = pl.ds(d + SHARED * PAIR, d - SHARED * PAIR)
    low_cols2 = pl.ds(d, SHARED * PAIR)

    lends = [
        between(9, qkv.at[:, high_cols], cross.at[:, high_cols]),
        between(15, go.at[:, high_cols], cross.at[:, high_cols2]),
        between(16, lset, far_lse),
        between(10, deltat, far_delta),
    ]
    gives = [
        between(11, cross.at[:, low_cols], cross.at[:, low_cols]),
        between(12, cross.at[:, low_cols2], cross.at[:, low_cols2]),
    ]
    returns = between(13, cross.at[:, high_cols], cross.at[:, high_cols])

    @pl.when(c == 1)
    def _():
        for copy in lends:
            copy.start()

    rs.tick(5)
    ht[...] = att[...].T
    maker.run(2, lambda j: dot_nn(row_half(j), gz[...]), row_blocks, target(gp, 3 * d))
    fill_bias(bias, pre[0:1, 0:1], c, True)

    @pl.when(c == 0)
    def _():
        for copy in lends:
            copy.wait_recv()

    @pl.when(c == 1)
    def _():
        for copy in lends:
            copy.wait_send()

    def give_back():
        @pl.when(c == 1)
        def _():
            for copy in gives:
                copy.start()

    def return_queries():
        @pl.when(c == 0)
        def _():
            returns.start()

    def flush_tick():
        maker.flush()
        rs.stage(8, 0)
        rs.tick(6)

    hooks = {0: flush_tick, 2: return_queries, 3: rs_tick(7), 4: give_back, 6: rs_tick(8)}
    attend_backward(c, qkv, cross, bias, lset, deltat, far_lse, far_delta, go, narrow, narrow2, gh, hooks)
    ht[...] = h1[...].T

    @pl.when(c == 1)
    def _():
        for copy in gives:
            copy.wait_send()
        returns.wait_recv()

        def add(j, part):
            qkv[part, high_cols] = (qkv[part, high_cols].astype(F32) + cross[part, high_cols].astype(F32)).astype(BF)

        tiles(rows // step, step, add)

    @pl.when(c == 0)
    def _():
        returns.wait_send()
        for copy in gives:
            copy.wait_recv()

        def add(j, part):
            for base in (0, d):
                to, src = pl.ds(d + base, SHARED * PAIR), pl.ds(base, SHARED * PAIR)
                qkv[part, to] = (qkv[part, to].astype(F32) + cross[part, src].astype(F32)).astype(BF)

        tiles(rows // step, step, add)

    def mixed_cols(j):
        return pl.ds(pl.multiple_of(lax.rem(lax.div(j, 2) + 1, 3) * d, d), d)

    def mixed_target(j, i):
        return gp.at[2 * lax.rem(j, 2) + i // 2, i % 2, :, :, mixed_cols(j)]

    maker.run(
        6, lambda j: dot_nn(row_half(j), qkv[:, mixed_cols(j)]), row_blocks, mixed_target, {1: rs_tick(9), 2: rs_begin(9), 4: rs_begin(10)}
    )
    maker.flush()
    rs.stage(11, 0)
    rs.stage(12, 0)
    rs.tick(10)
    for i, b in enumerate((0, 1, 2)):
        load_block(15 + i, b).wait()
    for i in range(2):
        total = None
        for b in range(3):
            part = dot_nt(qkv[:, pl.ds(b * d, d)], block(b, pl.ds(2 * i, 2)))
            total = part if total is None else total + part
        gh[:, pl.ds(i * TILE, TILE)] = total
        if i == 1:
            rs.tick(11)

    def back_one(j, part):
        nrm, scale = normalise(x[part, :].astype(F32))
        g = gh[part, :]
        collect(0, g * nrm)
        collect(2, g)
        total = x1[part, :] + norm_back(g, nrm, scale, par[0:1, :])
        gh[part, :] = total
        gz[part, :] = total.astype(BF)

    tiles(rows // step, step, back_one)
    backs = []
    for i, q in enumerate(quarters):
        backs.append(
            (
                pltpu.make_async_copy(gh.at[q], gi.at[q], io_sem.at[4 + i]),
                remote(gz.at[q], gl.at[q], io_sem.at[4 + i], io_recv.at[4 + i], far),
            )
        )
    begin(backs[0])
    for i in range(4):
        par[i : i + 1, :] = jnp.sum(acc[i], 0, keepdims=True)
    for t in range(d // PAIR):
        row = par[:, pl.ds(t * PAIR, PAIR)].astype(BF)
        for k in range(2):
            spar[t // 2, t % 2, k] = row
            ptheirs[t // 2, t % 2, k] = row
    pars = remote(ptheirs, pland, io_sem.at[8], io_recv.at[8], core)
    pars.start()
    rs.stage(11, 1)
    pars.wait_recv()
    add_blocks(spar, [pland])
    rs.stage(n, 0)
    begin(backs[1])
    for i, st in ((12, 1), (10, 2), (9, 3)):
        rs.stage(i, st)
    begin(backs[2])
    for i, st in ((n, 1), (11, 2), (12, 2)):
        rs.stage(i, st)
    begin(backs[3])
    for i, st in ((10, 3), (n, 2), (11, 3), (12, 3), (n, 3)):
        rs.stage(i, st)
    for pair in backs:
        end(pair)
    pars.wait_send()
    for i in range(len(chunks)):
        ag.finish(i)
    for i in range(n + 1):
        rs.finish(i)
    maker.finish()


def layer(nz, frames_in, cot, pre, w_qkv, w_out, w_up, w_down, tile):
    rows, d = frames_in.shape
    ff = w_up.shape[1]
    S = jax.ShapeDtypeStruct
    V = pltpu.VMEM
    REG = pltpu.SemaphoreType.REGULAR
    hbm, vm = pl.BlockSpec(memory_space=pl.ANY), pl.BlockSpec(memory_space=V)
    shards = (w_qkv, w_out, w_up, w_down, tile)
    parts = (nz, 2, 2, BLOCK)
    full = (nz, 2, 2, 2)
    return pl.pallas_call(
        functools.partial(layer_kernel, nz),
        out_shape=[S((rows, d), BF), S((rows, d), F32), S((rows, d), BF)]
        + [S(full + w.shape, BF) for w in shards]
        + [S(w.shape, F32) for w in shards],
        in_specs=[hbm] * 8,
        out_specs=[hbm] * 8 + [vm] * 5,
        scratch_shapes=[
            V((rows, d), BF), V((rows, d), BF), V((8, PAIR), jnp.int32), V((rows, d), BF), V((rows, 3 * d), BF),
            V((rows, 2 * d), BF), V((rows, d), BF), V((rows, d), F32), V((rows, d), BF),
            V(parts + (ff,), BF), V(parts + (ff,), BF),
            V(full + w_down.shape, BF), V(full + w_up.shape, BF),
            V((rows, d), F32), V((rows, d), BF), V((rows, d), BF), V((rows, rows), F32), V((rows, PAIR), F32), V((rows, PAIR), F32),
            V((H, rows), F32), V((H, rows), F32), V((H, rows), F32), V((H, rows), F32), V((4, 8, d), F32), V((16, d), F32), V(full + (16, PAIR), BF),
            V((d, rows), BF), V((2, 4, 2, 2, BLOCK, WIDE), BF), V((2, 4, 2, BLOCK, WIDE), BF),
            V((4,) + parts + (d,), BF), V((nz, 2, 2, 16, PAIR), BF), V((nz, 2, 2, 16, PAIR), BF), V((nz, 2, 2, 16, PAIR), BF),
            V((RING, nz, 2, BLOCK, WIDE), BF), V((RING, 7, BLOCK, WIDE), BF), V((nz, 2, 16, PAIR), BF), V((7, 16, PAIR), BF),
        ]
        + Gather.sem_shapes(15)
        + Scatter.sem_shapes(14)
        + [DMA((2,)), DMA((2,)), REG((2,)), DMA((18,)), DMA((17, 3)), DMA((9,)), DMA((9,))],
        compiler_params=pltpu.CompilerParams(collective_id=0, has_side_effects=True, vmem_limit_bytes=63 * 2**20),
    )(frames_in, cot, pre, *shards)


def settle_kernel(fo, gi, gl, g_qkv, g_out, g_up, g_down, g_par, fo_, gi_, qkv_, out_, up_, down_, gains_, shifts_, narrow, wide, *rest):
    straight = lax.rem(lax.axis_index("dp"), 2) == lax.axis_index("fsdp")
    stops, sems = rest[:5], rest[5]
    pairs = ((fo, fo_), (g_qkv, qkv_), (g_out, out_), (g_up, up_), (g_down, down_))
    ins = [pltpu.make_async_copy(src, stop, sems.at[0, i]) for i, ((src, _), stop) in enumerate(zip(pairs, stops))]
    outs = [pltpu.make_async_copy(stop, dst, sems.at[1, i]) for i, ((_, dst), stop) in enumerate(zip(pairs, stops))]
    rows = gi.shape[0] // 4
    parts = [pl.ds(i * rows, rows) for i in range(4)]
    own = [pltpu.make_async_copy(gi.at[p], wide.at[p], sems.at[2, i]) for i, p in enumerate(parts)]
    came = [pltpu.make_async_copy(gl.at[p], narrow.at[p], sems.at[2, i]) for i, p in enumerate(parts)]
    puts = [pltpu.make_async_copy(wide.at[p], gi_.at[p], sems.at[3, i]) for i, p in enumerate(parts)]

    @pl.when(straight)
    def _():
        for get in own:
            get.start()

    @pl.when(jnp.logical_not(straight))
    def _():
        for get in came:
            get.start()

    for copy in ins:
        copy.start()
    width = gains_.shape[1]
    mine = lax.rem(lax.axis_index("dp") * 2 + lax.axis_index("fsdp"), PAIR // width)
    small = g_par[:, pl.ds(0, width)]
    for i in range(1, PAIR // width):
        small = jnp.where(mine == i, g_par[:, pl.ds(i * width, width)], small)
    gains_[...] = small[0:2]
    shifts_[...] = small[2:4]

    @pl.when(straight)
    def _():
        for get, put in zip(own, puts):
            get.wait()
            put.start()

    @pl.when(jnp.logical_not(straight))
    def _():
        for get, put, p in zip(came, puts, parts):
            get.wait()
            wide[p, :] = narrow[p, :].astype(F32)
            put.start()

    for get, put in zip(ins, outs):
        get.wait()
        put.start()
    for put in puts + outs:
        put.wait()


def settle(width, fo, gi, gl, *grads):
    S = jax.ShapeDtypeStruct
    V = pltpu.VMEM
    hbm, vm = pl.BlockSpec(memory_space=pl.ANY), pl.BlockSpec(memory_space=V)
    kept = (fo, gi) + grads[:4]
    return pl.pallas_call(
        settle_kernel,
        out_shape=[S(v.shape, v.dtype) for v in kept] + [S((2, width), F32)] * 2,
        in_specs=[hbm] * 7 + [vm],
        out_specs=[hbm] * 6 + [vm] * 2,
        scratch_shapes=[V(gl.shape, BF), V(gi.shape, F32)] + [V(v.shape, v.dtype) for v in (fo,) + grads[:4]] + [DMA((4, 5))],
        compiler_params=pltpu.CompilerParams(vmem_limit_bytes=VMEM_LIMIT),
    )(fo, gi, gl, *grads)


def norm_rows(values, gain, shift):
    center = values - jnp.mean(values, -1, keepdims=True)
    spread = jnp.mean(center * center, -1, keepdims=True)
    return center * lax.rsqrt(spread + EPS) * gain + shift


def collect(w_qkv, w_out, w_up, w_down, gains, shifts):
    return (
        lax.all_gather(w_qkv, ("dp", "fsdp"), axis=0, tiled=True),
        lax.all_gather(w_out, ("dp", "fsdp"), axis=0, tiled=True),
        lax.all_gather(w_up, ("dp", "fsdp"), axis=0, tiled=True),
        lax.all_gather(w_down, ("dp", "fsdp"), axis=0, tiled=True),
        lax.all_gather(gains, ("dp", "fsdp"), axis=1, tiled=True),
        lax.all_gather(shifts, ("dp", "fsdp"), axis=1, tiled=True),
    )


def split_heads(matrix):
    return matrix.reshape(matrix.shape[0], H, HD).transpose(1, 0, 2)


def join_heads(stacked):
    return stacked.transpose(1, 0, 2).reshape(stacked.shape[1], H * HD)


def masked_scores(query_one, key_one, allowed):
    scores = jnp.dot(query_one, key_one.T, preferred_element_type=jnp.float32) * 0.125
    return jnp.where(allowed, scores, -1e30)


def forward(inputs, weights, allowed):
    w_qkv, w_out, w_up, w_down, gains, shifts = weights
    width = inputs.shape[1]
    gain_rows = gains.astype(jnp.float32)
    shift_rows = shifts.astype(jnp.float32)
    normed = norm_rows(inputs, gain_rows[0], shift_rows[0]).astype(jnp.bfloat16)
    mixed = jnp.dot(normed, w_qkv, preferred_element_type=jnp.float32).astype(jnp.bfloat16)
    queries = mixed[:, :width]
    keys_all, values_all = (
        lax.all_gather(mixed[:, width : 2 * width], "fsdp", axis=0, tiled=True),
        lax.all_gather(mixed[:, 2 * width :], "fsdp", axis=0, tiled=True),
    )
    query_heads = split_heads(queries)
    key_heads = split_heads(keys_all)
    value_heads = split_heads(values_all)

    def single(pieces):
        scores = masked_scores(pieces[0], pieces[1], allowed)
        peak_row = jnp.max(scores, -1, keepdims=True)
        log_total = peak_row + jnp.log(jnp.sum(jnp.exp(scores - peak_row), -1, keepdims=True))
        chance = jnp.exp(scores - log_total).astype(jnp.bfloat16)
        return (jnp.dot(chance, pieces[2], preferred_element_type=jnp.float32), log_total[:, 0])

    outputs, totals = lax.map(single, (query_heads, key_heads, value_heads))
    attended = join_heads(outputs).astype(jnp.bfloat16)
    middle = inputs + jnp.dot(attended, w_out, preferred_element_type=jnp.float32)
    normed_two = norm_rows(middle, gain_rows[1], shift_rows[1]).astype(jnp.bfloat16)
    hidden = jnp.dot(normed_two, w_up, preferred_element_type=jnp.float32)
    active = jax.nn.gelu(hidden, approximate=False).astype(jnp.bfloat16)
    result = middle + jnp.dot(active, w_down, preferred_element_type=jnp.float32)
    saved = (
        normed,
        query_heads,
        key_heads,
        value_heads,
        totals,
        attended,
        middle,
        normed_two,
        hidden,
        active,
    )
    return (result, saved)


def on_device(frames_in, prefix_len, w_qkv, w_out, w_up, w_down, gains, shifts, cotangent):
    inputs = frames_in[0].astype(jnp.float32)
    rows_here = inputs.shape[0]
    frames_all = rows_here * lax.axis_size("fsdp")
    first_row = lax.axis_index("fsdp") * rows_here
    places = first_row + jnp.arange(rows_here, dtype=jnp.int32)
    columns = jnp.arange(frames_all, dtype=jnp.int32)
    allowed = (columns[None, :] <= places[:, None]) | (columns[None, :] < prefix_len[0])
    weights = collect(w_qkv, w_out, w_up, w_down, gains, shifts)
    result, saved = forward(inputs, weights, allowed)
    weights = collect(w_qkv, w_out, w_up, w_down, gains, shifts)
    saved = forward(inputs, weights, allowed)[1]
    full_qkv, full_out, full_up, full_down, full_gains, full_shifts = weights
    (
        normed,
        query_heads,
        key_heads,
        value_heads,
        totals,
        attended,
        middle,
        normed_two,
        hidden,
        active,
    ) = saved
    gain_rows = full_gains.astype(jnp.float32)
    shift_rows = full_shifts.astype(jnp.float32)
    grad_top = cotangent[0].astype(jnp.float32)
    grad_branch = grad_top.astype(jnp.bfloat16)
    part_down = jnp.dot(active.T, grad_branch, preferred_element_type=jnp.float32)
    grad_active = jnp.dot(grad_branch, full_down.T, preferred_element_type=jnp.float32)
    gelu_pull = jax.vjp(functools.partial(jax.nn.gelu, approximate=False), hidden)[1]
    grad_hidden = gelu_pull(grad_active)[0].astype(jnp.bfloat16)
    part_up = jnp.dot(normed_two.T, grad_hidden, preferred_element_type=jnp.float32)
    grad_normed_two = jnp.dot(grad_hidden, full_up.T, preferred_element_type=jnp.float32)
    norm_pull_two = jax.vjp(norm_rows, middle, gain_rows[1], shift_rows[1])[1]
    back_middle, grad_gain_two, grad_shift_two = norm_pull_two(grad_normed_two)
    grad_middle = grad_top + back_middle
    grad_attn_out = grad_middle.astype(jnp.bfloat16)
    part_out = jnp.dot(attended.T, grad_attn_out, preferred_element_type=jnp.float32)
    grad_attended = jnp.dot(grad_attn_out, full_out.T, preferred_element_type=jnp.float32).astype(
        jnp.bfloat16
    )
    grad_att_heads = split_heads(grad_attended)

    def single_back(pieces):
        query_one, key_one, value_one, grad_one, log_total = pieces
        scores = masked_scores(query_one, key_one, allowed)
        chance = jnp.exp(scores - log_total[:, None])
        grad_chance = jnp.dot(grad_one, value_one.T, preferred_element_type=jnp.float32)
        inner = jnp.sum(chance * grad_chance, -1, keepdims=True)
        grad_scores = (chance * (grad_chance - inner)).astype(jnp.bfloat16)
        grad_query = jnp.dot(grad_scores, key_one, preferred_element_type=jnp.float32) * 0.125
        grad_key = (
            jnp.einsum("qk,qd->kd", grad_scores, query_one, preferred_element_type=jnp.float32)
            * 0.125
        )
        grad_value = jnp.einsum(
            "qk,qd->kd", chance.astype(jnp.bfloat16), grad_one, preferred_element_type=jnp.float32
        )
        return (grad_query, grad_key, grad_value)

    grad_q_heads, grad_k_heads, grad_v_heads = lax.map(
        single_back, (query_heads, key_heads, value_heads, grad_att_heads, totals)
    )
    grad_keys, grad_values = (
        lax.psum_scatter(
            join_heads(grad_k_heads).astype(jnp.bfloat16), "fsdp", scatter_dimension=0, tiled=True
        ).astype(jnp.float32),
        lax.psum_scatter(
            join_heads(grad_v_heads).astype(jnp.bfloat16), "fsdp", scatter_dimension=0, tiled=True
        ).astype(jnp.float32),
    )
    grad_mixed = jnp.concatenate([join_heads(grad_q_heads), grad_keys, grad_values], 1).astype(
        jnp.bfloat16
    )
    part_qkv = jnp.dot(normed.T, grad_mixed, preferred_element_type=jnp.float32)
    grad_normed = jnp.dot(grad_mixed, full_qkv.T, preferred_element_type=jnp.float32)
    norm_pull_one = jax.vjp(norm_rows, inputs, gain_rows[0], shift_rows[0])[1]
    back_inputs, grad_gain_one, grad_shift_one = norm_pull_one(grad_normed)
    grad_inputs = grad_middle + back_inputs
    part_gains = jnp.stack([grad_gain_one, grad_gain_two])
    part_shifts = jnp.stack([grad_shift_one, grad_shift_two])
    owned = (
        lax.psum_scatter(part_qkv, ("dp", "fsdp"), scatter_dimension=0, tiled=True),
        lax.psum_scatter(part_out, ("dp", "fsdp"), scatter_dimension=0, tiled=True),
        lax.psum_scatter(part_up, ("dp", "fsdp"), scatter_dimension=0, tiled=True),
        lax.psum_scatter(part_down, ("dp", "fsdp"), scatter_dimension=0, tiled=True),
        lax.psum_scatter(part_gains, ("dp", "fsdp"), scatter_dimension=1, tiled=True),
        lax.psum_scatter(part_shifts, ("dp", "fsdp"), scatter_dimension=1, tiled=True),
    )
    return (
        result.astype(jnp.bfloat16)[None],
        grad_inputs[None],
        owned[0],
        owned[1],
        owned[2],
        owned[3],
        owned[4],
        owned[5],
    )


def fast_device(ndp, frames_in, prefix_len, w_qkv, w_out, w_up, w_down, gains, shifts, cotangent):
    here = lax.axis_index("dp") * 2 + lax.axis_index("fsdp")
    width = gains.shape[1]
    per = PAIR // width
    rows = jnp.concatenate([gains, shifts, jnp.zeros((12, width), BF)], 0)
    tile = jnp.where(lax.broadcasted_iota(jnp.int32, (16, per, width), 1) == here % per, rows[:, None], 0.0)
    tile = tile.astype(BF).reshape(16, PAIR)
    pre = jnp.broadcast_to(prefix_len[None], (8, PAIR))
    result = layer(ndp // 4, frames_in[0], cotangent[0], pre, w_qkv, w_out, w_up, w_down, tile)
    frames_out, grad_in, *owned = settle(width, *result[:3], *result[8:])
    return (frames_out[None], grad_in[None]) + tuple(owned)


def solution(mesh):
    ndp, nf = mesh.shape["dp"], mesh.shape["fsdp"]
    both = P(("dp", "fsdp"), None)
    lanes = P(None, ("dp", "fsdp"))
    block = P("dp", "fsdp", None)
    body = functools.partial(fast_device, ndp) if (nf == 2 and ndp == 16) else on_device
    return jax.shard_map(
        body,
        mesh=mesh,
        in_specs=(block, P("dp"), both, both, both, both, lanes, lanes, block),
        out_specs=(block, block, both, both, both, both, lanes, lanes),
        check_vma=False,
    )
```

```python
import functools
import math

import jax
import jax.numpy as jnp
from jax import lax
from jax.experimental import pallas as pl
from jax.experimental.pallas import tpu as pltpu
from jax.sharding import PartitionSpec as P

H = 16
HD = 64
EPS = 1e-05
BF = jnp.bfloat16
F32 = jnp.float32
LOG2E = math.log2(math.e)
SCALE2 = 0.125 * LOG2E
PAIR = 2 * HD
TILE = 512
MESH = pl.DeviceIdType.MESH
DMA = pltpu.SemaphoreType.DMA
VMEM_LIMIT = 60 * 2**20


def coords():
    dp, f = lax.axis_index("dp"), lax.axis_index("fsdp")
    q = lax.div(dp, 2)
    return lax.div(q, 2), lax.rem(q, 2), lax.rem(dp, 2), f


def dev(z, y, c, f):
    return ((z * 2 + y) * 2 + c, f)


def remote(src, dst, send, recv, device):
    return pltpu.make_async_remote_copy(
        src_ref=src, dst_ref=dst, send_sem=send, recv_sem=recv, device_id=device, device_id_type=MESH
    )


def greet(peers):
    barrier = pltpu.get_barrier_semaphore()
    for peer in peers:
        pl.semaphore_signal(barrier, inc=1, device_id=peer, device_id_type=MESH)
    pl.semaphore_wait(barrier, len(peers))


def all_peers(nz, z, y, c, f):
    peers = [dev(lax.rem(z + k, nz), y, c, f) for k in range(1, nz)]
    return peers + [dev(z, 1 - y, c, f), dev(z, y, c, 1 - f), dev(z, y, 1 - c, f)]


def dot_nn(a, b):
    return lax.dot_general(a, b, (((1,), (0,)), ((), ())), preferred_element_type=F32)


def dot_nt(a, b):
    return lax.dot_general(a, b, (((1,), (1,)), ((), ())), preferred_element_type=F32)


def dot_tn(a, b):
    return lax.dot_general(a, b, (((0,), (0,)), ((), ())), preferred_element_type=F32)


def normalise(v):
    center = v - jnp.mean(v, -1, keepdims=True)
    scale = lax.rsqrt(jnp.mean(center * center, -1, keepdims=True) + EPS)
    return center * scale, scale


def lane_half():
    return lax.broadcasted_iota(jnp.int32, (1, PAIR), 1) // HD


def fill_bias(bias, prefix, c, transposed):
    rows = bias.shape[0]
    step = 64

    def body(j, part):
        a = lax.broadcasted_iota(jnp.int32, (step, rows), 0) + j * step
        b = lax.broadcasted_iota(jnp.int32, (step, rows), 1)
        row, key = (b, a) if transposed else (a, b)
        bias[part, :] = jnp.where((key <= row) | (key + c * rows < prefix), 0.0, -1e30)

    tiles(rows // step, step, body)


def norm_back(gh, n, scale, gain):
    gn = gh * gain
    return scale * (gn - jnp.mean(gn, -1, keepdims=True) - n * jnp.mean(gn * n, -1, keepdims=True))


class Gather:
    def __init__(self, nz, place, shards, outs, chunks, sems):
        self.nz, self.place, self.shards, self.outs, self.chunks = nz, place, shards, outs, chunks
        self.send, self.recv, self.own = sems

    @staticmethod
    def sem_shapes(n):
        return [DMA((n, 12)), DMA((n, 12)), DMA((n,))]

    def mine(self, i):
        w, r0, r, c0, n = self.chunks[i]
        return self.shards[w].at[pl.ds(r0, r), pl.ds(c0, n)]

    def at(self, i, *where):
        w, r0, r, c0, n = self.chunks[i]
        where += (slice(None),) * (4 - len(where))
        return self.outs[w].at[where + (pl.ds(r0, r), pl.ds(c0, n))]

    def hop(self, i, slot, src, dst, device):
        return remote(src, dst, self.send.at[i, slot], self.recv.at[i, slot], device)

    def copies(self, i):
        z, y, c, f = self.place
        nz = self.nz
        every = slice(None)
        core, xp, yp = dev(z, y, 1 - c, f), dev(z, y, c, 1 - f), dev(z, 1 - y, c, f)
        mine, home = self.mine(i), self.at(i, z, y, c, f)

        def same(slot, ref, device):
            return self.hop(i, slot, ref, ref, device)

        zs = [dev(lax.rem(z + k, nz), y, c, f) for k in range(1, nz)]
        line = self.at(i, every, y, c, f)
        other = self.at(i, every, 1 - y, c, f)
        zero = {
            0: [self.hop(i, k, mine, home, zs[k]) for k in range(nz - 1)],
            1: [same(3, line, yp), same(4, line, xp), same(8, line, core)],
            2: [same(5, other, xp), same(9, other, core)],
            3: [same(10, self.at(i, every, every, c, 1 - f), core)],
        }
        rows = self.at(i, z, y, c)
        plane = self.at(i, every, y, c)
        one = {
            0: [self.hop(i, 3, mine, home, xp)],
            1: [same(k, rows, zs[k]) for k in range(nz - 1)],
            2: [same(4, plane, yp), same(8, plane, core)],
            3: [same(9, self.at(i, every, 1 - y, c), core)],
        }
        return zero, one

    def arrivals(self, i):
        z, y, c, f = self.place
        nz = self.nz
        every = slice(None)
        zk = [lax.rem(z + nz - k, nz) for k in range(1, nz)]
        core = dev(z, y, 1 - c, f)

        def here(slot, *where):
            ref = self.at(i, *where)
            return self.hop(i, slot, ref, ref, core)

        zero = {
            1: [here(k, zk[k], y, c, f) for k in range(nz - 1)],
            2: [here(3, every, 1 - y, c, f)],
            3: [here(4, every, y, c, 1 - f), here(5, every, 1 - y, c, 1 - f)],
            4: [here(8, every, y, 1 - c), here(9, every, 1 - y, 1 - c)],
        }
        one = {
            1: [here(3, z, y, c, 1 - f)],
            2: [here(k, zk[k], y, c) for k in range(nz - 1)],
            3: [here(4, every, 1 - y, c)],
            4: [here(8, every, y, 1 - c, f), here(9, every, 1 - y, 1 - c, f), here(10, every, every, 1 - c, 1 - f)],
        }
        return zero, one

    def local(self, i):
        z, y, c, f = self.place
        return pltpu.make_async_copy(self.mine(i), self.at(i, z, y, c, f), self.own.at[i])

    def stage(self, i, s):
        if s == 1:
            self.local(i).wait()
        for core in range(2):

            @pl.when(self.place[2] == core)
            def _():
                if s:
                    for copy in self.arrivals(i)[core][s]:
                        copy.wait_recv()
                if s < 4:
                    for copy in self.copies(i)[core][s]:
                        copy.start()

    def tick(self, t, stages=(0, 1, 2, 3)):
        for s in stages:
            if 0 <= t - s < len(self.chunks):
                self.stage(t - s, s)

    def finish(self, i):
        for core in range(2):

            @pl.when(self.place[2] == core)
            def _():
                for copies in self.copies(i)[core].values():
                    for copy in copies:
                        copy.wait_send()


RING = 6
BLOCK = 32
WIDE = 1024


def tiles(count, size, body, hooks=None):
    @pl.loop(0, count)
    def _(j):
        body(j, pl.ds(pl.multiple_of(j * size, size), size))
        run_hooks(j, hooks)


def run_hooks(j, hooks):
    for at, hook in (hooks or {}).items():

        @pl.when(j == at)
        def _():
            hook()


def flat(ref, cols):
    v = ref[:, :, :, :, cols]
    return v.reshape(math.prod(v.shape[:-1]), v.shape[-1])


def add_blocks(dst, parts, out=None):
    lead, n = dst.shape[:-2], dst.shape[-1]
    size = min(n, 256)

    @pl.loop(0, math.prod(lead) * (n // size))
    def _(j):
        cols = pl.ds(pl.multiple_of(lax.rem(j, n // size) * size, size), size)
        at, rest = [], lax.div(j, n // size)
        for count in reversed(lead):
            at.insert(0, lax.rem(rest, count))
            rest = lax.div(rest, count)
        at = tuple(at) + (slice(None), cols)
        total = dst[at].astype(F32)
        for p in parts:
            total = total + p[at].astype(F32)
        if out is None:
            dst[at] = total.astype(dst.dtype)
        else:
            out[at] = total


class Scatter:
    def __init__(self, nz, place, sums, second, third, outs, sems):
        self.nz, self.place, self.sums, self.second, self.third = nz, place, sums, second, third
        self.outs, self.done = outs, set()
        self.send, self.recv, self.free = sems

    @staticmethod
    def sem_shapes(n):
        return [DMA((n, 5)), DMA((n, 5)), pltpu.SemaphoreType.REGULAR((RING,))]

    def peers(self):
        z, y, c, f = self.place
        zs = [dev(lax.rem(z + k, self.nz), y, c, f) for k in range(1, self.nz)]
        return zs, dev(z, 1 - y, c, f), dev(z, y, c, 1 - f)

    def hop(self, i, slot, src, dst, device):
        return remote(src, dst, self.send.at[i, slot], self.recv.at[i, slot], device)

    def copies(self, i):
        z, y, c, f = self.place
        s, b2, b3, nz = self.sums[i], self.second[i], self.third[i], self.nz
        zs, yp, xp = self.peers()
        zt = [lax.rem(z + k, nz) for k in range(1, nz)]
        zero = {
            0: [self.hop(i, 0, s.at[:, :, 1 - f], b2, xp)],
            1: [self.hop(i, 1, s.at[:, 1 - y, f], b3.at[pl.ds(0, nz)], yp)],
            2: [self.hop(i, 2 + k, s.at[zt[k], y, f], b3.at[nz + k], zs[k]) for k in range(nz - 1)],
        }
        one = {
            0: [self.hop(i, 0, s.at[:, 1 - y], b2, yp)],
            1: [self.hop(i, 1 + k, s.at[zt[k], y], b3.at[pl.ds(2 * k, 2)], zs[k]) for k in range(nz - 1)],
            2: [self.hop(i, nz, s.at[z, y, 1 - f], b3.at[2 * (nz - 1)], xp)],
        }
        return zero, one

    def stage(self, i, st):
        z, y, c, f = self.place
        nz = self.nz
        self.done.add((i, st))
        s, b2, b3 = self.sums[i], self.second[i], self.third[i]
        copies = self.copies(i)
        zs, yp, xp = self.peers()
        ringed = i < len(self.sums) - 1
        if st == 0 and ringed and i >= RING:
            pl.semaphore_wait(self.free.at[i % RING], nz + 1)

        @pl.when(c == 0)
        def _():
            if st:
                for copy in copies[0][st - 1]:
                    copy.wait_recv()
            if st == 0:
                copies[0][0][0].start()
            if st == 1:
                add_blocks(s.at[:, 1 - y, f], [b2.at[:, 1 - y]])
                copies[0][1][0].start()
                add_blocks(s.at[:, y, f], [b2.at[:, y]])
            if st == 2:
                for k in range(nz - 1):
                    zt = lax.rem(z + k + 1, nz)
                    add_blocks(s.at[zt, y, f], [b3.at[zt]])
                    copies[0][2][k].start()
                add_blocks(s.at[z, y, f], [b3.at[z]])
            if st == 3:
                add_blocks(s.at[z, y, f], [b3.at[nz + k] for k in range(nz - 1)], self.outs[i])

        @pl.when(c == 1)
        def _():
            if st:
                for copy in copies[1][st - 1]:
                    copy.wait_recv()
            if st == 0:
                copies[1][0][0].start()
            if st == 1:
                for k in range(nz - 1):
                    zt = lax.rem(z + k + 1, nz)
                    add_blocks(s.at[zt, y], [b2.at[zt]])
                    copies[1][1][k].start()
                add_blocks(s.at[z, y], [b2.at[z]])
            if st == 2:
                add_blocks(s.at[z, y, 1 - f], [b3.at[2 * k + 1 - f] for k in range(nz - 1)])
                copies[1][2][0].start()
                add_blocks(s.at[z, y, f], [b3.at[2 * k + f] for k in range(nz - 1)])
            if st == 3:
                add_blocks(s.at[z, y, f], [b3.at[2 * (nz - 1)]], self.outs[i])

        if st == 3 and ringed and i + RING < len(self.sums) - 1:
            for peer in zs + [yp, xp]:
                pl.semaphore_signal(self.free.at[i % RING], inc=1, device_id=peer, device_id_type=MESH)

    def tick(self, t):
        for st in range(1, 4):
            i = t - st
            if (i, st - 1) in self.done and (i, st) not in self.done:
                self.stage(i, st)

    def finish(self, i):
        for core in range(2):

            @pl.when(self.place[2] == core)
            def _():
                for copies in self.copies(i)[core].values():
                    for copy in copies:
                        copy.wait_send()


class Producer:
    def __init__(self, place, buf, land, sems):
        self.place, self.buf, self.land = place, buf, land
        self.send, self.recv, self.credit = sems
        z, y, c, f = place
        self.core = dev(z, y, 1 - c, f)
        self.made, self.pending = 0, None

    def copy(self, slot):
        theirs = self.buf.at[slot, :, 1 - self.place[2]]
        return remote(theirs, self.land.at[slot], self.send.at[slot], self.recv.at[slot], self.core)

    def before(self, slot):
        self.copy(slot).wait_send()
        pl.semaphore_wait(self.credit.at[slot], 1)

    def absorb(self, j, target):
        c = self.place[2]
        slot = lax.rem(j, 2)
        self.copy(slot).wait_recv()
        for i in range(4):
            ref = target(j, i)
            for k in range(2):
                ref[k] = (self.buf[slot, i, c, k].astype(F32) + self.land[slot, i, k].astype(F32)).astype(BF)
        pl.semaphore_signal(self.credit.at[slot], inc=1, device_id=self.core, device_id_type=MESH)

    def flush(self):
        if self.pending is not None:
            self.absorb(*self.pending)
            self.pending = None

    def run(self, count, product, where, target, hooks=None):
        fresh, pending = self.made == 0, self.pending

        @pl.loop(0, count)
        def _(j):
            slot = lax.rem(j, 2)
            if not fresh:
                self.before(slot)
            elif count > 2:

                @pl.when(j >= 2)
                def _():
                    self.before(slot)

            v = product(j)
            for i in range(4):
                for k in range(2):
                    for core in range(2):
                        at = where(i, core, k)
                        self.buf[slot, i, core, k] = v[at : at + BLOCK].astype(BF)
            self.copy(slot).start()
            if pending is not None:

                @pl.when(j == 0)
                def _():
                    self.absorb(*pending)

            @pl.when(j >= 1)
            def _():
                self.absorb(j - 1, target)

            run_hooks(j, hooks)

        self.made += count
        self.pending = (count - 1, target)

    def finish(self):
        for slot in range(2):
            self.before(slot)


def row_blocks(i, core, k):
    return BLOCK * (4 * i + 2 * core + k)


def deep_blocks(i, core, k):
    return BLOCK * (8 * core + 4 * k + i)


def attend_forward(c, qkv, cross, bias, att, lse, hooks):
    rows, d = att.shape
    half = lane_half()
    lane = lax.broadcasted_iota(jnp.int32, (1, PAIR), 1)
    rt = rows // 2

    def one(q, blocks):
        scores = []
        for keys, _, extra in blocks:
            s = dot_nt(q, keys) * SCALE2
            scores.append(s if extra is None else s + extra)
        peak = functools.reduce(jnp.maximum, [jnp.max(s, -1, keepdims=True) for s in scores])
        total = None
        for s, (_, values, _) in zip(scores, blocks):
            part = dot_nn(jnp.exp2(s - peak).astype(BF), values)
            total = part if total is None else total + part
        return total, peak

    def pair(p, second):
        cols = pl.ds(pl.multiple_of(p * PAIR, PAIR), PAIR)
        kcols = pl.ds(pl.multiple_of(d + p * PAIR, PAIR), PAIR)
        vcols = pl.ds(pl.multiple_of(2 * d + p * PAIR, PAIR), PAIR)
        def half_rows(r, part):
            results = []
            for h in range(2):
                mine = half == h
                q = jnp.where(mine, qkv[part, cols], 0.0).astype(BF)

                def val(v):
                    return jnp.where(mine, v, 1.0).astype(BF)

                if second:
                    blocks = [(cross[:, cols], val(cross[:, kcols]), None)]
                    if r > 0:
                        blocks.append((qkv[pl.ds(0, rt), kcols], val(qkv[pl.ds(0, rt), vcols]), None))
                    blocks.append((qkv[part, kcols], val(qkv[part, vcols]), bias[part, pl.ds(r * rt, rt)]))
                else:
                    blocks = [(qkv[:, kcols], val(qkv[:, vcols]), bias[part, :])]
                total, peak = one(q, blocks)
                sums = pltpu.roll(total, HD, axis=1)
                results.append(total / sums)
                both = jnp.where(mine, sums, total)
                lse[part, :] = jnp.where(lane == 2 * p + h, peak + jnp.log2(both), lse[part, :])
            att[part, cols] = jnp.where(half == 0, results[0], results[1]).astype(BF)

        if second:
            for r in range(2):
                half_rows(r, pl.ds(r * rt, rt))
        else:
            tiles(2, rt, half_rows)

    @pl.loop(0, d // PAIR)
    def _(p):
        for second in range(2):

            @pl.when(c == second)
            def _():
                pair(p, second == 1)

        run_hooks(p, hooks)


SHARED = 5


def attend_backward(c, qkv, cross, biast, lset, deltat, far_lse, far_delta, go, gq, gq2, more, hooks):
    rows, d = go.shape
    half = lane_half()
    rt = rows // 2
    pairs = d // PAIR

    def term(p, keys, values, krows, qrows, queries, grads, lse, delta, masked, total):
        gk = gv = None
        for h in range(2):
            mine = half == h
            q = jnp.where(mine, queries, 0.0).astype(BF)
            g = jnp.where(mine, grads, 0.0).astype(BF)
            km = jnp.where(mine, keys, 0.0).astype(BF)
            s = dot_nt(keys, q) * SCALE2
            if masked:
                s = s + biast[krows, qrows]
            pr = jnp.exp2(s - lse[pl.ds(2 * p + h, 1), qrows])
            gs = (pr * (dot_nt(values, g) - delta[pl.ds(2 * p + h, 1), qrows])).astype(BF)
            k1, v1 = dot_nn(gs, q), dot_nn(pr.astype(BF), g)
            gk, gv = (k1, v1) if gk is None else (gk + k1, gv + v1)
            total[qrows, :] = total[qrows, :] + dot_tn(gs, km)
        return gk, gv

    every = pl.ds(0, rows)
    first, last = pl.ds(0, PAIR), pl.ds(PAIR, PAIR)

    @pl.loop(0, pairs)
    def _(i):
        @pl.when(c == 0)
        def _():
            heavy = i < pairs - SHARED
            p = lax.rem(i + SHARED, pairs)
            cols = pl.ds(pl.multiple_of(p * PAIR, PAIR), PAIR)
            kcols = pl.ds(pl.multiple_of(d + p * PAIR, PAIR), PAIR)
            vcols = pl.ds(pl.multiple_of(2 * d + p * PAIR, PAIR), PAIR)
            gq[...] = jnp.zeros_like(gq)

            @pl.when(heavy)
            def _():
                gq2[...] = jnp.zeros_like(gq2)

                def far_part(r, krows):
                    more[krows, first], more[krows, last] = term(
                        p, qkv[krows, kcols], qkv[krows, vcols], krows, every, cross[:, cols], cross[:, kcols], far_lse, far_delta, False, gq2
                    )

                tiles(2, rt, far_part)
                cross[:, cols] = (gq2[...] * 0.125).astype(BF)

            @pl.when(i == pairs - SHARED)
            def _():
                more[:, first] = jnp.zeros_like(gq)
                more[:, last] = jnp.zeros_like(gq)

            def own_part(r, krows):
                gk, gv = term(
                    p, qkv[krows, kcols], qkv[krows, vcols], krows, every, qkv[:, cols], go[:, cols], lset, deltat, True, gq
                )
                qkv[krows, kcols] = ((gk + more[krows, first]) * 0.125).astype(BF)
                qkv[krows, vcols] = (gv + more[krows, last]).astype(BF)

            tiles(2, rt, own_part)
            qkv[:, cols] = (gq[...] * 0.125).astype(BF)

        @pl.when(c == 1)
        def _():
            p = i
            cols = pl.ds(pl.multiple_of(p * PAIR, PAIR), PAIR)
            kcols = pl.ds(pl.multiple_of(d + p * PAIR, PAIR), PAIR)
            vcols = pl.ds(pl.multiple_of(2 * d + p * PAIR, PAIR), PAIR)
            gq[...] = jnp.zeros_like(gq)

            @pl.when(p < SHARED)
            def _():
                def near_part(r, krows):
                    gk, gv = term(
                        p, cross[krows, cols], cross[krows, kcols], krows, every, qkv[:, cols], go[:, cols], lset, deltat, False, gq
                    )
                    cross[krows, cols] = (gk * 0.125).astype(BF)
                    cross[krows, kcols] = gv.astype(BF)

                tiles(2, rt, near_part)

            for r in range(2):
                krows, qrows = pl.ds(r * rt, rt), pl.ds(r * rt, rows - r * rt)
                gk, gv = term(
                    p, qkv[krows, kcols], qkv[krows, vcols], krows, qrows, qkv[qrows, cols], go[qrows, cols], lset, deltat, True, gq
                )
                qkv[krows, kcols] = (gk * 0.125).astype(BF)
                qkv[krows, vcols] = gv.astype(BF)
            qkv[:, cols] = (gq[...] * 0.125).astype(BF)

        run_hooks(i, hooks)


def layer_kernel(nz, *refs):
    (
        frames_in, cot_in, pre_in, s_qkv, s_out, s_up, s_down, s_par,
        fo, gi, gl, f_qkv, f_out, f_up, f_down, f_par, g_qkv, g_out, g_up, g_down, g_par,
        x, cot, pre, h1, qkv, cross, att, x1, h2, a, gp, wa, wb, gh, gz, go, bias, narrow, narrow2, lset, deltat, far_lse, far_delta,
        acc, par, parv, ht, buf, land, sdown, spar, ptheirs, pland, second, third, psecond, pthird,
        ag_send, ag_recv, ag_own, rs_send, rs_recv, rs_free, p_send, p_recv, p_credit,
        load_sem, swap_sem, io_sem, io_recv,
    ) = refs
    place = z, y, c, f = coords()
    rows, d = x.shape
    ff = a.shape[-1]
    core, far = dev(z, y, 1 - c, f), dev(z, y, 1 - c, 1 - f)
    straight = c == f
    nk = d // WIDE

    chunks = [(4, 0, 16, 0, PAIR)]
    chunks += [(0, 0, BLOCK, d + h * TILE, TILE) for h in range(2)] + [(0, 0, BLOCK, b * d, d) for b in (2, 0)]
    chunks += [(1, 0, BLOCK, 0, d)]
    chunks += [(2, 0, BLOCK, k * WIDE, WIDE) for k in range(ff // WIDE)]
    down_cols = [(0, 256), (256, 256), (512, 256), (768, 128), (896, 128)]
    chunks += [(3, 0, 4 * BLOCK, c0, w) for c0, w in down_cols]
    ag = Gather(nz, place, (s_qkv, s_out, s_up, s_down, s_par), (f_qkv, f_out, f_up, f_down, f_par), chunks, (ag_send, ag_recv, ag_own))

    ups, downs = ff // WIDE, 4
    sums = [sdown.at[k] for k in range(downs)]
    sums += [a.at[:, :, :, :, pl.ds(k * WIDE, WIDE)] for k in range(ups)]
    tail = [(3 * d, d), (d, d), (2 * d, d), (0, TILE), (TILE, TILE)]
    sums += [gp.at[:, :, :, :, pl.ds(c0, w)] for c0, w in tail]
    goes = [g_down.at[pl.ds(k * BLOCK, BLOCK)] for k in range(downs)]
    goes += [g_up.at[:, pl.ds(k * WIDE, WIDE)] for k in range(ups)]
    goes += [g_out] + [g_qkv.at[:, pl.ds(c0, w)] for c0, w in tail[1:]]
    n = len(sums)
    widths = [WIDE] * (downs + ups) + [w for _, w in tail]
    rs = Scatter(
        nz, place, sums + [spar], [second.at[i % RING, :, :, :, pl.ds(0, widths[i])] for i in range(n)] + [psecond],
        [third.at[i % RING, :, :, pl.ds(0, widths[i])] for i in range(n)] + [pthird], goes + [g_par], (rs_send, rs_recv, rs_free),
    )
    maker = Producer(place, buf, land, (p_send, p_recv, p_credit))

    for i in range(len(chunks)):
        ag.local(i).start()
    greet(all_peers(nz, *place) + [far])

    swaps = []
    quarter = rows // 4
    quarters = [pl.ds(i * quarter, quarter) for i in range(4)]
    moves = [(pre_in, pre)]
    moves += [(cot_in.at[q], cot.at[q]) for q in quarters] + [(frames_in.at[q], x.at[q]) for q in quarters]
    for i, (src, dst) in enumerate(moves):
        swaps.append((pltpu.make_async_copy(src, dst, swap_sem.at[i, 0]), remote(src, dst, swap_sem.at[i, 1], swap_sem.at[i, 2], far)))

    def swap_start(i):
        @pl.when(straight)
        def _():
            swaps[i][0].start()

        @pl.when(jnp.logical_not(straight))
        def _():
            swaps[i][1].start()

    def swap_wait(i):
        @pl.when(straight)
        def _():
            swaps[i][0].wait()

        @pl.when(jnp.logical_not(straight))
        def _():
            swaps[i][1].wait()

    def between(i, src, dst):
        return remote(src, dst, swap_sem.at[i, 1], swap_sem.at[i, 2], core)

    def ag_tick(t):
        return lambda: ag.tick(t)

    def rs_tick(t):
        return lambda: rs.tick(t)

    def rs_begin(i):
        return lambda: rs.stage(i, 0)

    def small(b):
        return pl.ds(b * BLOCK, BLOCK)

    def load(i, src, dst):
        return pltpu.make_async_copy(src, dst, load_sem.at[i])

    def load_block(i, b):
        if b == 3:
            return load(i, f_out, wa.at[:, :, :, :, small(3)])
        return load(i, f_qkv.at[:, :, :, :, :, pl.ds(b * d, d)], wa.at[:, :, :, :, small(b)])

    def block(b, at=slice(None)):
        v = wa[at, :, :, :, small(b)]
        return v.reshape(math.prod(v.shape[:-1]), d)

    ag.stage(0, 0)
    ag.stage(1, 0)
    swap_start(0)
    ag.stage(0, 1)
    ag.tick(2)
    swap_start(5)
    ag.tick(3)
    swap_start(6)
    ag.stage(0, 4)
    get_par = load(0, f_par, parv)
    get_par.start()
    swap_wait(0)
    fill_bias(bias, pre[0:1, 0:1], c, False)
    get_par.wait()
    for t in range(d // PAIR):
        total = None
        for k in range(4):
            piece = parv[t // 2, t % 2, k // 2, k % 2].astype(F32)
            total = piece if total is None else total + piece
        par[:, pl.ds(t * PAIR, PAIR)] = total
    step = 64

    def norm_one(j, part):
        nrm, _ = normalise(x[part, :].astype(F32))
        h1[part, :] = (nrm * par[0:1, :] + par[2:3, :]).astype(BF)

    ag.tick(4)
    swap_start(7)
    keyvals = between(14, qkv.at[:, pl.ds(d, 2 * d)], cross)
    ag.stage(1, 4)
    for i, b in enumerate((1, 2, 0)):
        ag.tick(5 + i)
        if i == 0:
            swap_start(8)
            for k in range(4):
                swap_wait(5 + k)
            tiles(rows // step, step, norm_one)
        ag.stage(2 + i, 4)
        get = load_block(1 + i, b)
        get.start()
        get.wait()
        for t in range(d // TILE):
            cols = pl.ds(t * TILE, TILE)
            w = wa[:, :, :, :, small(b), cols].reshape(d, TILE)
            qkv[:, pl.ds(b * d + t * TILE, TILE)] = dot_nn(h1[...], w).astype(BF)
        swap_start(1 + i)
        if b == 2:

            @pl.when(c == 0)
            def _():
                keyvals.start()

    @pl.when(c == 1)
    def _():
        keyvals.wait_recv()

    swap_start(4)
    narrow[...] = jnp.zeros_like(narrow)
    attend_forward(c, qkv, cross, bias, att, narrow, {0: ag_tick(8), 5: ag_tick(9)})
    ag.stage(5, 4)
    get_out = load_block(4, 3)
    get_out.start()

    @pl.when(c == 0)
    def _():
        keyvals.wait_send()

    lset[...] = narrow[...].T[:H, :]

    def get_up(k):
        return load(5 + k, f_up.at[:, :, :, :, :, pl.ds(k * WIDE, WIDE)], wb.at[:, :, :, :, :, pl.ds(k * WIDE, WIDE)])

    ag.stage(6, 4)
    get_up(0).start()
    get_out.wait()
    for t in range(d // TILE):
        cols = pl.ds(t * TILE, TILE)
        w = wa[:, :, :, :, small(3), cols].reshape(d, TILE)
        x1[:, cols] = x[:, cols].astype(F32) + dot_nn(att[...], w)
    ag.tick(10)

    def norm_two(j, part):
        nrm, _ = normalise(x1[part, :])
        h2[part, :] = (nrm * par[1:2, :] + par[3:4, :]).astype(BF)

    tiles(rows // step, step, norm_two)
    u = gh.at[:, pl.ds(0, TILE)]

    def up(cols):
        gh[:, pl.ds(0, TILE)] = dot_nn(h2[...], wb[:, :, :, :, :, cols].reshape(d, TILE))

        @pl.loop(0, rows // BLOCK)
        def _(j):
            at = (lax.div(j, 4), lax.rem(lax.div(j, 2), 2), lax.rem(j, 2), slice(None), cols)
            v = gh[pl.ds(pl.multiple_of(j * BLOCK, BLOCK), BLOCK), pl.ds(0, TILE)]
            phi = 0.5 * (1.0 + lax.erf(v * math.sqrt(0.5)))
            dens = jnp.exp2(v * v * (-0.5 * LOG2E)) * (1.0 / math.sqrt(2.0 * math.pi))
            a[at] = (v * phi).astype(BF)
            gp[at] = (phi + v * dens).astype(BF)

    for i in range(4):
        swap_wait(1 + i)

    def down_product(j):
        for k in range(ups):

            @pl.when(j == 2 * k)
            def _():
                if k:
                    ag.stage(6 + k, 4)
                    get_up(k).start()
                get_up(k).wait()

        cols = pl.ds(pl.multiple_of(j * TILE, TILE), TILE)
        up(cols)
        for k in range(ups):

            @pl.when(j == 2 * k)
            def _():
                ag.tick(11 + k, (0, 1))

            @pl.when(j == 2 * k + 1)
            def _():
                ag.tick(11 + k, (2, 3))

        return dot_tn(flat(a, cols), cot[...])

    maker.run(2 * ups, down_product, deep_blocks, lambda j, i: sdown.at[i, lax.div(j, 2), lax.rem(j, 2)])

    def get_down(k):
        part = pl.ds(*down_cols[k])
        return load(9 + k, f_down.at[:, :, :, :, :, part], wa.at[:, :, :, :, :, part])

    def down(k):
        cols = pl.ds(k * TILE, TILE)
        w = wa[:, :, :, :, :, cols].reshape(ff, TILE)
        go[:, cols] = (x1[:, cols] + dot_nn(flat(a, slice(None)), w)).astype(BF)

    ag.tick(15)
    maker.flush()
    for k in range(2):
        ag.stage(10 + k, 4)
        get_down(k).start()
    ag.tick(16)
    ag.tick(17)
    rs.stage(0, 0)
    for k in range(2):
        get_down(k).wait()
    down(0)
    for k in range(2, len(down_cols)):
        ag.stage(10 + k, 4)
        get_down(k).start()
    for k in range(2, len(down_cols)):
        get_down(k).wait()
    rs.stage(1, 0)
    down(1)
    rs.stage(2, 0)
    outs = []
    for q in quarters:
        outs.append(
            (
                pltpu.make_async_copy(go.at[q], fo.at[q], io_sem.at[len(outs)]),
                remote(go.at[q], fo.at[q], io_sem.at[len(outs)], io_recv.at[len(outs)], far),
            )
        )

    def either(pair, act_on):
        @pl.when(straight)
        def _():
            act_on(pair[0])

        @pl.when(jnp.logical_not(straight))
        def _():
            act_on(pair[1])

    def begin(pair):
        either(pair, lambda copy: copy.start())

    def end(pair):
        either(pair, lambda copy: copy.wait())

    begin(outs[0])
    def act(j, cols):
        w = wa[lax.div(j, 2), lax.rem(j, 2)].reshape(TILE, d)
        v = dot_nt(cot[...], w) * flat(gp, cols).astype(F32)
        gp[:, :, :, :, cols] = v.astype(BF).reshape(a.shape[:-1] + (TILE,))

    rs.stage(3, 0)
    tiles(8, TILE, act, {5: rs_tick(1)})
    begin(outs[1])
    for i, b in enumerate((3, 0, 1, 2)):
        load_block(14 + i, b).start()
    ht[...] = h2[...].T
    for i in range(2):
        gh[:, pl.ds(i * TILE, TILE)] = dot_nt(flat(gp, slice(None)), wb[2 * i : 2 * i + 2].reshape(TILE, ff))
        if i == 0:
            rs.tick(2)
    begin(outs[2])
    acc[...] = jnp.zeros_like(acc)
    step = 32

    def collect(row, v):
        part = v.reshape(step // 8, 8, d)
        acc[row] = acc[row] + functools.reduce(jnp.add, [part[i] for i in range(step // 8)])

    def back_two(j, part):
        nrm, scale = normalise(x1[part, :])
        g = gh[part, :]
        collect(1, g * nrm)
        collect(3, g)
        total = cot[part, :].astype(F32) + norm_back(g, nrm, scale, par[1:2, :])
        x1[part, :] = total
        gz[part, :] = total.astype(BF)

    tiles(rows // step, step, back_two)

    def row_half(j):
        return ht[pl.ds(pl.multiple_of(lax.rem(j, 2) * TILE, TILE), TILE), :]

    def wide(j):
        return pl.ds(pl.multiple_of(lax.div(j, 2) * WIDE, WIDE), WIDE)

    def up_product(j):
        return dot_nn(row_half(j), flat(gp, wide(j)))

    def target(ref, first):
        def of(j, i):
            cols = pl.ds(pl.multiple_of(first + lax.div(j, 2) * WIDE, WIDE), WIDE)
            return ref.at[2 * lax.rem(j, 2) + i // 2, i % 2, :, :, cols]

        return of

    rs.tick(3)
    begin(outs[3])
    maker.run(
        2 * ups, up_product, row_blocks, target(a, 0), {2: rs_begin(4), 3: rs_tick(4), 4: rs_begin(5), 6: rs_begin(6)}
    )
    maker.flush()
    rs.stage(7, 0)
    for pair in outs:
        end(pair)
    load_block(14, 3).wait()
    for i in range(2):
        go[:, pl.ds(i * TILE, TILE)] = dot_nt(gz[...], block(3, pl.ds(2 * i, 2))).astype(BF)
    pick = (
        lax.broadcasted_iota(jnp.int32, (H, d), 1) // HD == lax.broadcasted_iota(jnp.int32, (H, d), 0)
    ).astype(BF)
    for i in range(4):
        part = pl.ds(i * quarter, quarter)
        prod = go[part, :].astype(F32) * att[part, :].astype(F32)
        high = prod.astype(BF)
        low = (prod - high.astype(F32)).astype(BF)
        deltat[:, part] = dot_nt(pick, high) + dot_nt(pick, low)
    low_cols, high_cols = pl.ds(0, SHARED * PAIR), pl.ds(SHARED * PAIR, d - SHARED * PAIR)
    high_cols2 = pl.ds(d + SHARED * PAIR, d - SHARED * PAIR)
    low_cols2 = pl.ds(d, SHARED * PAIR)

    lends = [
        between(9, qkv.at[:, high_cols], cross.at[:, high_cols]),
        between(15, go.at[:, high_cols], cross.at[:, high_cols2]),
        between(16, lset, far_lse),
        between(10, deltat, far_delta),
    ]
    gives = [
        between(11, cross.at[:, low_cols], cross.at[:, low_cols]),
        between(12, cross.at[:, low_cols2], cross.at[:, low_cols2]),
    ]
    returns = between(13, cross.at[:, high_cols], cross.at[:, high_cols])

    @pl.when(c == 1)
    def _():
        for copy in lends:
            copy.start()

    rs.tick(5)
    ht[...] = att[...].T
    maker.run(2, lambda j: dot_nn(row_half(j), gz[...]), row_blocks, target(gp, 3 * d))
    fill_bias(bias, pre[0:1, 0:1], c, True)

    @pl.when(c == 0)
    def _():
        for copy in lends:
            copy.wait_recv()

    @pl.when(c == 1)
    def _():
        for copy in lends:
            copy.wait_send()

    def give_back():
        @pl.when(c == 1)
        def _():
            for copy in gives:
                copy.start()

    def return_queries():
        @pl.when(c == 0)
        def _():
            returns.start()

    def flush_tick():
        maker.flush()
        rs.stage(8, 0)
        rs.tick(6)

    hooks = {0: flush_tick, 2: return_queries, 3: rs_tick(7), 4: give_back, 6: rs_tick(8)}
    attend_backward(c, qkv, cross, bias, lset, deltat, far_lse, far_delta, go, narrow, narrow2, gh, hooks)
    ht[...] = h1[...].T

    @pl.when(c == 1)
    def _():
        for copy in gives:
            copy.wait_send()
        returns.wait_recv()

        def add(j, part):
            qkv[part, high_cols] = (qkv[part, high_cols].astype(F32) + cross[part, high_cols].astype(F32)).astype(BF)

        tiles(rows // step, step, add)

    @pl.when(c == 0)
    def _():
        returns.wait_send()
        for copy in gives:
            copy.wait_recv()

        def add(j, part):
            for base in (0, d):
                to, src = pl.ds(d + base, SHARED * PAIR), pl.ds(base, SHARED * PAIR)
                qkv[part, to] = (qkv[part, to].astype(F32) + cross[part, src].astype(F32)).astype(BF)

        tiles(rows // step, step, add)

    def mixed_cols(j):
        return pl.ds(pl.multiple_of(lax.rem(lax.div(j, 2) + 1, 3) * d, d), d)

    def mixed_target(j, i):
        return gp.at[2 * lax.rem(j, 2) + i // 2, i % 2, :, :, mixed_cols(j)]

    maker.run(
        6, lambda j: dot_nn(row_half(j), qkv[:, mixed_cols(j)]), row_blocks, mixed_target, {1: rs_tick(9), 2: rs_begin(9), 4: rs_begin(10)}
    )
    maker.flush()
    rs.stage(11, 0)
    rs.stage(12, 0)
    rs.tick(10)
    for i, b in enumerate((0, 1, 2)):
        load_block(15 + i, b).wait()
    for i in range(2):
        total = None
        for b in range(3):
            part = dot_nt(qkv[:, pl.ds(b * d, d)], block(b, pl.ds(2 * i, 2)))
            total = part if total is None else total + part
        gh[:, pl.ds(i * TILE, TILE)] = total
        if i == 1:
            rs.tick(11)

    def back_one(j, part):
        nrm, scale = normalise(x[part, :].astype(F32))
        g = gh[part, :]
        collect(0, g * nrm)
        collect(2, g)
        total = x1[part, :] + norm_back(g, nrm, scale, par[0:1, :])
        gh[part, :] = total
        gz[part, :] = total.astype(BF)

    tiles(rows // step, step, back_one)
    backs = []
    for i, q in enumerate(quarters):
        backs.append(
            (
                pltpu.make_async_copy(gh.at[q], gi.at[q], io_sem.at[4 + i]),
                remote(gz.at[q], gl.at[q], io_sem.at[4 + i], io_recv.at[4 + i], far),
            )
        )
    begin(backs[0])
    for i in range(4):
        par[i : i + 1, :] = jnp.sum(acc[i], 0, keepdims=True)
    for t in range(d // PAIR):
        row = par[:, pl.ds(t * PAIR, PAIR)].astype(BF)
        for k in range(2):
            spar[t // 2, t % 2, k] = row
            ptheirs[t // 2, t % 2, k] = row
    pars = remote(ptheirs, pland, io_sem.at[8], io_recv.at[8], core)
    pars.start()
    rs.stage(11, 1)
    pars.wait_recv()
    add_blocks(spar, [pland])
    rs.stage(n, 0)
    begin(backs[1])
    for i, st in ((12, 1), (10, 2), (9, 3)):
        rs.stage(i, st)
    begin(backs[2])
    for i, st in ((n, 1), (11, 2), (12, 2)):
        rs.stage(i, st)
    begin(backs[3])
    for i, st in ((10, 3), (n, 2), (11, 3), (12, 3), (n, 3)):
        rs.stage(i, st)
    for pair in backs:
        end(pair)
    pars.wait_send()
    for i in range(len(chunks)):
        ag.finish(i)
    for i in range(n + 1):
        rs.finish(i)
    maker.finish()


def layer(nz, frames_in, cot, pre, w_qkv, w_out, w_up, w_down, tile):
    rows, d = frames_in.shape
    ff = w_up.shape[1]
    S = jax.ShapeDtypeStruct
    V = pltpu.VMEM
    REG = pltpu.SemaphoreType.REGULAR
    hbm, vm = pl.BlockSpec(memory_space=pl.ANY), pl.BlockSpec(memory_space=V)
    shards = (w_qkv, w_out, w_up, w_down, tile)
    parts = (nz, 2, 2, BLOCK)
    full = (nz, 2, 2, 2)
    return pl.pallas_call(
        functools.partial(layer_kernel, nz),
        out_shape=[S((rows, d), BF), S((rows, d), F32), S((rows, d), BF)]
        + [S(full + w.shape, BF) for w in shards]
        + [S(w.shape, F32) for w in shards],
        in_specs=[hbm] * 8,
        out_specs=[hbm] * 8 + [vm] * 5,
        scratch_shapes=[
            V((rows, d), BF), V((rows, d), BF), V((8, PAIR), jnp.int32), V((rows, d), BF), V((rows, 3 * d), BF),
            V((rows, 2 * d), BF), V((rows, d), BF), V((rows, d), F32), V((rows, d), BF),
            V(parts + (ff,), BF), V(parts + (ff,), BF),
            V(full + w_down.shape, BF), V(full + w_up.shape, BF),
            V((rows, d), F32), V((rows, d), BF), V((rows, d), BF), V((rows, rows), F32), V((rows, PAIR), F32), V((rows, PAIR), F32),
            V((H, rows), F32), V((H, rows), F32), V((H, rows), F32), V((H, rows), F32), V((4, 8, d), F32), V((16, d), F32), V(full + (16, PAIR), BF),
            V((d, rows), BF), V((2, 4, 2, 2, BLOCK, WIDE), BF), V((2, 4, 2, BLOCK, WIDE), BF),
            V((4,) + parts + (d,), BF), V((nz, 2, 2, 16, PAIR), BF), V((nz, 2, 2, 16, PAIR), BF), V((nz, 2, 2, 16, PAIR), BF),
            V((RING, nz, 2, BLOCK, WIDE), BF), V((RING, 7, BLOCK, WIDE), BF), V((nz, 2, 16, PAIR), BF), V((7, 16, PAIR), BF),
        ]
        + Gather.sem_shapes(15)
        + Scatter.sem_shapes(14)
        + [DMA((2,)), DMA((2,)), REG((2,)), DMA((18,)), DMA((17, 3)), DMA((9,)), DMA((9,))],
        compiler_params=pltpu.CompilerParams(collective_id=0, has_side_effects=True, vmem_limit_bytes=63 * 2**20),
    )(frames_in, cot, pre, *shards)


def settle_kernel(fo, gi, gl, g_qkv, g_out, g_up, g_down, g_par, fo_, gi_, qkv_, out_, up_, down_, gains_, shifts_, narrow, wide, *rest):
    straight = lax.rem(lax.axis_index("dp"), 2) == lax.axis_index("fsdp")
    stops, sems = rest[:5], rest[5]
    pairs = ((fo, fo_), (g_qkv, qkv_), (g_out, out_), (g_up, up_), (g_down, down_))
    ins = [pltpu.make_async_copy(src, stop, sems.at[0, i]) for i, ((src, _), stop) in enumerate(zip(pairs, stops))]
    outs = [pltpu.make_async_copy(stop, dst, sems.at[1, i]) for i, ((_, dst), stop) in enumerate(zip(pairs, stops))]
    rows = gi.shape[0] // 4
    parts = [pl.ds(i * rows, rows) for i in range(4)]
    own = [pltpu.make_async_copy(gi.at[p], wide.at[p], sems.at[2, i]) for i, p in enumerate(parts)]
    came = [pltpu.make_async_copy(gl.at[p], narrow.at[p], sems.at[2, i]) for i, p in enumerate(parts)]
    puts = [pltpu.make_async_copy(wide.at[p], gi_.at[p], sems.at[3, i]) for i, p in enumerate(parts)]

    @pl.when(straight)
    def _():
        for get in own:
            get.start()

    @pl.when(jnp.logical_not(straight))
    def _():
        for get in came:
            get.start()

    for copy in ins:
        copy.start()
    width = gains_.shape[1]
    mine = lax.rem(lax.axis_index("dp") * 2 + lax.axis_index("fsdp"), PAIR // width)
    small = g_par[:, pl.ds(0, width)]
    for i in range(1, PAIR // width):
        small = jnp.where(mine == i, g_par[:, pl.ds(i * width, width)], small)
    gains_[...] = small[0:2]
    shifts_[...] = small[2:4]

    @pl.when(straight)
    def _():
        for get, put in zip(own, puts):
            get.wait()
            put.start()

    @pl.when(jnp.logical_not(straight))
    def _():
        for get, put, p in zip(came, puts, parts):
            get.wait()
            wide[p, :] = narrow[p, :].astype(F32)
            put.start()

    for get, put in zip(ins, outs):
        get.wait()
        put.start()
    for put in puts + outs:
        put.wait()


def settle(width, fo, gi, gl, *grads):
    S = jax.ShapeDtypeStruct
    V = pltpu.VMEM
    hbm, vm = pl.BlockSpec(memory_space=pl.ANY), pl.BlockSpec(memory_space=V)
    kept = (fo, gi) + grads[:4]
    return pl.pallas_call(
        settle_kernel,
        out_shape=[S(v.shape, v.dtype) for v in kept] + [S((2, width), F32)] * 2,
        in_specs=[hbm] * 7 + [vm],
        out_specs=[hbm] * 6 + [vm] * 2,
        scratch_shapes=[V(gl.shape, BF), V(gi.shape, F32)] + [V(v.shape, v.dtype) for v in (fo,) + grads[:4]] + [DMA((4, 5))],
        compiler_params=pltpu.CompilerParams(vmem_limit_bytes=VMEM_LIMIT),
    )(fo, gi, gl, *grads)


def norm_rows(values, gain, shift):
    center = values - jnp.mean(values, -1, keepdims=True)
    spread = jnp.mean(center * center, -1, keepdims=True)
    return center * lax.rsqrt(spread + EPS) * gain + shift


def collect(w_qkv, w_out, w_up, w_down, gains, shifts):
    return (
        lax.all_gather(w_qkv, ("dp", "fsdp"), axis=0, tiled=True),
        lax.all_gather(w_out, ("dp", "fsdp"), axis=0, tiled=True),
        lax.all_gather(w_up, ("dp", "fsdp"), axis=0, tiled=True),
        lax.all_gather(w_down, ("dp", "fsdp"), axis=0, tiled=True),
        lax.all_gather(gains, ("dp", "fsdp"), axis=1, tiled=True),
        lax.all_gather(shifts, ("dp", "fsdp"), axis=1, tiled=True),
    )


def split_heads(matrix):
    return matrix.reshape(matrix.shape[0], H, HD).transpose(1, 0, 2)


def join_heads(stacked):
    return stacked.transpose(1, 0, 2).reshape(stacked.shape[1], H * HD)


def masked_scores(query_one, key_one, allowed):
    scores = jnp.dot(query_one, key_one.T, preferred_element_type=jnp.float32) * 0.125
    return jnp.where(allowed, scores, -1e30)


def forward(inputs, weights, allowed):
    w_qkv, w_out, w_up, w_down, gains, shifts = weights
    width = inputs.shape[1]
    gain_rows = gains.astype(jnp.float32)
    shift_rows = shifts.astype(jnp.float32)
    normed = norm_rows(inputs, gain_rows[0], shift_rows[0]).astype(jnp.bfloat16)
    mixed = jnp.dot(normed, w_qkv, preferred_element_type=jnp.float32).astype(jnp.bfloat16)
    queries = mixed[:, :width]
    keys_all, values_all = (
        lax.all_gather(mixed[:, width : 2 * width], "fsdp", axis=0, tiled=True),
        lax.all_gather(mixed[:, 2 * width :], "fsdp", axis=0, tiled=True),
    )
    query_heads = split_heads(queries)
    key_heads = split_heads(keys_all)
    value_heads = split_heads(values_all)

    def single(pieces):
        scores = masked_scores(pieces[0], pieces[1], allowed)
        peak_row = jnp.max(scores, -1, keepdims=True)
        log_total = peak_row + jnp.log(jnp.sum(jnp.exp(scores - peak_row), -1, keepdims=True))
        chance = jnp.exp(scores - log_total).astype(jnp.bfloat16)
        return (jnp.dot(chance, pieces[2], preferred_element_type=jnp.float32), log_total[:, 0])

    outputs, totals = lax.map(single, (query_heads, key_heads, value_heads))
    attended = join_heads(outputs).astype(jnp.bfloat16)
    middle = inputs + jnp.dot(attended, w_out, preferred_element_type=jnp.float32)
    normed_two = norm_rows(middle, gain_rows[1], shift_rows[1]).astype(jnp.bfloat16)
    hidden = jnp.dot(normed_two, w_up, preferred_element_type=jnp.float32)
    active = jax.nn.gelu(hidden, approximate=False).astype(jnp.bfloat16)
    result = middle + jnp.dot(active, w_down, preferred_element_type=jnp.float32)
    saved = (
        normed,
        query_heads,
        key_heads,
        value_heads,
        totals,
        attended,
        middle,
        normed_two,
        hidden,
        active,
    )
    return (result, saved)


def on_device(frames_in, prefix_len, w_qkv, w_out, w_up, w_down, gains, shifts, cotangent):
    inputs = frames_in[0].astype(jnp.float32)
    rows_here = inputs.shape[0]
    frames_all = rows_here * lax.axis_size("fsdp")
    first_row = lax.axis_index("fsdp") * rows_here
    places = first_row + jnp.arange(rows_here, dtype=jnp.int32)
    columns = jnp.arange(frames_all, dtype=jnp.int32)
    allowed = (columns[None, :] <= places[:, None]) | (columns[None, :] < prefix_len[0])
    weights = collect(w_qkv, w_out, w_up, w_down, gains, shifts)
    result, saved = forward(inputs, weights, allowed)
    weights = collect(w_qkv, w_out, w_up, w_down, gains, shifts)
    saved = forward(inputs, weights, allowed)[1]
    full_qkv, full_out, full_up, full_down, full_gains, full_shifts = weights
    (
        normed,
        query_heads,
        key_heads,
        value_heads,
        totals,
        attended,
        middle,
        normed_two,
        hidden,
        active,
    ) = saved
    gain_rows = full_gains.astype(jnp.float32)
    shift_rows = full_shifts.astype(jnp.float32)
    grad_top = cotangent[0].astype(jnp.float32)
    grad_branch = grad_top.astype(jnp.bfloat16)
    part_down = jnp.dot(active.T, grad_branch, preferred_element_type=jnp.float32)
    grad_active = jnp.dot(grad_branch, full_down.T, preferred_element_type=jnp.float32)
    gelu_pull = jax.vjp(functools.partial(jax.nn.gelu, approximate=False), hidden)[1]
    grad_hidden = gelu_pull(grad_active)[0].astype(jnp.bfloat16)
    part_up = jnp.dot(normed_two.T, grad_hidden, preferred_element_type=jnp.float32)
    grad_normed_two = jnp.dot(grad_hidden, full_up.T, preferred_element_type=jnp.float32)
    norm_pull_two = jax.vjp(norm_rows, middle, gain_rows[1], shift_rows[1])[1]
    back_middle, grad_gain_two, grad_shift_two = norm_pull_two(grad_normed_two)
    grad_middle = grad_top + back_middle
    grad_attn_out = grad_middle.astype(jnp.bfloat16)
    part_out = jnp.dot(attended.T, grad_attn_out, preferred_element_type=jnp.float32)
    grad_attended = jnp.dot(grad_attn_out, full_out.T, preferred_element_type=jnp.float32).astype(
        jnp.bfloat16
    )
    grad_att_heads = split_heads(grad_attended)

    def single_back(pieces):
        query_one, key_one, value_one, grad_one, log_total = pieces
        scores = masked_scores(query_one, key_one, allowed)
        chance = jnp.exp(scores - log_total[:, None])
        grad_chance = jnp.dot(grad_one, value_one.T, preferred_element_type=jnp.float32)
        inner = jnp.sum(chance * grad_chance, -1, keepdims=True)
        grad_scores = (chance * (grad_chance - inner)).astype(jnp.bfloat16)
        grad_query = jnp.dot(grad_scores, key_one, preferred_element_type=jnp.float32) * 0.125
        grad_key = (
            jnp.einsum("qk,qd->kd", grad_scores, query_one, preferred_element_type=jnp.float32)
            * 0.125
        )
        grad_value = jnp.einsum(
            "qk,qd->kd", chance.astype(jnp.bfloat16), grad_one, preferred_element_type=jnp.float32
        )
        return (grad_query, grad_key, grad_value)

    grad_q_heads, grad_k_heads, grad_v_heads = lax.map(
        single_back, (query_heads, key_heads, value_heads, grad_att_heads, totals)
    )
    grad_keys, grad_values = (
        lax.psum_scatter(
            join_heads(grad_k_heads).astype(jnp.bfloat16), "fsdp", scatter_dimension=0, tiled=True
        ).astype(jnp.float32),
        lax.psum_scatter(
            join_heads(grad_v_heads).astype(jnp.bfloat16), "fsdp", scatter_dimension=0, tiled=True
        ).astype(jnp.float32),
    )
    grad_mixed = jnp.concatenate([join_heads(grad_q_heads), grad_keys, grad_values], 1).astype(
        jnp.bfloat16
    )
    part_qkv = jnp.dot(normed.T, grad_mixed, preferred_element_type=jnp.float32)
    grad_normed = jnp.dot(grad_mixed, full_qkv.T, preferred_element_type=jnp.float32)
    norm_pull_one = jax.vjp(norm_rows, inputs, gain_rows[0], shift_rows[0])[1]
    back_inputs, grad_gain_one, grad_shift_one = norm_pull_one(grad_normed)
    grad_inputs = grad_middle + back_inputs
    part_gains = jnp.stack([grad_gain_one, grad_gain_two])
    part_shifts = jnp.stack([grad_shift_one, grad_shift_two])
    owned = (
        lax.psum_scatter(part_qkv, ("dp", "fsdp"), scatter_dimension=0, tiled=True),
        lax.psum_scatter(part_out, ("dp", "fsdp"), scatter_dimension=0, tiled=True),
        lax.psum_scatter(part_up, ("dp", "fsdp"), scatter_dimension=0, tiled=True),
        lax.psum_scatter(part_down, ("dp", "fsdp"), scatter_dimension=0, tiled=True),
        lax.psum_scatter(part_gains, ("dp", "fsdp"), scatter_dimension=1, tiled=True),
        lax.psum_scatter(part_shifts, ("dp", "fsdp"), scatter_dimension=1, tiled=True),
    )
    return (
        result.astype(jnp.bfloat16)[None],
        grad_inputs[None],
        owned[0],
        owned[1],
        owned[2],
        owned[3],
        owned[4],
        owned[5],
    )


def fast_device(ndp, frames_in, prefix_len, w_qkv, w_out, w_up, w_down, gains, shifts, cotangent):
    here = lax.axis_index("dp") * 2 + lax.axis_index("fsdp")
    width = gains.shape[1]
    per = PAIR // width
    rows = jnp.concatenate([gains, shifts, jnp.zeros((12, width), BF)], 0)
    tile = jnp.where(lax.broadcasted_iota(jnp.int32, (16, per, width), 1) == here % per, rows[:, None], 0.0)
    tile = tile.astype(BF).reshape(16, PAIR)
    pre = jnp.broadcast_to(prefix_len[None], (8, PAIR))
    result = layer(ndp // 4, frames_in[0], cotangent[0], pre, w_qkv, w_out, w_up, w_down, tile)
    frames_out, grad_in, *owned = settle(width, *result[:3], *result[8:])
    return (frames_out[None], grad_in[None]) + tuple(owned)


def solution(mesh):
    ndp, nf = mesh.shape["dp"], mesh.shape["fsdp"]
    both = P(("dp", "fsdp"), None)
    lanes = P(None, ("dp", "fsdp"))
    block = P("dp", "fsdp", None)
    body = functools.partial(fast_device, ndp) if (nf == 2 and ndp == 16) else on_device
    return jax.shard_map(
        body,
        mesh=mesh,
        in_specs=(block, P("dp"), both, both, both, both, lanes, lanes, block),
        out_specs=(block, block, both, both, both, both, lanes, lanes),
        check_vma=False,
    )
```

```python
import functools
import math

import jax
import jax.numpy as jnp
from jax import lax
from jax.experimental import pallas as pl
from jax.experimental.pallas import tpu as pltpu
from jax.sharding import PartitionSpec as P

H = 16
HD = 64
EPS = 1e-05
BF = jnp.bfloat16
F32 = jnp.float32
LOG2E = math.log2(math.e)
SCALE2 = 0.125 * LOG2E
PAIR = 2 * HD
TILE = 512
MESH = pl.DeviceIdType.MESH
DMA = pltpu.SemaphoreType.DMA
VMEM_LIMIT = 60 * 2**20


def coords():
    dp, f = lax.axis_index("dp"), lax.axis_index("fsdp")
    q = lax.div(dp, 2)
    return lax.div(q, 2), lax.rem(q, 2), lax.rem(dp, 2), f


def dev(z, y, c, f):
    return ((z * 2 + y) * 2 + c, f)


def remote(src, dst, send, recv, device):
    return pltpu.make_async_remote_copy(
        src_ref=src, dst_ref=dst, send_sem=send, recv_sem=recv, device_id=device, device_id_type=MESH
    )


def greet(peers):
    barrier = pltpu.get_barrier_semaphore()
    for peer in peers:
        pl.semaphore_signal(barrier, inc=1, device_id=peer, device_id_type=MESH)
    pl.semaphore_wait(barrier, len(peers))


def all_peers(nz, z, y, c, f):
    peers = [dev(lax.rem(z + k, nz), y, c, f) for k in range(1, nz)]
    return peers + [dev(z, 1 - y, c, f), dev(z, y, c, 1 - f), dev(z, y, 1 - c, f)]


def dot_nn(a, b):
    return lax.dot_general(a, b, (((1,), (0,)), ((), ())), preferred_element_type=F32)


def dot_nt(a, b):
    return lax.dot_general(a, b, (((1,), (1,)), ((), ())), preferred_element_type=F32)


def dot_tn(a, b):
    return lax.dot_general(a, b, (((0,), (0,)), ((), ())), preferred_element_type=F32)


def normalise(v):
    center = v - jnp.mean(v, -1, keepdims=True)
    scale = lax.rsqrt(jnp.mean(center * center, -1, keepdims=True) + EPS)
    return center * scale, scale


def lane_half():
    return lax.broadcasted_iota(jnp.int32, (1, PAIR), 1) // HD


def fill_bias(bias, prefix, c, transposed):
    rows = bias.shape[0]
    step = 64

    def body(j, part):
        a = lax.broadcasted_iota(jnp.int32, (step, rows), 0) + j * step
        b = lax.broadcasted_iota(jnp.int32, (step, rows), 1)
        row, key = (b, a) if transposed else (a, b)
        bias[part, :] = jnp.where((key <= row) | (key + c * rows < prefix), 0.0, -1e30)

    tiles(rows // step, step, body)


def norm_back(gh, n, scale, gain):
    gn = gh * gain
    return scale * (gn - jnp.mean(gn, -1, keepdims=True) - n * jnp.mean(gn * n, -1, keepdims=True))


class Gather:
    def __init__(self, nz, place, shards, outs, chunks, sems):
        self.nz, self.place, self.shards, self.outs, self.chunks = nz, place, shards, outs, chunks
        self.send, self.recv, self.own = sems

    @staticmethod
    def sem_shapes(n):
        return [DMA((n, 12)), DMA((n, 12)), DMA((n,))]

    def mine(self, i):
        w, r0, r, c0, n = self.chunks[i]
        return self.shards[w].at[pl.ds(r0, r), pl.ds(c0, n)]

    def at(self, i, *where):
        w, r0, r, c0, n = self.chunks[i]
        where += (slice(None),) * (4 - len(where))
        return self.outs[w].at[where + (pl.ds(r0, r), pl.ds(c0, n))]

    def hop(self, i, slot, src, dst, device):
        return remote(src, dst, self.send.at[i, slot], self.recv.at[i, slot], device)

    def copies(self, i):
        z, y, c, f = self.place
        nz = self.nz
        every = slice(None)
        core, xp, yp = dev(z, y, 1 - c, f), dev(z, y, c, 1 - f), dev(z, 1 - y, c, f)
        mine, home = self.mine(i), self.at(i, z, y, c, f)

        def same(slot, ref, device):
            return self.hop(i, slot, ref, ref, device)

        zs = [dev(lax.rem(z + k, nz), y, c, f) for k in range(1, nz)]
        line = self.at(i, every, y, c, f)
        other = self.at(i, every, 1 - y, c, f)
        zero = {
            0: [self.hop(i, k, mine, home, zs[k]) for k in range(nz - 1)],
            1: [same(3, line, yp), same(4, line, xp), same(8, line, core)],
            2: [same(5, other, xp), same(9, other, core)],
            3: [same(10, self.at(i, every, every, c, 1 - f), core)],
        }
        rows = self.at(i, z, y, c)
        plane = self.at(i, every, y, c)
        one = {
            0: [self.hop(i, 3, mine, home, xp)],
            1: [same(k, rows, zs[k]) for k in range(nz - 1)],
            2: [same(4, plane, yp), same(8, plane, core)],
            3: [same(9, self.at(i, every, 1 - y, c), core)],
        }
        return zero, one

    def arrivals(self, i):
        z, y, c, f = self.place
        nz = self.nz
        every = slice(None)
        zk = [lax.rem(z + nz - k, nz) for k in range(1, nz)]
        core = dev(z, y, 1 - c, f)

        def here(slot, *where):
            ref = self.at(i, *where)
            return self.hop(i, slot, ref, ref, core)

        zero = {
            1: [here(k, zk[k], y, c, f) for k in range(nz - 1)],
            2: [here(3, every, 1 - y, c, f)],
            3: [here(4, every, y, c, 1 - f), here(5, every, 1 - y, c, 1 - f)],
            4: [here(8, every, y, 1 - c), here(9, every, 1 - y, 1 - c)],
        }
        one = {
            1: [here(3, z, y, c, 1 - f)],
            2: [here(k, zk[k], y, c) for k in range(nz - 1)],
            3: [here(4, every, 1 - y, c)],
            4: [here(8, every, y, 1 - c, f), here(9, every, 1 - y, 1 - c, f), here(10, every, every, 1 - c, 1 - f)],
        }
        return zero, one

    def local(self, i):
        z, y, c, f = self.place
        return pltpu.make_async_copy(self.mine(i), self.at(i, z, y, c, f), self.own.at[i])

    def stage(self, i, s):
        if s == 1:
            self.local(i).wait()
        for core in range(2):

            @pl.when(self.place[2] == core)
            def _():
                if s:
                    for copy in self.arrivals(i)[core][s]:
                        copy.wait_recv()
                if s < 4:
                    for copy in self.copies(i)[core][s]:
                        copy.start()

    def tick(self, t, stages=(0, 1, 2, 3)):
        for s in stages:
            if 0 <= t - s < len(self.chunks):
                self.stage(t - s, s)

    def finish(self, i):
        for core in range(2):

            @pl.when(self.place[2] == core)
            def _():
                for copies in self.copies(i)[core].values():
                    for copy in copies:
                        copy.wait_send()


RING = 6
BLOCK = 32
WIDE = 1024


def tiles(count, size, body, hooks=None):
    @pl.loop(0, count)
    def _(j):
        body(j, pl.ds(pl.multiple_of(j * size, size), size))
        run_hooks(j, hooks)


def run_hooks(j, hooks):
    for at, hook in (hooks or {}).items():

        @pl.when(j == at)
        def _():
            hook()


def flat(ref, cols):
    v = ref[:, :, :, :, cols]
    return v.reshape(math.prod(v.shape[:-1]), v.shape[-1])


def add_blocks(dst, parts, out=None):
    lead, n = dst.shape[:-2], dst.shape[-1]
    size = min(n, 256)

    @pl.loop(0, math.prod(lead) * (n // size))
    def _(j):
        cols = pl.ds(pl.multiple_of(lax.rem(j, n // size) * size, size), size)
        at, rest = [], lax.div(j, n // size)
        for count in reversed(lead):
            at.insert(0, lax.rem(rest, count))
            rest = lax.div(rest, count)
        at = tuple(at) + (slice(None), cols)
        total = dst[at].astype(F32)
        for p in parts:
            total = total + p[at].astype(F32)
        if out is None:
            dst[at] = total.astype(dst.dtype)
        else:
            out[at] = total


class Scatter:
    def __init__(self, nz, place, sums, second, third, outs, sems):
        self.nz, self.place, self.sums, self.second, self.third = nz, place, sums, second, third
        self.outs, self.done = outs, set()
        self.send, self.recv, self.free = sems

    @staticmethod
    def sem_shapes(n):
        return [DMA((n, 5)), DMA((n, 5)), pltpu.SemaphoreType.REGULAR((RING,))]

    def peers(self):
        z, y, c, f = self.place
        zs = [dev(lax.rem(z + k, self.nz), y, c, f) for k in range(1, self.nz)]
        return zs, dev(z, 1 - y, c, f), dev(z, y, c, 1 - f)

    def hop(self, i, slot, src, dst, device):
        return remote(src, dst, self.send.at[i, slot], self.recv.at[i, slot], device)

    def copies(self, i):
        z, y, c, f = self.place
        s, b2, b3, nz = self.sums[i], self.second[i], self.third[i], self.nz
        zs, yp, xp = self.peers()
        zt = [lax.rem(z + k, nz) for k in range(1, nz)]
        zero = {
            0: [self.hop(i, 0, s.at[:, :, 1 - f], b2, xp)],
            1: [self.hop(i, 1, s.at[:, 1 - y, f], b3.at[pl.ds(0, nz)], yp)],
            2: [self.hop(i, 2 + k, s.at[zt[k], y, f], b3.at[nz + k], zs[k]) for k in range(nz - 1)],
        }
        one = {
            0: [self.hop(i, 0, s.at[:, 1 - y], b2, yp)],
            1: [self.hop(i, 1 + k, s.at[zt[k], y], b3.at[pl.ds(2 * k, 2)], zs[k]) for k in range(nz - 1)],
            2: [self.hop(i, nz, s.at[z, y, 1 - f], b3.at[2 * (nz - 1)], xp)],
        }
        return zero, one

    def stage(self, i, st):
        z, y, c, f = self.place
        nz = self.nz
        self.done.add((i, st))
        s, b2, b3 = self.sums[i], self.second[i], self.third[i]
        copies = self.copies(i)
        zs, yp, xp = self.peers()
        ringed = i < len(self.sums) - 1
        if st == 0 and ringed and i >= RING:
            pl.semaphore_wait(self.free.at[i % RING], nz + 1)

        @pl.when(c == 0)
        def _():
            if st:
                for copy in copies[0][st - 1]:
                    copy.wait_recv()
            if st == 0:
                copies[0][0][0].start()
            if st == 1:
                add_blocks(s.at[:, 1 - y, f], [b2.at[:, 1 - y]])
                copies[0][1][0].start()
                add_blocks(s.at[:, y, f], [b2.at[:, y]])
            if st == 2:
                for k in range(nz - 1):
                    zt = lax.rem(z + k + 1, nz)
                    add_blocks(s.at[zt, y, f], [b3.at[zt]])
                    copies[0][2][k].start()
                add_blocks(s.at[z, y, f], [b3.at[z]])
            if st == 3:
                add_blocks(s.at[z, y, f], [b3.at[nz + k] for k in range(nz - 1)], self.outs[i])

        @pl.when(c == 1)
        def _():
            if st:
                for copy in copies[1][st - 1]:
                    copy.wait_recv()
            if st == 0:
                copies[1][0][0].start()
            if st == 1:
                for k in range(nz - 1):
                    zt = lax.rem(z + k + 1, nz)
                    add_blocks(s.at[zt, y], [b2.at[zt]])
                    copies[1][1][k].start()
                add_blocks(s.at[z, y], [b2.at[z]])
            if st == 2:
                add_blocks(s.at[z, y, 1 - f], [b3.at[2 * k + 1 - f] for k in range(nz - 1)])
                copies[1][2][0].start()
                add_blocks(s.at[z, y, f], [b3.at[2 * k + f] for k in range(nz - 1)])
            if st == 3:
                add_blocks(s.at[z, y, f], [b3.at[2 * (nz - 1)]], self.outs[i])

        if st == 3 and ringed and i + RING < len(self.sums) - 1:
            for peer in zs + [yp, xp]:
                pl.semaphore_signal(self.free.at[i % RING], inc=1, device_id=peer, device_id_type=MESH)

    def tick(self, t):
        for st in range(1, 4):
            i = t - st
            if (i, st - 1) in self.done and (i, st) not in self.done:
                self.stage(i, st)

    def finish(self, i):
        for core in range(2):

            @pl.when(self.place[2] == core)
            def _():
                for copies in self.copies(i)[core].values():
                    for copy in copies:
                        copy.wait_send()


class Producer:
    def __init__(self, place, buf, land, sems):
        self.place, self.buf, self.land = place, buf, land
        self.send, self.recv, self.credit = sems
        z, y, c, f = place
        self.core = dev(z, y, 1 - c, f)
        self.made, self.pending = 0, None

    def copy(self, slot):
        theirs = self.buf.at[slot, :, 1 - self.place[2]]
        return remote(theirs, self.land.at[slot], self.send.at[slot], self.recv.at[slot], self.core)

    def before(self, slot):
        self.copy(slot).wait_send()
        pl.semaphore_wait(self.credit.at[slot], 1)

    def absorb(self, j, target):
        c = self.place[2]
        slot = lax.rem(j, 2)
        self.copy(slot).wait_recv()
        for i in range(4):
            ref = target(j, i)
            for k in range(2):
                ref[k] = (self.buf[slot, i, c, k].astype(F32) + self.land[slot, i, k].astype(F32)).astype(BF)
        pl.semaphore_signal(self.credit.at[slot], inc=1, device_id=self.core, device_id_type=MESH)

    def flush(self):
        if self.pending is not None:
            self.absorb(*self.pending)
            self.pending = None

    def run(self, count, product, where, target, hooks=None):
        fresh, pending = self.made == 0, self.pending

        @pl.loop(0, count)
        def _(j):
            slot = lax.rem(j, 2)
            if not fresh:
                self.before(slot)
            elif count > 2:

                @pl.when(j >= 2)
                def _():
                    self.before(slot)

            v = product(j)
            for i in range(4):
                for k in range(2):
                    for core in range(2):
                        at = where(i, core, k)
                        self.buf[slot, i, core, k] = v[at : at + BLOCK].astype(BF)
            self.copy(slot).start()
            if pending is not None:

                @pl.when(j == 0)
                def _():
                    self.absorb(*pending)

            @pl.when(j >= 1)
            def _():
                self.absorb(j - 1, target)

            run_hooks(j, hooks)

        self.made += count
        self.pending = (count - 1, target)

    def finish(self):
        for slot in range(2):
            self.before(slot)


def row_blocks(i, core, k):
    return BLOCK * (4 * i + 2 * core + k)


def deep_blocks(i, core, k):
    return BLOCK * (8 * core + 4 * k + i)


def attend_forward(c, qkv, cross, bias, att, lse, hooks):
    rows, d = att.shape
    half = lane_half()
    lane = lax.broadcasted_iota(jnp.int32, (1, PAIR), 1)
    rt = rows // 2

    def one(q, blocks):
        scores = []
        for keys, _, extra in blocks:
            s = dot_nt(q, keys) * SCALE2
            scores.append(s if extra is None else s + extra)
        peak = functools.reduce(jnp.maximum, [jnp.max(s, -1, keepdims=True) for s in scores])
        total = None
        for s, (_, values, _) in zip(scores, blocks):
            part = dot_nn(jnp.exp2(s - peak).astype(BF), values)
            total = part if total is None else total + part
        return total, peak

    def pair(p, second):
        cols = pl.ds(pl.multiple_of(p * PAIR, PAIR), PAIR)
        kcols = pl.ds(pl.multiple_of(d + p * PAIR, PAIR), PAIR)
        vcols = pl.ds(pl.multiple_of(2 * d + p * PAIR, PAIR), PAIR)
        def half_rows(r, part):
            results = []
            for h in range(2):
                mine = half == h
                q = jnp.where(mine, qkv[part, cols], 0.0).astype(BF)

                def val(v):
                    return jnp.where(mine, v, 1.0).astype(BF)

                if second:
                    blocks = [(cross[:, cols], val(cross[:, kcols]), None)]
                    if r > 0:
                        blocks.append((qkv[pl.ds(0, rt), kcols], val(qkv[pl.ds(0, rt), vcols]), None))
                    blocks.append((qkv[part, kcols], val(qkv[part, vcols]), bias[part, pl.ds(r * rt, rt)]))
                else:
                    blocks = [(qkv[:, kcols], val(qkv[:, vcols]), bias[part, :])]
                total, peak = one(q, blocks)
                sums = pltpu.roll(total, HD, axis=1)
                results.append(total / sums)
                both = jnp.where(mine, sums, total)
                lse[part, :] = jnp.where(lane == 2 * p + h, peak + jnp.log2(both), lse[part, :])
            att[part, cols] = jnp.where(half == 0, results[0], results[1]).astype(BF)

        if second:
            for r in range(2):
                half_rows(r, pl.ds(r * rt, rt))
        else:
            tiles(2, rt, half_rows)

    @pl.loop(0, d // PAIR)
    def _(p):
        for second in range(2):

            @pl.when(c == second)
            def _():
                pair(p, second == 1)

        run_hooks(p, hooks)


SHARED = 5


def attend_backward(c, qkv, cross, biast, lset, deltat, far_lse, far_delta, go, gq, gq2, more, hooks):
    rows, d = go.shape
    half = lane_half()
    rt = rows // 2
    pairs = d // PAIR

    def term(p, keys, values, krows, qrows, queries, grads, lse, delta, masked, total):
        gk = gv = None
        for h in range(2):
            mine = half == h
            q = jnp.where(mine, queries, 0.0).astype(BF)
            g = jnp.where(mine, grads, 0.0).astype(BF)
            km = jnp.where(mine, keys, 0.0).astype(BF)
            s = dot_nt(keys, q) * SCALE2
            if masked:
                s = s + biast[krows, qrows]
            pr = jnp.exp2(s - lse[pl.ds(2 * p + h, 1), qrows])
            gs = (pr * (dot_nt(values, g) - delta[pl.ds(2 * p + h, 1), qrows])).astype(BF)
            k1, v1 = dot_nn(gs, q), dot_nn(pr.astype(BF), g)
            gk, gv = (k1, v1) if gk is None else (gk + k1, gv + v1)
            total[qrows, :] = total[qrows, :] + dot_tn(gs, km)
        return gk, gv

    every = pl.ds(0, rows)
    first, last = pl.ds(0, PAIR), pl.ds(PAIR, PAIR)

    @pl.loop(0, pairs)
    def _(i):
        @pl.when(c == 0)
        def _():
            heavy = i < pairs - SHARED
            p = lax.rem(i + SHARED, pairs)
            cols = pl.ds(pl.multiple_of(p * PAIR, PAIR), PAIR)
            kcols = pl.ds(pl.multiple_of(d + p * PAIR, PAIR), PAIR)
            vcols = pl.ds(pl.multiple_of(2 * d + p * PAIR, PAIR), PAIR)
            gq[...] = jnp.zeros_like(gq)

            @pl.when(heavy)
            def _():
                gq2[...] = jnp.zeros_like(gq2)

                def far_part(r, krows):
                    more[krows, first], more[krows, last] = term(
                        p, qkv[krows, kcols], qkv[krows, vcols], krows, every, cross[:, cols], cross[:, kcols], far_lse, far_delta, False, gq2
                    )

                tiles(2, rt, far_part)
                cross[:, cols] = (gq2[...] * 0.125).astype(BF)

            @pl.when(i == pairs - SHARED)
            def _():
                more[:, first] = jnp.zeros_like(gq)
                more[:, last] = jnp.zeros_like(gq)

            def own_part(r, krows):
                gk, gv = term(
                    p, qkv[krows, kcols], qkv[krows, vcols], krows, every, qkv[:, cols], go[:, cols], lset, deltat, True, gq
                )
                qkv[krows, kcols] = ((gk + more[krows, first]) * 0.125).astype(BF)
                qkv[krows, vcols] = (gv + more[krows, last]).astype(BF)

            tiles(2, rt, own_part)
            qkv[:, cols] = (gq[...] * 0.125).astype(BF)

        @pl.when(c == 1)
        def _():
            p = i
            cols = pl.ds(pl.multiple_of(p * PAIR, PAIR), PAIR)
            kcols = pl.ds(pl.multiple_of(d + p * PAIR, PAIR), PAIR)
            vcols = pl.ds(pl.multiple_of(2 * d + p * PAIR, PAIR), PAIR)
            gq[...] = jnp.zeros_like(gq)

            @pl.when(p < SHARED)
            def _():
                def near_part(r, krows):
                    gk, gv = term(
                        p, cross[krows, cols], cross[krows, kcols], krows, every, qkv[:, cols], go[:, cols], lset, deltat, False, gq
                    )
                    cross[krows, cols] = (gk * 0.125).astype(BF)
                    cross[krows, kcols] = gv.astype(BF)

                tiles(2, rt, near_part)

            for r in range(2):
                krows, qrows = pl.ds(r * rt, rt), pl.ds(r * rt, rows - r * rt)
                gk, gv = term(
                    p, qkv[krows, kcols], qkv[krows, vcols], krows, qrows, qkv[qrows, cols], go[qrows, cols], lset, deltat, True, gq
                )
                qkv[krows, kcols] = (gk * 0.125).astype(BF)
                qkv[krows, vcols] = gv.astype(BF)
            qkv[:, cols] = (gq[...] * 0.125).astype(BF)

        run_hooks(i, hooks)


def layer_kernel(nz, *refs):
    (
        frames_in, cot_in, pre_in, s_qkv, s_out, s_up, s_down, s_par,
        fo, gi, gl, f_qkv, f_out, f_up, f_down, f_par, g_qkv, g_out, g_up, g_down, g_par,
        x, cot, pre, h1, qkv, cross, att, x1, h2, a, gp, wa, wb, gh, gz, go, bias, narrow, narrow2, lset, deltat, far_lse, far_delta,
        acc, par, parv, ht, buf, land, sdown, spar, ptheirs, pland, second, third, psecond, pthird,
        ag_send, ag_recv, ag_own, rs_send, rs_recv, rs_free, p_send, p_recv, p_credit,
        load_sem, swap_sem, io_sem, io_recv,
    ) = refs
    place = z, y, c, f = coords()
    rows, d = x.shape
    ff = a.shape[-1]
    core, far = dev(z, y, 1 - c, f), dev(z, y, 1 - c, 1 - f)
    straight = c == f
    nk = d // WIDE

    chunks = [(4, 0, 16, 0, PAIR)]
    chunks += [(0, 0, BLOCK, d + h * TILE, TILE) for h in range(2)] + [(0, 0, BLOCK, b * d, d) for b in (2, 0)]
    chunks += [(1, 0, BLOCK, 0, d)]
    chunks += [(2, 0, BLOCK, k * WIDE, WIDE) for k in range(ff // WIDE)]
    down_cols = [(0, 256), (256, 256), (512, 256), (768, 128), (896, 128)]
    chunks += [(3, 0, 4 * BLOCK, c0, w) for c0, w in down_cols]
    ag = Gather(nz, place, (s_qkv, s_out, s_up, s_down, s_par), (f_qkv, f_out, f_up, f_down, f_par), chunks, (ag_send, ag_recv, ag_own))

    ups, downs = ff // WIDE, 4
    sums = [sdown.at[k] for k in range(downs)]
    sums += [a.at[:, :, :, :, pl.ds(k * WIDE, WIDE)] for k in range(ups)]
    tail = [(3 * d, d), (d, d), (2 * d, d), (0, TILE), (TILE, TILE)]
    sums += [gp.at[:, :, :, :, pl.ds(c0, w)] for c0, w in tail]
    goes = [g_down.at[pl.ds(k * BLOCK, BLOCK)] for k in range(downs)]
    goes += [g_up.at[:, pl.ds(k * WIDE, WIDE)] for k in range(ups)]
    goes += [g_out] + [g_qkv.at[:, pl.ds(c0, w)] for c0, w in tail[1:]]
    n = len(sums)
    widths = [WIDE] * (downs + ups) + [w for _, w in tail]
    rs = Scatter(
        nz, place, sums + [spar], [second.at[i % RING, :, :, :, pl.ds(0, widths[i])] for i in range(n)] + [psecond],
        [third.at[i % RING, :, :, pl.ds(0, widths[i])] for i in range(n)] + [pthird], goes + [g_par], (rs_send, rs_recv, rs_free),
    )
    maker = Producer(place, buf, land, (p_send, p_recv, p_credit))

    for i in range(len(chunks)):
        ag.local(i).start()
    greet(all_peers(nz, *place) + [far])

    swaps = []
    quarter = rows // 4
    quarters = [pl.ds(i * quarter, quarter) for i in range(4)]
    moves = [(pre_in, pre)]
    moves += [(cot_in.at[q], cot.at[q]) for q in quarters] + [(frames_in.at[q], x.at[q]) for q in quarters]
    for i, (src, dst) in enumerate(moves):
        swaps.append((pltpu.make_async_copy(src, dst, swap_sem.at[i, 0]), remote(src, dst, swap_sem.at[i, 1], swap_sem.at[i, 2], far)))

    def swap_start(i):
        @pl.when(straight)
        def _():
            swaps[i][0].start()

        @pl.when(jnp.logical_not(straight))
        def _():
            swaps[i][1].start()

    def swap_wait(i):
        @pl.when(straight)
        def _():
            swaps[i][0].wait()

        @pl.when(jnp.logical_not(straight))
        def _():
            swaps[i][1].wait()

    def between(i, src, dst):
        return remote(src, dst, swap_sem.at[i, 1], swap_sem.at[i, 2], core)

    def ag_tick(t):
        return lambda: ag.tick(t)

    def rs_tick(t):
        return lambda: rs.tick(t)

    def rs_begin(i):
        return lambda: rs.stage(i, 0)

    def small(b):
        return pl.ds(b * BLOCK, BLOCK)

    def load(i, src, dst):
        return pltpu.make_async_copy(src, dst, load_sem.at[i])

    def load_block(i, b):
        if b == 3:
            return load(i, f_out, wa.at[:, :, :, :, small(3)])
        return load(i, f_qkv.at[:, :, :, :, :, pl.ds(b * d, d)], wa.at[:, :, :, :, small(b)])

    def block(b, at=slice(None)):
        v = wa[at, :, :, :, small(b)]
        return v.reshape(math.prod(v.shape[:-1]), d)

    ag.stage(0, 0)
    ag.stage(1, 0)
    swap_start(0)
    swap_start(5)
    ag.stage(0, 1)
    ag.tick(2)
    swap_start(6)
    ag.tick(3)
    swap_start(7)
    ag.stage(0, 4)
    get_par = load(0, f_par, parv)
    get_par.start()
    swap_wait(0)
    fill_bias(bias, pre[0:1, 0:1], c, False)
    get_par.wait()
    for t in range(d // PAIR):
        total = None
        for k in range(4):
            piece = parv[t // 2, t % 2, k // 2, k % 2].astype(F32)
            total = piece if total is None else total + piece
        par[:, pl.ds(t * PAIR, PAIR)] = total
    step = 64

    def norm_one(j, part):
        nrm, _ = normalise(x[part, :].astype(F32))
        h1[part, :] = (nrm * par[0:1, :] + par[2:3, :]).astype(BF)

    ag.tick(4)
    swap_start(8)
    for i in range(4):
        swap_wait(5 + i)
    tiles(rows // step, step, norm_one)
    keyvals = between(14, qkv.at[:, pl.ds(d, 2 * d)], cross)
    ag.stage(1, 4)
    for i, b in enumerate((1, 2, 0)):
        ag.tick(5 + i)
        ag.stage(2 + i, 4)
        get = load_block(1 + i, b)
        get.start()
        get.wait()
        for t in range(d // TILE):
            cols = pl.ds(t * TILE, TILE)
            w = wa[:, :, :, :, small(b), cols].reshape(d, TILE)
            qkv[:, pl.ds(b * d + t * TILE, TILE)] = dot_nn(h1[...], w).astype(BF)
        swap_start(1 + i)
        if b == 2:

            @pl.when(c == 0)
            def _():
                keyvals.start()

    @pl.when(c == 1)
    def _():
        keyvals.wait_recv()

    swap_start(4)
    narrow[...] = jnp.zeros_like(narrow)
    attend_forward(c, qkv, cross, bias, att, narrow, {0: ag_tick(8), 5: ag_tick(9)})
    ag.stage(5, 4)
    get_out = load_block(4, 3)
    get_out.start()

    @pl.when(c == 0)
    def _():
        keyvals.wait_send()

    lset[...] = narrow[...].T[:H, :]

    def get_up(k):
        return load(5 + k, f_up.at[:, :, :, :, :, pl.ds(k * WIDE, WIDE)], wb.at[:, :, :, :, :, pl.ds(k * WIDE, WIDE)])

    ag.stage(6, 4)
    get_up(0).start()
    get_out.wait()
    for t in range(d // TILE):
        cols = pl.ds(t * TILE, TILE)
        w = wa[:, :, :, :, small(3), cols].reshape(d, TILE)
        x1[:, cols] = x[:, cols].astype(F32) + dot_nn(att[...], w)
    ag.tick(10)

    def norm_two(j, part):
        nrm, _ = normalise(x1[part, :])
        h2[part, :] = (nrm * par[1:2, :] + par[3:4, :]).astype(BF)

    tiles(rows // step, step, norm_two)
    u = gh.at[:, pl.ds(0, TILE)]

    def up(cols):
        gh[:, pl.ds(0, TILE)] = dot_nn(h2[...], wb[:, :, :, :, :, cols].reshape(d, TILE))

        @pl.loop(0, rows // BLOCK)
        def _(j):
            at = (lax.div(j, 4), lax.rem(lax.div(j, 2), 2), lax.rem(j, 2), slice(None), cols)
            v = gh[pl.ds(pl.multiple_of(j * BLOCK, BLOCK), BLOCK), pl.ds(0, TILE)]
            phi = 0.5 * (1.0 + lax.erf(v * math.sqrt(0.5)))
            dens = jnp.exp2(v * v * (-0.5 * LOG2E)) * (1.0 / math.sqrt(2.0 * math.pi))
            a[at] = (v * phi).astype(BF)
            gp[at] = (phi + v * dens).astype(BF)

    for i in range(4):
        swap_wait(1 + i)

    def down_product(j):
        for k in range(ups):

            @pl.when(j == 2 * k)
            def _():
                if k:
                    ag.stage(6 + k, 4)
                    get_up(k).start()
                get_up(k).wait()

        cols = pl.ds(pl.multiple_of(j * TILE, TILE), TILE)
        up(cols)
        for k in range(ups):

            @pl.when(j == 2 * k)
            def _():
                ag.tick(11 + k, (0, 1))

            @pl.when(j == 2 * k + 1)
            def _():
                ag.tick(11 + k, (2, 3))

        return dot_tn(flat(a, cols), cot[...])

    maker.run(2 * ups, down_product, deep_blocks, lambda j, i: sdown.at[i, lax.div(j, 2), lax.rem(j, 2)])

    def get_down(k):
        part = pl.ds(*down_cols[k])
        return load(9 + k, f_down.at[:, :, :, :, :, part], wa.at[:, :, :, :, :, part])

    def down(k):
        cols = pl.ds(k * TILE, TILE)
        w = wa[:, :, :, :, :, cols].reshape(ff, TILE)
        go[:, cols] = (x1[:, cols] + dot_nn(flat(a, slice(None)), w)).astype(BF)

    ag.tick(15)
    maker.flush()
    for k in range(2):
        ag.stage(10 + k, 4)
        get_down(k).start()
    ag.tick(16)
    ag.tick(17)
    rs.stage(0, 0)
    for k in range(2):
        get_down(k).wait()
    down(0)
    for k in range(2, len(down_cols)):
        ag.stage(10 + k, 4)
        get_down(k).start()
    for k in range(2, len(down_cols)):
        get_down(k).wait()
    rs.stage(1, 0)
    down(1)
    rs.stage(2, 0)
    outs = []
    for q in quarters:
        outs.append(
            (
                pltpu.make_async_copy(go.at[q], fo.at[q], io_sem.at[len(outs)]),
                remote(go.at[q], fo.at[q], io_sem.at[len(outs)], io_recv.at[len(outs)], far),
            )
        )

    def either(pair, act_on):
        @pl.when(straight)
        def _():
            act_on(pair[0])

        @pl.when(jnp.logical_not(straight))
        def _():
            act_on(pair[1])

    def begin(pair):
        either(pair, lambda copy: copy.start())

    def end(pair):
        either(pair, lambda copy: copy.wait())

    begin(outs[0])
    def act(j, cols):
        w = wa[lax.div(j, 2), lax.rem(j, 2)].reshape(TILE, d)
        v = dot_nt(cot[...], w) * flat(gp, cols).astype(F32)
        gp[:, :, :, :, cols] = v.astype(BF).reshape(a.shape[:-1] + (TILE,))

    rs.stage(3, 0)
    tiles(8, TILE, act, {5: rs_tick(1)})
    begin(outs[1])
    for i, b in enumerate((3, 0, 1, 2)):
        load_block(14 + i, b).start()
    ht[...] = h2[...].T
    for i in range(2):
        gh[:, pl.ds(i * TILE, TILE)] = dot_nt(flat(gp, slice(None)), wb[2 * i : 2 * i + 2].reshape(TILE, ff))
        if i == 0:
            rs.tick(2)
    begin(outs[2])
    acc[...] = jnp.zeros_like(acc)
    step = 32

    def collect(row, v):
        part = v.reshape(step // 8, 8, d)
        acc[row] = acc[row] + functools.reduce(jnp.add, [part[i] for i in range(step // 8)])

    def back_two(j, part):
        nrm, scale = normalise(x1[part, :])
        g = gh[part, :]
        collect(1, g * nrm)
        collect(3, g)
        total = cot[part, :].astype(F32) + norm_back(g, nrm, scale, par[1:2, :])
        x1[part, :] = total
        gz[part, :] = total.astype(BF)

    tiles(rows // step, step, back_two)

    def row_half(j):
        return ht[pl.ds(pl.multiple_of(lax.rem(j, 2) * TILE, TILE), TILE), :]

    def wide(j):
        return pl.ds(pl.multiple_of(lax.div(j, 2) * WIDE, WIDE), WIDE)

    def up_product(j):
        return dot_nn(row_half(j), flat(gp, wide(j)))

    def target(ref, first):
        def of(j, i):
            cols = pl.ds(pl.multiple_of(first + lax.div(j, 2) * WIDE, WIDE), WIDE)
            return ref.at[2 * lax.rem(j, 2) + i // 2, i % 2, :, :, cols]

        return of

    rs.tick(3)
    begin(outs[3])
    maker.run(
        2 * ups, up_product, row_blocks, target(a, 0), {2: rs_begin(4), 3: rs_tick(4), 4: rs_begin(5), 6: rs_begin(6)}
    )
    maker.flush()
    rs.stage(7, 0)
    for pair in outs:
        end(pair)
    load_block(14, 3).wait()
    for i in range(2):
        go[:, pl.ds(i * TILE, TILE)] = dot_nt(gz[...], block(3, pl.ds(2 * i, 2))).astype(BF)
    pick = (
        lax.broadcasted_iota(jnp.int32, (H, d), 1) // HD == lax.broadcasted_iota(jnp.int32, (H, d), 0)
    ).astype(BF)
    for i in range(4):
        part = pl.ds(i * quarter, quarter)
        prod = go[part, :].astype(F32) * att[part, :].astype(F32)
        high = prod.astype(BF)
        low = (prod - high.astype(F32)).astype(BF)
        deltat[:, part] = dot_nt(pick, high) + dot_nt(pick, low)
    low_cols, high_cols = pl.ds(0, SHARED * PAIR), pl.ds(SHARED * PAIR, d - SHARED * PAIR)
    high_cols2 = pl.ds(d + SHARED * PAIR, d - SHARED * PAIR)
    low_cols2 = pl.ds(d, SHARED * PAIR)

    lends = [
        between(9, qkv.at[:, high_cols], cross.at[:, high_cols]),
        between(15, go.at[:, high_cols], cross.at[:, high_cols2]),
        between(16, lset, far_lse),
        between(10, deltat, far_delta),
    ]
    gives = [
        between(11, cross.at[:, low_cols], cross.at[:, low_cols]),
        between(12, cross.at[:, low_cols2], cross.at[:, low_cols2]),
    ]
    returns = between(13, cross.at[:, high_cols], cross.at[:, high_cols])

    @pl.when(c == 1)
    def _():
        for copy in lends:
            copy.start()

    rs.tick(5)
    ht[...] = att[...].T
    maker.run(2, lambda j: dot_nn(row_half(j), gz[...]), row_blocks, target(gp, 3 * d))
    fill_bias(bias, pre[0:1, 0:1], c, True)

    @pl.when(c == 0)
    def _():
        for copy in lends:
            copy.wait_recv()

    @pl.when(c == 1)
    def _():
        for copy in lends:
            copy.wait_send()

    def give_back():
        @pl.when(c == 1)
        def _():
            for copy in gives:
                copy.start()

    def return_queries():
        @pl.when(c == 0)
        def _():
            returns.start()

    def flush_tick():
        maker.flush()
        rs.stage(8, 0)
        rs.tick(6)

    hooks = {0: flush_tick, 2: return_queries, 3: rs_tick(7), 4: give_back, 6: rs_tick(8)}
    attend_backward(c, qkv, cross, bias, lset, deltat, far_lse, far_delta, go, narrow, narrow2, gh, hooks)
    ht[...] = h1[...].T

    @pl.when(c == 1)
    def _():
        for copy in gives:
            copy.wait_send()
        returns.wait_recv()

        def add(j, part):
            qkv[part, high_cols] = (qkv[part, high_cols].astype(F32) + cross[part, high_cols].astype(F32)).astype(BF)

        tiles(rows // step, step, add)

    @pl.when(c == 0)
    def _():
        returns.wait_send()
        for copy in gives:
            copy.wait_recv()

        def add(j, part):
            for base in (0, d):
                to, src = pl.ds(d + base, SHARED * PAIR), pl.ds(base, SHARED * PAIR)
                qkv[part, to] = (qkv[part, to].astype(F32) + cross[part, src].astype(F32)).astype(BF)

        tiles(rows // step, step, add)

    def mixed_cols(j):
        return pl.ds(pl.multiple_of(lax.rem(lax.div(j, 2) + 1, 3) * d, d), d)

    def mixed_target(j, i):
        return gp.at[2 * lax.rem(j, 2) + i // 2, i % 2, :, :, mixed_cols(j)]

    maker.run(
        6, lambda j: dot_nn(row_half(j), qkv[:, mixed_cols(j)]), row_blocks, mixed_target, {2: rs_begin(9), 3: rs_tick(9), 4: rs_begin(10)}
    )
    maker.flush()
    rs.stage(11, 0)
    rs.stage(12, 0)
    rs.tick(10)
    for i, b in enumerate((0, 1, 2)):
        load_block(15 + i, b).wait()
    for i in range(2):
        total = None
        for b in range(3):
            part = dot_nt(qkv[:, pl.ds(b * d, d)], block(b, pl.ds(2 * i, 2)))
            total = part if total is None else total + part
        gh[:, pl.ds(i * TILE, TILE)] = total
        if i == 1:
            rs.tick(11)

    def back_one(j, part):
        nrm, scale = normalise(x[part, :].astype(F32))
        g = gh[part, :]
        collect(0, g * nrm)
        collect(2, g)
        total = x1[part, :] + norm_back(g, nrm, scale, par[0:1, :])
        gh[part, :] = total
        gz[part, :] = total.astype(BF)

    tiles(rows // step, step, back_one)
    backs = []
    for i, q in enumerate(quarters):
        backs.append(
            (
                pltpu.make_async_copy(gh.at[q], gi.at[q], io_sem.at[4 + i]),
                remote(gz.at[q], gl.at[q], io_sem.at[4 + i], io_recv.at[4 + i], far),
            )
        )
    begin(backs[0])
    for i in range(4):
        par[i : i + 1, :] = jnp.sum(acc[i], 0, keepdims=True)
    for t in range(d // PAIR):
        row = par[:, pl.ds(t * PAIR, PAIR)].astype(BF)
        for k in range(2):
            spar[t // 2, t % 2, k] = row
            ptheirs[t // 2, t % 2, k] = row
    pars = remote(ptheirs, pland, io_sem.at[8], io_recv.at[8], core)
    pars.start()
    rs.stage(11, 1)
    pars.wait_recv()
    add_blocks(spar, [pland])
    rs.stage(n, 0)
    begin(backs[1])
    for i, st in ((12, 1), (10, 2), (9, 3)):
        rs.stage(i, st)
    begin(backs[2])
    for i, st in ((n, 1), (11, 2), (12, 2)):
        rs.stage(i, st)
    begin(backs[3])
    for i, st in ((10, 3), (n, 2), (11, 3), (12, 3), (n, 3)):
        rs.stage(i, st)
    for pair in backs:
        end(pair)
    pars.wait_send()
    for i in range(len(chunks)):
        ag.finish(i)
    for i in range(n + 1):
        rs.finish(i)
    maker.finish()


def layer(nz, frames_in, cot, pre, w_qkv, w_out, w_up, w_down, tile):
    rows, d = frames_in.shape
    ff = w_up.shape[1]
    S = jax.ShapeDtypeStruct
    V = pltpu.VMEM
    REG = pltpu.SemaphoreType.REGULAR
    hbm, vm = pl.BlockSpec(memory_space=pl.ANY), pl.BlockSpec(memory_space=V)
    shards = (w_qkv, w_out, w_up, w_down, tile)
    parts = (nz, 2, 2, BLOCK)
    full = (nz, 2, 2, 2)
    return pl.pallas_call(
        functools.partial(layer_kernel, nz),
        out_shape=[S((rows, d), BF), S((rows, d), F32), S((rows, d), BF)]
        + [S(full + w.shape, BF) for w in shards]
        + [S(w.shape, F32) for w in shards],
        in_specs=[hbm] * 8,
        out_specs=[hbm] * 8 + [vm] * 5,
        scratch_shapes=[
            V((rows, d), BF), V((rows, d), BF), V((8, PAIR), jnp.int32), V((rows, d), BF), V((rows, 3 * d), BF),
            V((rows, 2 * d), BF), V((rows, d), BF), V((rows, d), F32), V((rows, d), BF),
            V(parts + (ff,), BF), V(parts + (ff,), BF),
            V(full + w_down.shape, BF), V(full + w_up.shape, BF),
            V((rows, d), F32), V((rows, d), BF), V((rows, d), BF), V((rows, rows), F32), V((rows, PAIR), F32), V((rows, PAIR), F32),
            V((H, rows), F32), V((H, rows), F32), V((H, rows), F32), V((H, rows), F32), V((4, 8, d), F32), V((16, d), F32), V(full + (16, PAIR), BF),
            V((d, rows), BF), V((2, 4, 2, 2, BLOCK, WIDE), BF), V((2, 4, 2, BLOCK, WIDE), BF),
            V((4,) + parts + (d,), BF), V((nz, 2, 2, 16, PAIR), BF), V((nz, 2, 2, 16, PAIR), BF), V((nz, 2, 2, 16, PAIR), BF),
            V((RING, nz, 2, BLOCK, WIDE), BF), V((RING, 7, BLOCK, WIDE), BF), V((nz, 2, 16, PAIR), BF), V((7, 16, PAIR), BF),
        ]
        + Gather.sem_shapes(15)
        + Scatter.sem_shapes(14)
        + [DMA((2,)), DMA((2,)), REG((2,)), DMA((18,)), DMA((17, 3)), DMA((9,)), DMA((9,))],
        compiler_params=pltpu.CompilerParams(collective_id=0, has_side_effects=True, vmem_limit_bytes=63 * 2**20),
    )(frames_in, cot, pre, *shards)


def settle_kernel(fo, gi, gl, g_qkv, g_out, g_up, g_down, g_par, fo_, gi_, qkv_, out_, up_, down_, gains_, shifts_, narrow, wide, *rest):
    straight = lax.rem(lax.axis_index("dp"), 2) == lax.axis_index("fsdp")
    stops, sems = rest[:5], rest[5]
    pairs = ((fo, fo_), (g_qkv, qkv_), (g_out, out_), (g_up, up_), (g_down, down_))
    ins = [pltpu.make_async_copy(src, stop, sems.at[0, i]) for i, ((src, _), stop) in enumerate(zip(pairs, stops))]
    outs = [pltpu.make_async_copy(stop, dst, sems.at[1, i]) for i, ((_, dst), stop) in enumerate(zip(pairs, stops))]
    rows = gi.shape[0] // 4
    parts = [pl.ds(i * rows, rows) for i in range(4)]
    own = [pltpu.make_async_copy(gi.at[p], wide.at[p], sems.at[2, i]) for i, p in enumerate(parts)]
    came = [pltpu.make_async_copy(gl.at[p], narrow.at[p], sems.at[2, i]) for i, p in enumerate(parts)]
    puts = [pltpu.make_async_copy(wide.at[p], gi_.at[p], sems.at[3, i]) for i, p in enumerate(parts)]

    @pl.when(straight)
    def _():
        for get in own:
            get.start()

    @pl.when(jnp.logical_not(straight))
    def _():
        for get in came:
            get.start()

    for copy in ins:
        copy.start()
    width = gains_.shape[1]
    mine = lax.rem(lax.axis_index("dp") * 2 + lax.axis_index("fsdp"), PAIR // width)
    small = g_par[:, pl.ds(0, width)]
    for i in range(1, PAIR // width):
        small = jnp.where(mine == i, g_par[:, pl.ds(i * width, width)], small)
    gains_[...] = small[0:2]
    shifts_[...] = small[2:4]

    @pl.when(straight)
    def _():
        for get, put in zip(own, puts):
            get.wait()
            put.start()

    @pl.when(jnp.logical_not(straight))
    def _():
        for get, put, p in zip(came, puts, parts):
            get.wait()
            wide[p, :] = narrow[p, :].astype(F32)
            put.start()

    for get, put in zip(ins, outs):
        get.wait()
        put.start()
    for put in puts + outs:
        put.wait()


def settle(width, fo, gi, gl, *grads):
    S = jax.ShapeDtypeStruct
    V = pltpu.VMEM
    hbm, vm = pl.BlockSpec(memory_space=pl.ANY), pl.BlockSpec(memory_space=V)
    kept = (fo, gi) + grads[:4]
    return pl.pallas_call(
        settle_kernel,
        out_shape=[S(v.shape, v.dtype) for v in kept] + [S((2, width), F32)] * 2,
        in_specs=[hbm] * 7 + [vm],
        out_specs=[hbm] * 6 + [vm] * 2,
        scratch_shapes=[V(gl.shape, BF), V(gi.shape, F32)] + [V(v.shape, v.dtype) for v in (fo,) + grads[:4]] + [DMA((4, 5))],
        compiler_params=pltpu.CompilerParams(vmem_limit_bytes=VMEM_LIMIT),
    )(fo, gi, gl, *grads)


def norm_rows(values, gain, shift):
    center = values - jnp.mean(values, -1, keepdims=True)
    spread = jnp.mean(center * center, -1, keepdims=True)
    return center * lax.rsqrt(spread + EPS) * gain + shift


def collect(w_qkv, w_out, w_up, w_down, gains, shifts):
    return (
        lax.all_gather(w_qkv, ("dp", "fsdp"), axis=0, tiled=True),
        lax.all_gather(w_out, ("dp", "fsdp"), axis=0, tiled=True),
        lax.all_gather(w_up, ("dp", "fsdp"), axis=0, tiled=True),
        lax.all_gather(w_down, ("dp", "fsdp"), axis=0, tiled=True),
        lax.all_gather(gains, ("dp", "fsdp"), axis=1, tiled=True),
        lax.all_gather(shifts, ("dp", "fsdp"), axis=1, tiled=True),
    )


def split_heads(matrix):
    return matrix.reshape(matrix.shape[0], H, HD).transpose(1, 0, 2)


def join_heads(stacked):
    return stacked.transpose(1, 0, 2).reshape(stacked.shape[1], H * HD)


def masked_scores(query_one, key_one, allowed):
    scores = jnp.dot(query_one, key_one.T, preferred_element_type=jnp.float32) * 0.125
    return jnp.where(allowed, scores, -1e30)


def forward(inputs, weights, allowed):
    w_qkv, w_out, w_up, w_down, gains, shifts = weights
    width = inputs.shape[1]
    gain_rows = gains.astype(jnp.float32)
    shift_rows = shifts.astype(jnp.float32)
    normed = norm_rows(inputs, gain_rows[0], shift_rows[0]).astype(jnp.bfloat16)
    mixed = jnp.dot(normed, w_qkv, preferred_element_type=jnp.float32).astype(jnp.bfloat16)
    queries = mixed[:, :width]
    keys_all, values_all = (
        lax.all_gather(mixed[:, width : 2 * width], "fsdp", axis=0, tiled=True),
        lax.all_gather(mixed[:, 2 * width :], "fsdp", axis=0, tiled=True),
    )
    query_heads = split_heads(queries)
    key_heads = split_heads(keys_all)
    value_heads = split_heads(values_all)

    def single(pieces):
        scores = masked_scores(pieces[0], pieces[1], allowed)
        peak_row = jnp.max(scores, -1, keepdims=True)
        log_total = peak_row + jnp.log(jnp.sum(jnp.exp(scores - peak_row), -1, keepdims=True))
        chance = jnp.exp(scores - log_total).astype(jnp.bfloat16)
        return (jnp.dot(chance, pieces[2], preferred_element_type=jnp.float32), log_total[:, 0])

    outputs, totals = lax.map(single, (query_heads, key_heads, value_heads))
    attended = join_heads(outputs).astype(jnp.bfloat16)
    middle = inputs + jnp.dot(attended, w_out, preferred_element_type=jnp.float32)
    normed_two = norm_rows(middle, gain_rows[1], shift_rows[1]).astype(jnp.bfloat16)
    hidden = jnp.dot(normed_two, w_up, preferred_element_type=jnp.float32)
    active = jax.nn.gelu(hidden, approximate=False).astype(jnp.bfloat16)
    result = middle + jnp.dot(active, w_down, preferred_element_type=jnp.float32)
    saved = (
        normed,
        query_heads,
        key_heads,
        value_heads,
        totals,
        attended,
        middle,
        normed_two,
        hidden,
        active,
    )
    return (result, saved)


def on_device(frames_in, prefix_len, w_qkv, w_out, w_up, w_down, gains, shifts, cotangent):
    inputs = frames_in[0].astype(jnp.float32)
    rows_here = inputs.shape[0]
    frames_all = rows_here * lax.axis_size("fsdp")
    first_row = lax.axis_index("fsdp") * rows_here
    places = first_row + jnp.arange(rows_here, dtype=jnp.int32)
    columns = jnp.arange(frames_all, dtype=jnp.int32)
    allowed = (columns[None, :] <= places[:, None]) | (columns[None, :] < prefix_len[0])
    weights = collect(w_qkv, w_out, w_up, w_down, gains, shifts)
    result, saved = forward(inputs, weights, allowed)
    weights = collect(w_qkv, w_out, w_up, w_down, gains, shifts)
    saved = forward(inputs, weights, allowed)[1]
    full_qkv, full_out, full_up, full_down, full_gains, full_shifts = weights
    (
        normed,
        query_heads,
        key_heads,
        value_heads,
        totals,
        attended,
        middle,
        normed_two,
        hidden,
        active,
    ) = saved
    gain_rows = full_gains.astype(jnp.float32)
    shift_rows = full_shifts.astype(jnp.float32)
    grad_top = cotangent[0].astype(jnp.float32)
    grad_branch = grad_top.astype(jnp.bfloat16)
    part_down = jnp.dot(active.T, grad_branch, preferred_element_type=jnp.float32)
    grad_active = jnp.dot(grad_branch, full_down.T, preferred_element_type=jnp.float32)
    gelu_pull = jax.vjp(functools.partial(jax.nn.gelu, approximate=False), hidden)[1]
    grad_hidden = gelu_pull(grad_active)[0].astype(jnp.bfloat16)
    part_up = jnp.dot(normed_two.T, grad_hidden, preferred_element_type=jnp.float32)
    grad_normed_two = jnp.dot(grad_hidden, full_up.T, preferred_element_type=jnp.float32)
    norm_pull_two = jax.vjp(norm_rows, middle, gain_rows[1], shift_rows[1])[1]
    back_middle, grad_gain_two, grad_shift_two = norm_pull_two(grad_normed_two)
    grad_middle = grad_top + back_middle
    grad_attn_out = grad_middle.astype(jnp.bfloat16)
    part_out = jnp.dot(attended.T, grad_attn_out, preferred_element_type=jnp.float32)
    grad_attended = jnp.dot(grad_attn_out, full_out.T, preferred_element_type=jnp.float32).astype(
        jnp.bfloat16
    )
    grad_att_heads = split_heads(grad_attended)

    def single_back(pieces):
        query_one, key_one, value_one, grad_one, log_total = pieces
        scores = masked_scores(query_one, key_one, allowed)
        chance = jnp.exp(scores - log_total[:, None])
        grad_chance = jnp.dot(grad_one, value_one.T, preferred_element_type=jnp.float32)
        inner = jnp.sum(chance * grad_chance, -1, keepdims=True)
        grad_scores = (chance * (grad_chance - inner)).astype(jnp.bfloat16)
        grad_query = jnp.dot(grad_scores, key_one, preferred_element_type=jnp.float32) * 0.125
        grad_key = (
            jnp.einsum("qk,qd->kd", grad_scores, query_one, preferred_element_type=jnp.float32)
            * 0.125
        )
        grad_value = jnp.einsum(
            "qk,qd->kd", chance.astype(jnp.bfloat16), grad_one, preferred_element_type=jnp.float32
        )
        return (grad_query, grad_key, grad_value)

    grad_q_heads, grad_k_heads, grad_v_heads = lax.map(
        single_back, (query_heads, key_heads, value_heads, grad_att_heads, totals)
    )
    grad_keys, grad_values = (
        lax.psum_scatter(
            join_heads(grad_k_heads).astype(jnp.bfloat16), "fsdp", scatter_dimension=0, tiled=True
        ).astype(jnp.float32),
        lax.psum_scatter(
            join_heads(grad_v_heads).astype(jnp.bfloat16), "fsdp", scatter_dimension=0, tiled=True
        ).astype(jnp.float32),
    )
    grad_mixed = jnp.concatenate([join_heads(grad_q_heads), grad_keys, grad_values], 1).astype(
        jnp.bfloat16
    )
    part_qkv = jnp.dot(normed.T, grad_mixed, preferred_element_type=jnp.float32)
    grad_normed = jnp.dot(grad_mixed, full_qkv.T, preferred_element_type=jnp.float32)
    norm_pull_one = jax.vjp(norm_rows, inputs, gain_rows[0], shift_rows[0])[1]
    back_inputs, grad_gain_one, grad_shift_one = norm_pull_one(grad_normed)
    grad_inputs = grad_middle + back_inputs
    part_gains = jnp.stack([grad_gain_one, grad_gain_two])
    part_shifts = jnp.stack([grad_shift_one, grad_shift_two])
    owned = (
        lax.psum_scatter(part_qkv, ("dp", "fsdp"), scatter_dimension=0, tiled=True),
        lax.psum_scatter(part_out, ("dp", "fsdp"), scatter_dimension=0, tiled=True),
        lax.psum_scatter(part_up, ("dp", "fsdp"), scatter_dimension=0, tiled=True),
        lax.psum_scatter(part_down, ("dp", "fsdp"), scatter_dimension=0, tiled=True),
        lax.psum_scatter(part_gains, ("dp", "fsdp"), scatter_dimension=1, tiled=True),
        lax.psum_scatter(part_shifts, ("dp", "fsdp"), scatter_dimension=1, tiled=True),
    )
    return (
        result.astype(jnp.bfloat16)[None],
        grad_inputs[None],
        owned[0],
        owned[1],
        owned[2],
        owned[3],
        owned[4],
        owned[5],
    )


def fast_device(ndp, frames_in, prefix_len, w_qkv, w_out, w_up, w_down, gains, shifts, cotangent):
    here = lax.axis_index("dp") * 2 + lax.axis_index("fsdp")
    width = gains.shape[1]
    per = PAIR // width
    rows = jnp.concatenate([gains, shifts, jnp.zeros((12, width), BF)], 0)
    tile = jnp.where(lax.broadcasted_iota(jnp.int32, (16, per, width), 1) == here % per, rows[:, None], 0.0)
    tile = tile.astype(BF).reshape(16, PAIR)
    pre = jnp.broadcast_to(prefix_len[None], (8, PAIR))
    result = layer(ndp // 4, frames_in[0], cotangent[0], pre, w_qkv, w_out, w_up, w_down, tile)
    frames_out, grad_in, *owned = settle(width, *result[:3], *result[8:])
    return (frames_out[None], grad_in[None]) + tuple(owned)


def solution(mesh):
    ndp, nf = mesh.shape["dp"], mesh.shape["fsdp"]
    both = P(("dp", "fsdp"), None)
    lanes = P(None, ("dp", "fsdp"))
    block = P("dp", "fsdp", None)
    body = functools.partial(fast_device, ndp) if (nf == 2 and ndp == 16) else on_device
    return jax.shard_map(
        body,
        mesh=mesh,
        in_specs=(block, P("dp"), both, both, both, both, lanes, lanes, block),
        out_specs=(block, block, both, both, both, both, lanes, lanes),
        check_vma=False,
    )
```
